32 devices in a mesh: blk: 32 (over z, y, x, core).
Axes of the slice: x: 2, y: 2, z: 4, core: 2. Of those that a mesh axis runs over, the one named last changes fastest.
Arguments:
- layer_input: bfloat16 [4096, 2560], P('blk'), may hold values from -6 to 6
- norm1_scale: bfloat16 [2560], P('blk'), may hold values from 0.25 to 1.75
- query_weight: bfloat16 [2560, 2560], P('blk'), may hold values from -0.125 to 0.125
- keyvalue_weight: bfloat16 [2560, 512], P('blk'), may hold values from -0.125 to 0.125
- out_weight: bfloat16 [2560, 2560], P('blk'), may hold values from -1.25 to 1.25
- norm2_scale: bfloat16 [2560], P('blk'), may hold values from 0.25 to 1.75
- gate_weight: bfloat16 [2560, 7680], P('blk'), may hold values from -0.125 to 0.125
- gate_bias: bfloat16 [7680], P('blk'), may hold values from -3 to 3
- up_weight: bfloat16 [2560, 7680], P('blk'), may hold values from -0.125 to 0.125
- up_bias: bfloat16 [7680], P('blk'), may hold values from -3 to 3
- down_weight: bfloat16 [7680, 2560], P('blk'), may hold values from -0.0625 to 0.0625
- down_bias: bfloat16 [2560], P('blk'), may hold values from -2 to 2
- out_cotangent: bfloat16 [4096, 2560], P('blk'), may hold values from -6 to 6
Outputs:
- layer_output: bfloat16 [4096, 2560], P('blk')
- residual_mid: float32 [4096, 2560], P('blk')
- rms_values: float32 [2, 4096], P(None, 'blk')
- input_grad: bfloat16 [4096, 2560], P('blk')
- grad_norm1_scale: float32 [2560], P('blk')
- grad_query_weight: float32 [2560, 2560], P('blk')
- grad_keyvalue_weight: float32 [2560, 512], P('blk')
- grad_out_weight: float32 [2560, 2560], P('blk')
- grad_norm2_scale: float32 [2560], P('blk')
- grad_gate_weight: float32 [2560, 7680], P('blk')
- grad_gate_bias: float32 [7680], P('blk')
- grad_up_weight: float32 [2560, 7680], P('blk')
- grad_up_bias: float32 [7680], P('blk')
- grad_down_weight: float32 [7680, 2560], P('blk')
- grad_down_bias: float32 [2560], P('blk')
The draws below stay inside these ranges and needn't reach their ends.
All inputs are finite; a program needn't handle non-finite values.
Results may differ from the reference program's by a relative error of at most 0.015.
Values may be sent and summed in bfloat16 or wider, within the bound.
A program may use at most 576 MiB of HBM per device.

```python
import math
import jax
import jax.numpy as jnp
from jax import lax

D = 2560
H = 10
HD = 256
FF = 7680
WINDOW = 2048
HQ = 2560
TOKENS = 4096


def raised(values, key, source, target, blocks, factor):
    def block_of(dim):
        return (jnp.arange(values.shape[dim]) // (values.shape[dim] // blocks)).reshape((-1,) + (1,) * (values.ndim - 1 - dim))

    one_side = jax.random.permutation(key, blocks)[block_of(target)]
    other_side = (block_of(target) + blocks // 2) % blocks
    return jnp.where((block_of(source) == one_side) | (block_of(source) == other_side), factor * values, values)


def block_scale(stream_key, extent, cuts, least, largest):
    gain, own = 1.0, jax.random.fold_in(stream_key, 6)
    for position, blocks in cuts:
        heights = jnp.exp(jax.random.uniform(jax.random.fold_in(own, position), (blocks,), jnp.float32, least / len(cuts), largest / len(cuts)))
        gain = gain * jnp.repeat(heights, extent[position] // blocks).reshape([-1 if axis == position else 1 for axis in range(len(extent))])
    return gain


def scatter_about(own_key, shape, scale, most, pieces=(), kind=jnp.bfloat16):
    drawn = jax.random.normal(own_key, shape, jnp.float32) * scale
    if len(pieces) > 0:
        drawn = block_scale(own_key, shape, pieces, -0.22, 0.18) * drawn
    return jnp.clip(drawn, min=-most, max=most).astype(kind)


def gaussian_with(own_key, shape, scale, most, split, heavy, held_as=jnp.bfloat16):
    entries = scale * jax.random.normal(own_key, shape, jnp.float32)
    if split:
        entries = entries * block_scale(own_key, shape, split, -0.22, 0.18)
    return jnp.clip(raised(entries, jax.random.fold_in(own_key, 3), *heavy), -most, most).astype(held_as)


def setup_inputs(seed: int = 0) -> dict:
    arg_keys = jax.random.split(jax.random.key(seed), 14)
    return {
        "layer_input": gaussian_with(arg_keys[0], (TOKENS, D), 1.0, 6.0, ((0, 32),), (0, 1, 32, 2.75)),
        "norm1_scale": jnp.clip(1.0 + 0.15 * jax.random.normal(arg_keys[1], (D,), jnp.float32), 0.25, 1.75).astype(jnp.bfloat16),
        "query_weight": scatter_about(arg_keys[2], (D, HQ), D ** -0.5, 0.125, ((0, 32),)),
        "keyvalue_weight": scatter_about(arg_keys[3], (D, 2 * HD), D ** -0.5, 0.125, ((0, 32),)),
        "out_weight": scatter_about(arg_keys[4], (HQ, D), (max(HQ // 128, 1)) ** -0.5, 1.25, ((0, 32),)),
        "norm2_scale": jnp.clip(1.0 + 0.15 * jax.random.normal(arg_keys[5], (D,), jnp.float32), 0.25, 1.75).astype(jnp.bfloat16),
        "gate_weight": scatter_about(arg_keys[6], (D, FF), D ** -0.5, 0.125, ((0, 32),)),
        "gate_bias": scatter_about(arg_keys[7], (FF,), 0.5, 3.0, ((0, 32),)),
        "up_weight": scatter_about(arg_keys[8], (D, FF), D ** -0.5, 0.125, ((0, 32),)),
        "up_bias": scatter_about(arg_keys[9], (FF,), 0.5, 3.0, ((0, 32),)),
        "down_weight": scatter_about(arg_keys[10], (FF, D), FF ** -0.5, 0.0625, ((0, 32),)),
        "down_bias": scatter_about(arg_keys[11], (D,), 0.3, 2.0, ((0, 32),)),
        "out_cotangent": scatter_about(arg_keys[12], (TOKENS, D), 1.0, 6.0, ((0, 32),)),
    }


EPSILON = 1e-06
NEGATIVE = -1e+30
ROTARY_BASE = 10000.0
HIGHEST = lax.Precision.HIGHEST

@jax.custom_vjp
def low(v):
    return lax.optimization_barrier(v.astype(jnp.bfloat16)).astype(jnp.float32)

@jax.custom_vjp
def low_back(v):
    return v

def low_keep(v):
    return (low(v), None)

def low_pass(kept, grad):
    return (grad,)

def back_keep(v):
    return (v, None)

def back_low(kept, grad):
    return (low(grad),)
low.defvjp(low_keep, low_pass)
low_back.defvjp(back_keep, back_low)

def rotary_tables(positions, quarter):
    frequency = ROTARY_BASE ** (-(jnp.arange(quarter, dtype=jnp.float32) / quarter))
    angles = positions[:, None] * frequency[None, :]
    return (jnp.cos(angles), jnp.sin(angles))

def rotate(vector, cosine, sine_table, quarter):
    leading = vector[..., :quarter]
    trailing = vector[..., quarter:2 * quarter]
    return jnp.concatenate([leading * cosine - trailing * sine_table, trailing * cosine + leading * sine_table, vector[..., 2 * quarter:]], axis=-1)

def gelu_tanh(values):
    return jax.nn.gelu(values, approximate=True)

def attend(queries, keys, values):
    block_rows = 256
    padding = (WINDOW + block_rows - 2) // block_rows * block_rows
    key_pad = jnp.pad(keys, ((padding, 0), (0, 0)))
    value_pad = jnp.pad(values, ((padding, 0), (0, 0)))
    starts = jnp.arange(TOKENS // block_rows, dtype=jnp.int32) * block_rows

    def one_block(inputs):
        query_block, block_start = inputs
        key_block = lax.dynamic_slice_in_dim(key_pad, block_start, padding + block_rows, 0)
        value_block = lax.dynamic_slice_in_dim(value_pad, block_start, padding + block_rows, 0)
        raw_scores = low_back(jnp.einsum('thd,kd->thk', query_block, key_block, precision=HIGHEST))
        query_pos = block_start + jnp.arange(block_rows, dtype=jnp.int32)
        key_pos = block_start - padding + jnp.arange(padding + block_rows, dtype=jnp.int32)
        distance = query_pos[:, None] - key_pos[None, :]
        allowed = (key_pos[None, :] >= 0) & (distance >= 0) & (distance < WINDOW)
        scores = jnp.where(allowed[:, None, :], raw_scores, NEGATIVE)
        row_max = lax.optimization_barrier(jnp.max(scores, axis=-1, keepdims=True))
        log_total = row_max + jnp.log(lax.optimization_barrier(jnp.sum(jnp.exp(scores - row_max), axis=-1, keepdims=True)))
        probs = low(jnp.exp(scores - log_total))
        return jnp.einsum('thk,kd->thd', probs, value_block, precision=HIGHEST)
    blocks = lax.map(jax.checkpoint(one_block), (queries.reshape(TOKENS // block_rows, block_rows, H, HD), starts))
    return blocks.reshape(TOKENS, H, HD)

def reference(layer_input, norm1_scale, query_weight, keyvalue_weight, out_weight, norm2_scale, gate_weight, gate_bias, up_weight, up_bias, down_weight, down_bias, out_cotangent):
    query_scale = 1.0 / math.sqrt(HD)
    quarter = HD // 4
    positions = jnp.arange(TOKENS, dtype=jnp.float32)
    cosine, sine_table = rotary_tables(positions, quarter)

    def forward(resid_in, gain_one, query_full, keyvalue_full, out_full, gain_two, gate_full, gate_b, up_full, up_b, down_full, down_b):
        square_one = lax.optimization_barrier(jnp.mean(resid_in * resid_in, axis=1, keepdims=True))
        normed_one = resid_in * lax.rsqrt(square_one + EPSILON)
        hidden_one = low(normed_one * gain_one)
        query_raw = low_back(jnp.dot(hidden_one, query_full, precision=HIGHEST))
        keyvalue_raw = low_back(jnp.dot(hidden_one, keyvalue_full, precision=HIGHEST))
        queries = low(rotate(query_raw.reshape(TOKENS, H, HD), cosine[:, None, :], sine_table[:, None, :], quarter) * query_scale)
        keys = low(rotate(keyvalue_raw[:, :HD], cosine, sine_table, quarter))
        values = low(keyvalue_raw[:, HD:])
        attended = attend(queries, keys, values)
        attention = low(low_back(attended)).reshape(TOKENS, H * HD)
        residual_mid = resid_in + low_back(jnp.dot(attention, out_full, precision=HIGHEST))
        square_two = lax.optimization_barrier(jnp.mean(residual_mid * residual_mid, axis=1, keepdims=True))
        normed_two = residual_mid * lax.rsqrt(square_two + EPSILON)
        hidden_two = low(normed_two * gain_two)
        gate_pre = low_back(jnp.dot(hidden_two, gate_full, precision=HIGHEST) + gate_b)
        up_pre = low_back(jnp.dot(hidden_two, up_full, precision=HIGHEST) + up_b)
        hidden_ffn = low(gelu_tanh(gate_pre) * up_pre)
        output = residual_mid + (jnp.dot(hidden_ffn, down_full, precision=HIGHEST) + down_b)
        rms_values = jnp.stack([jnp.sqrt(square_one[:, 0] + EPSILON), jnp.sqrt(square_two[:, 0] + EPSILON)], axis=0)
        return (output, (residual_mid, rms_values))
    output, pull, extras = jax.vjp(forward, layer_input.astype(jnp.float32), norm1_scale.astype(jnp.float32), query_weight.astype(jnp.float32), keyvalue_weight.astype(jnp.float32), out_weight.astype(jnp.float32), norm2_scale.astype(jnp.float32), gate_weight.astype(jnp.float32), gate_bias.astype(jnp.float32), up_weight.astype(jnp.float32), up_bias.astype(jnp.float32), down_weight.astype(jnp.float32), down_bias.astype(jnp.float32), has_aux=True)
    grads = pull(out_cotangent.astype(jnp.float32))
    return (output.astype(jnp.bfloat16), extras[0], extras[1], grads[0].astype(jnp.bfloat16), grads[1], grads[2], grads[3], grads[4], grads[5], grads[6], grads[7], grads[8], grads[9], grads[10], grads[11])
```

```python
import functools
import math

import jax
import jax.numpy as jnp
from jax import lax
from jax.experimental import pallas as pl
from jax.experimental.pallas import tpu as pltpu
from jax.sharding import PartitionSpec as P

HD = 256
WINDOW = 2048
EPSILON = 1e-06
NEGATIVE = -1e30
ROTARY_BASE = 10000.0
AXIS = "blk"
LANES = 128
DEVICES = 32
PAIR = 2
VMEM_BYTES = 48 * 1024 * 1024
F32 = jnp.float32
BF16 = jnp.bfloat16


def rotary_tables(positions, quarter):
    frequency = ROTARY_BASE ** (-(jnp.arange(quarter, dtype=F32) / quarter))
    angles = positions[:, None] * frequency[None, :]
    return (jnp.cos(angles), jnp.sin(angles))


def rotate(vector, cosine, sine_table, quarter):
    leading = vector[..., :quarter]
    trailing = vector[..., quarter : 2 * quarter]
    return jnp.concatenate(
        [
            leading * cosine - trailing * sine_table,
            trailing * cosine + leading * sine_table,
            vector[..., 2 * quarter :],
        ],
        axis=-1,
    )


def gelu_tanh(values):
    return jax.nn.gelu(values, approximate=True)


def dot(left, right, contract):
    return lax.dot_general(left, right, (contract, ((), ())), preferred_element_type=F32)


def round_up(count, step):
    return (count + step - 1) // step * step


def pad_columns(values, columns):
    pad = [(0, 0)] * (values.ndim - 1) + [(0, columns - values.shape[-1])]
    return jnp.pad(values, pad)


def masked_scores(place_ref, query_rows, keys, tok_rows):
    scores = dot(query_rows, keys, ((1,), (1,)))
    rows = lax.broadcasted_iota(jnp.int32, scores.shape, 0) % tok_rows
    columns = lax.broadcasted_iota(jnp.int32, scores.shape, 1)
    distance = rows - columns + place_ref[0]
    return jnp.where((distance >= 0) & (distance < WINDOW), scores, NEGATIVE)


def stack_heads(block):
    return jnp.concatenate([block[:, i * HD : (i + 1) * HD] for i in range(PAIR)], axis=0)


def unstack_heads(rows):
    tok_rows = rows.shape[0] // PAIR
    return jnp.concatenate([rows[i * tok_rows : (i + 1) * tok_rows] for i in range(PAIR)], axis=1)


def attend_kernel(place_ref, query_ref, kv_ref, out_ref, log_ref):
    tok_rows = query_ref.shape[0]
    scores = masked_scores(place_ref, stack_heads(query_ref[...]), kv_ref[:, :HD], tok_rows)
    row_max = jnp.max(scores, axis=1, keepdims=True)
    probs = jnp.exp(scores - row_max)
    row_sum = jnp.sum(probs, axis=1, keepdims=True)
    probs_low = (probs * (1.0 / row_sum)).astype(BF16)
    attended = dot(probs_low, kv_ref[:, HD:], ((1,), (0,)))
    out_ref[...] = unstack_heads(attended).astype(BF16)
    log_ref[0] = jnp.broadcast_to(row_max + jnp.log(row_sum), log_ref.shape[1:])


def attend_back_kernel(place_ref, query_ref, kv_ref, log_ref, grad_ref, query_grad_ref, kv_grad_ref):
    tok_rows = query_ref.shape[0]
    query_rows = stack_heads(query_ref[...])
    grad_rows = stack_heads(grad_ref[...])
    keys, values = kv_ref[:, :HD], kv_ref[:, HD:]
    scores = masked_scores(place_ref, query_rows, keys, tok_rows)
    probs = jnp.exp(scores - log_ref[0][:, :1])
    prob_grad = dot(grad_rows, values, ((1,), (1,)))
    delta = jnp.sum(probs * prob_grad, axis=1, keepdims=True)
    score_grad = (probs * (prob_grad - delta)).astype(BF16)
    query_grad_ref[...] = unstack_heads(dot(score_grad, keys, ((1,), (0,))))
    key_part = dot(score_grad, query_rows, ((0,), (0,)))
    value_part = dot(probs.astype(BF16), grad_rows, ((0,), (0,)))

    @pl.when(pl.program_id(0) == 0)
    def _():
        kv_grad_ref[:, :HD] = key_part
        kv_grad_ref[:, HD:] = value_part

    @pl.when(pl.program_id(0) > 0)
    def _():
        kv_grad_ref[:, :HD] += key_part
        kv_grad_ref[:, HD:] += value_part


def attention_specs(tok_rows, heads, window_rows):
    place = pl.BlockSpec(memory_space=pltpu.SMEM)
    by_head = pl.BlockSpec((tok_rows, PAIR * HD), lambda i: (0, i))
    whole = pl.BlockSpec((window_rows, 2 * HD), lambda i: (0, 0))
    logs = pl.BlockSpec((1, PAIR * tok_rows, LANES), lambda i: (i, 0, 0))
    return place, by_head, whole, logs


def attend(place, queries, kv_window):
    tok_rows, features = queries.shape
    window_rows = kv_window.shape[0]
    pairs = features // HD // PAIR
    place_spec, by_head, whole, logs = attention_specs(tok_rows, features // HD, window_rows)
    work = tok_rows * features * window_rows
    return pl.pallas_call(
        attend_kernel,
        grid=(pairs,),
        out_shape=(
            jax.ShapeDtypeStruct((tok_rows, features), BF16),
            jax.ShapeDtypeStruct((pairs, PAIR * tok_rows, LANES), F32),
        ),
        in_specs=[place_spec, by_head, whole],
        out_specs=(by_head, logs),
        compiler_params=pltpu.CompilerParams(vmem_limit_bytes=VMEM_BYTES),
        cost_estimate=pl.CostEstimate(
            flops=4 * work, bytes_accessed=8 * kv_window.size, transcendentals=work // HD
        ),
        name="attend",
    )(place, queries, kv_window)


def attend_back(place, queries, kv_window, logs_in, grad):
    tok_rows, features = queries.shape
    window_rows = kv_window.shape[0]
    pairs = features // HD // PAIR
    place_spec, by_head, whole, logs = attention_specs(tok_rows, features // HD, window_rows)
    work = tok_rows * features * window_rows
    return pl.pallas_call(
        attend_back_kernel,
        grid=(pairs,),
        out_shape=(
            jax.ShapeDtypeStruct((tok_rows, features), F32),
            jax.ShapeDtypeStruct((window_rows, 2 * HD), F32),
        ),
        in_specs=[place_spec, by_head, whole, logs, by_head],
        out_specs=(by_head, whole),
        compiler_params=pltpu.CompilerParams(vmem_limit_bytes=VMEM_BYTES),
        cost_estimate=pl.CostEstimate(
            flops=10 * work, bytes_accessed=8 * kv_window.size, transcendentals=work // HD
        ),
        name="attend_back",
    )(place, queries, kv_window, logs_in, grad)


MESH=pl.DeviceIdType.MESH

class Place:
    def __init__(self):
        me = lax.axis_index(AXIS)
        self.core = me % 2
        self.x = (me // 2) % 2
        self.y = (me // 4) % 2
        self.z = me // 8
        self.sibling = self.index(self.z, self.y, self.x, 1 - self.core)
        self.next_x = self.index(self.z, self.y, 1 - self.x, self.core)
        self.next_y = self.index(self.z, 1 - self.y, self.x, self.core)
        self.plane = [self.z] + [(self.z + o) % 4 for o in (1, 2, 3)]
        self.line = [self.index(p, self.y, self.x, self.core) for p in self.plane]
    def index(self, z, y, x, core):
        return ((z * 2 + y) * 2 + x) * 2 + core
    def side(self, dy, dx):
        return (1 - self.y if dy else self.y), (1 - self.x if dx else self.x)
    def meet(self):
        barrier = pltpu.get_barrier_semaphore()
        partners = [self.sibling, self.next_x, self.next_y] + self.line[1:]
        for device in partners:
            pl.semaphore_signal(barrier, inc=1, device_id=(device,), device_id_type=MESH)
        pl.semaphore_wait(barrier, len(partners))

def send(src, dst, sems, device):
    copy = pltpu.make_async_remote_copy(src_ref=src, dst_ref=dst, send_sem=sems[0], recv_sem=sems[1], device_id=(device,), device_id_type=MESH)
    copy.start()
    return copy

TILE=16
def add_rows(total, other, first, count):
    planes = other.shape[0]
    steps = count // TILE
    @pl.loop(0, planes * steps)
    def _(i):
        plane, row = i // steps, (i % steps) * TILE
        here = (plane, pl.ds(pl.multiple_of(row + first, TILE), TILE), slice(None))
        there = (plane, pl.ds(pl.multiple_of(row, TILE), TILE), slice(None))
        total[here] = (total[here].astype(F32) + other[there].astype(F32)).astype(BF16)

def sum_kernel(chunk, in_ref, out_ref, acc, got_core, got_diag_x, got_diag_y, got_x, got_y, got_z,
               load_sem, core_sems, diag_sems, side_sems, line_sems):
    place = Place()
    rows, columns = out_ref.shape
    upper = got_diag_x.shape[1]
    lower = rows - upper
    chunks = columns // chunk
    corners = [(1, 1), (0, 1), (1, 0), (0, 0)]
    cols = [pl.ds(k * chunk, chunk) for k in range(chunks)]
    loads, cores, sends = {}, {}, []
    for k in range(chunks):
        for i, (dy, dx) in enumerate(corners):
            y, x = place.side(dy, dx)
            load = pltpu.make_async_copy(in_ref.at[:, y, x, place.core, :, cols[k]], acc.at[i, :, :, cols[k]], load_sem.at[k, i])
            load.start()
            loads[k, i] = load
    place.meet()
    for k in range(chunks):
        for i, (dy, dx) in enumerate(corners):
            y, x = place.side(dy, dx)
            cores[k, i] = send(in_ref.at[:, y, x, 1 - place.core, :, cols[k]], got_core.at[i, :, :, cols[k]],
                               (core_sems.at[0, k, i], core_sems.at[1, k, i]), place.sibling)
    top, bottom = pl.ds(0, upper), pl.ds(upper, lower)
    diag, side, line = {}, {}, {}
    def pair(sems, k, i): return (sems.at[0, k, i], sems.at[1, k, i])
    def stage0(k):
        for i in range(4):
            loads[k, i].wait(); cores[k, i].wait_recv()
            add_rows(acc.at[i, :, :, cols[k]], got_core.at[i, :, :, cols[k]], 0, rows)
            if i == 0:
                diag[k, 0] = send(acc.at[0, :, top, cols[k]], got_diag_x.at[:, :, cols[k]], pair(diag_sems, k, 0), place.next_x)
                diag[k, 1] = send(acc.at[0, :, bottom, cols[k]], got_diag_y.at[:, :, cols[k]], pair(diag_sems, k, 1), place.next_y)
            if i == 1:
                side[k, 0] = send(acc.at[1, :, top, cols[k]], got_x.at[:, top, cols[k]], pair(side_sems, k, 0), place.next_x)
            if i == 2:
                side[k, 1] = send(acc.at[2, :, bottom, cols[k]], got_y.at[:, bottom, cols[k]], pair(side_sems, k, 1), place.next_y)
    def stage1(k):
        diag[k, 0].wait_recv()
        add_rows(acc.at[2, :, :, cols[k]], got_diag_x.at[:, :, cols[k]], 0, upper)
        side[k, 2] = send(acc.at[2, :, top, cols[k]], got_y.at[:, top, cols[k]], pair(side_sems, k, 2), place.next_y)
        diag[k, 1].wait_recv()
        add_rows(acc.at[1, :, :, cols[k]], got_diag_y.at[:, :, cols[k]], upper, lower)
        side[k, 3] = send(acc.at[1, :, bottom, cols[k]], got_x.at[:, bottom, cols[k]], pair(side_sems, k, 3), place.next_x)
    def stage2(k):
        for i in range(4): side[k, i].wait_recv()
        steps = rows // TILE
        @pl.loop(0, 4 * steps)
        def _(i):
            plane, row = i // steps, (i % steps) * TILE
            here = (plane, pl.ds(pl.multiple_of(row, TILE), TILE), cols[k])
            acc[(3,) + here] = (acc[(3,) + here].astype(F32) + got_x[here].astype(F32) + got_y[here].astype(F32)).astype(BF16)
        for o in (1, 2, 3):
            line[k, o] = send(acc.at[3, place.plane[o], :, cols[k]], got_z.at[o - 1, :, cols[k]], pair(line_sems, k, o - 1), place.line[o])
    def stage3(k):
        for o in (1, 2, 3): line[k, o].wait_recv()
        @pl.loop(0, rows // TILE)
        def _(i):
            here = (pl.ds(pl.multiple_of(i * TILE, TILE), TILE), cols[k])
            total = acc[(3, place.z) + here].astype(F32)
            for o in range(3): total += got_z[(o,) + here].astype(F32)
            out_ref[here] = total
    stages = [stage0, stage1, stage2, stage3]
    for step in range(chunks + 3):
        for s in range(3, -1, -1):
            if 0 <= step - s < chunks: stages[s](step - s)
    for group in (cores, diag, side, line):
        for copy in group.values(): copy.wait_send()

def sum_over_devices(partial, chunk, collective_id, name):
    rows, columns = partial.shape[0] // 32, partial.shape[1]
    chunks = columns // chunk
    upper = (rows // 2 + TILE - 1) // TILE * TILE
    def buf(*shape): return pltpu.VMEM(shape, BF16)
    def sems(count): return pltpu.SemaphoreType.DMA((2, chunks, count))
    return pl.pallas_call(
        functools.partial(sum_kernel, chunk),
        out_shape=jax.ShapeDtypeStruct((rows, columns), F32),
        in_specs=[pl.BlockSpec(memory_space=pl.ANY)],
        out_specs=pl.BlockSpec(memory_space=pltpu.VMEM),
        scratch_shapes=[buf(4, 4, rows, columns), buf(4, 4, rows, columns), buf(4, upper, columns), buf(4, rows - upper, columns),
            buf(4, rows, columns), buf(4, rows, columns), buf(3, rows, columns),
            pltpu.SemaphoreType.DMA((chunks, 4)), sems(4), sems(2), sems(4), sems(3)],
        compiler_params=pltpu.CompilerParams(collective_id=collective_id, has_side_effects=True, vmem_limit_bytes=56*1024*1024),
        name=name,
    )(partial.reshape(4, 2, 2, 2, rows, columns))


def gather_rows(values):
    return lax.all_gather(values, AXIS, axis=0, tiled=True)


def sum_rows(partial, chunk, collective_id, name):
    if lax.axis_size(AXIS) == DEVICES:
        return sum_over_devices(partial.astype(BF16), chunk, collective_id, name)
    return lax.psum_scatter(
        partial.astype(BF16), AXIS, scatter_dimension=0, tiled=True
    ).astype(F32)


def swap(pieces):
    return lax.all_to_all(pieces, AXIS, 0, 0, tiled=False)


def feed_forward(hidden_two, out_cotangent, both_own, both_bias, down_own, rows):
    peers = lax.axis_size(AXIS)
    device = lax.axis_index(AXIS)
    tok_rows, width = hidden_two.shape
    ffn_pad = down_own.shape[0]

    def piece(sums, here):
        hidden_own, cotangent_own = here
        cotangent_full = gather_rows(cotangent_own)
        hidden_full = gather_rows(hidden_own)
        both_pre = jnp.dot(hidden_full, both_own, preferred_element_type=F32) + both_bias
        gate_pre, up_pre = both_pre[:, :ffn_pad], both_pre[:, ffn_pad:]
        activated, gelu_pull = jax.vjp(gelu_tanh, gate_pre)
        hidden_ffn = (activated * up_pre).astype(BF16)
        hidden_grad = dot(cotangent_full, down_own, ((1,), (1,)))
        gate_grad = gelu_pull(hidden_grad * up_pre)[0].astype(BF16)
        up_grad = (hidden_grad * activated).astype(BF16)
        both_grad = jnp.concatenate([gate_grad, up_grad], axis=1)
        normed_grad = sum_rows(dot(both_grad, both_own, ((1,), (1,))), 512, 1, "sum_hidden")
        ffn_out = sum_rows(
            jnp.dot(hidden_ffn, down_own, preferred_element_type=F32), 512, 1, "sum_hidden"
        )
        own_cotangent = lax.dynamic_slice_in_dim(cotangent_full, device * rows, rows, 1)
        shares = (
            dot(hidden_full, both_grad, ((0,), (0,))),
            dot(hidden_ffn, cotangent_full, ((0,), (0,))),
            jnp.sum(both_grad.astype(F32), axis=0),
            jnp.sum(own_cotangent.astype(F32), axis=0),
        )
        if sums is not None:
            shares = jax.tree.map(jnp.add, sums, shares)
        return shares, (normed_grad, ffn_out)

    pieces = max(1, peers // DEVICES)
    if pieces == 1:
        shares, (normed_grad, ffn_out) = piece(None, (hidden_two, out_cotangent))
    else:
        zeros = (
            jnp.zeros((width, 2 * ffn_pad), F32),
            jnp.zeros((ffn_pad, width), F32),
            jnp.zeros((2 * ffn_pad,), F32),
            jnp.zeros((rows,), F32),
        )
        cut = (pieces, tok_rows // pieces, width)
        shares, outs = lax.scan(piece, zeros, (hidden_two.reshape(cut), out_cotangent.reshape(cut)))
        normed_grad, ffn_out = (part.reshape(tok_rows, width) for part in outs)
    return (normed_grad, ffn_out) + shares


def body(
    layer_input,
    norm1_scale,
    query_weight,
    keyvalue_weight,
    out_weight,
    norm2_scale,
    gate_weight,
    gate_bias,
    up_weight,
    up_bias,
    down_weight,
    down_bias,
    out_cotangent,
):
    peers = lax.axis_size(AXIS)
    device = lax.axis_index(AXIS)
    tok_rows, width = layer_input.shape
    rows = query_weight.shape[0]
    query_cols = query_weight.shape[1]
    kv_cols = keyvalue_weight.shape[1]
    heads = query_cols // HD
    quarter = HD // 4
    query_scale = 1.0 / math.sqrt(HD)
    ffn_own = down_weight.shape[0]
    ffn_pad = round_up(ffn_own, LANES)

    vectors = jnp.stack([norm1_scale, norm2_scale, down_bias], axis=1)
    first = gather_rows(
        jnp.concatenate([query_weight, keyvalue_weight, pad_columns(vectors, LANES)], axis=1)
    )
    proj_cols = query_cols + kv_cols
    proj_full = first[:, :proj_cols]
    gains = first[:, proj_cols:].astype(F32).T
    gain_one, gain_two, bias_down = gains[0], gains[1], gains[2]

    resid_in = layer_input.astype(F32)
    square_one = jnp.mean(resid_in * resid_in, axis=1, keepdims=True)
    scale_one = lax.rsqrt(square_one + EPSILON)
    normed_one = resid_in * scale_one
    hidden_one = (normed_one * gain_one).astype(BF16)
    projected = jnp.dot(hidden_one, proj_full, preferred_element_type=F32)
    position = device * tok_rows + jnp.arange(tok_rows, dtype=jnp.int32)
    cosine, sine_table = rotary_tables(position.astype(F32), quarter)
    queries = (
        rotate(
            projected[:, :query_cols].reshape(tok_rows, heads, HD),
            cosine[:, None, :],
            sine_table[:, None, :],
            quarter,
        )
        * query_scale
    ).astype(BF16)
    queries = queries.reshape(tok_rows, query_cols)
    keys_rot = rotate(projected[:, query_cols : query_cols + HD], cosine, sine_table, quarter)
    own_kv = jnp.concatenate([keys_rot, projected[:, query_cols + HD :]], axis=1).astype(BF16)

    reach = min((WINDOW + tok_rows - 2) // tok_rows, peers - 1)
    window_rows = (reach + 1) * tok_rows
    window_start = jnp.maximum(device - reach, 0) * tok_rows
    kv_window = lax.dynamic_slice_in_dim(gather_rows(own_kv), window_start, window_rows, 0)
    place = (device * tok_rows - window_start).astype(jnp.int32).reshape(1)
    attention, logs = attend(place, queries, kv_window)

    out_full = gather_rows(out_weight)
    residual_mid = resid_in + jnp.dot(attention, out_full, preferred_element_type=F32)
    square_two = jnp.mean(residual_mid * residual_mid, axis=1, keepdims=True)
    scale_two = lax.rsqrt(square_two + EPSILON)
    normed_two = residual_mid * scale_two
    hidden_two = (normed_two * gain_two).astype(BF16)

    gate_pieces = pad_columns(gate_weight.reshape(rows, peers, ffn_own), ffn_pad)
    up_pieces = pad_columns(up_weight.reshape(rows, peers, ffn_own), ffn_pad)
    both_own = swap(
        jnp.concatenate([gate_pieces, up_pieces], axis=2).transpose(1, 0, 2)
    ).reshape(peers * rows, 2 * ffn_pad)
    both_bias = jnp.concatenate(
        [pad_columns(gate_bias, ffn_pad), pad_columns(up_bias, ffn_pad)]
    ).astype(F32)
    down_own = jnp.pad(down_weight, ((0, ffn_pad - ffn_own), (0, 0)))

    normed_grad_two, ffn_out, grad_both, grad_down, bias_share, down_bias_share = feed_forward(
        hidden_two, out_cotangent, both_own, both_bias, down_own, rows
    )
    layer_output = (residual_mid + (ffn_out + bias_down)).astype(BF16)
    rms_values = jnp.stack(
        [jnp.sqrt(square_one[:, 0] + EPSILON), jnp.sqrt(square_two[:, 0] + EPSILON)], axis=0
    )
    grad_down = grad_down[:ffn_own]
    grad_both = swap(grad_both.astype(BF16).reshape(peers, rows, 2 * ffn_pad)).transpose(1, 0, 2)
    grad_both = grad_both.astype(F32)
    grad_gate = grad_both[:, :, :ffn_own].reshape(rows, peers * ffn_own)
    grad_up = grad_both[:, :, ffn_pad : ffn_pad + ffn_own].reshape(rows, peers * ffn_own)

    norm2_part = jnp.sum(normed_grad_two * normed_two, axis=0)
    weighted_two = normed_grad_two * gain_two
    mid_grad = out_cotangent.astype(F32) + scale_two * (
        weighted_two - normed_two * jnp.mean(weighted_two * normed_two, axis=1, keepdims=True)
    )
    mid_grad_low = mid_grad.astype(BF16)
    attention_grad = dot(mid_grad_low, out_full, ((1,), (1,))).astype(BF16)
    grad_out = sum_rows(dot(attention, mid_grad_low, ((0,), (0,))), 640, 2, "sum_grad_out")

    query_grad, kv_part = attend_back(place, queries, kv_window, logs, attention_grad)
    kv_partial = lax.dynamic_update_slice_in_dim(
        jnp.zeros((peers * tok_rows, 2 * HD), BF16), kv_part.astype(BF16), window_start, 0
    )
    kv_grad = sum_rows(kv_partial, 256, 3, "sum_grad_kv")
    query_raw_grad = (
        rotate(
            query_grad.reshape(tok_rows, heads, HD) * query_scale,
            cosine[:, None, :],
            -sine_table[:, None, :],
            quarter,
        )
        .reshape(tok_rows, query_cols)
        .astype(BF16)
    )
    key_raw_grad = rotate(kv_grad[:, :HD], cosine, -sine_table, quarter)
    kv_raw_grad = jnp.concatenate([key_raw_grad, kv_grad[:, HD:]], axis=1).astype(BF16)
    proj_grad = jnp.concatenate([query_raw_grad, kv_raw_grad], axis=1)
    normed_grad_one = dot(proj_grad, proj_full, ((1,), (1,)))
    norm1_part = jnp.sum(normed_grad_one * normed_one, axis=0)
    weighted_one = normed_grad_one * gain_one
    input_grad = (
        mid_grad
        + scale_one
        * (weighted_one - normed_one * jnp.mean(weighted_one * normed_one, axis=1, keepdims=True))
    ).astype(BF16)

    parts = pad_columns(jnp.stack([norm1_part, norm2_part], axis=1), LANES)
    tail = jnp.concatenate([dot(hidden_one, proj_grad, ((0,), (0,))), parts], axis=1)
    tail = sum_rows(tail, 640, 4, "sum_grad_proj")
    grad_proj = tail[:, :proj_cols]
    norm1_share = tail[:, proj_cols]
    norm2_share = tail[:, proj_cols + 1]
    return (
        layer_output,
        residual_mid,
        rms_values,
        input_grad,
        norm1_share,
        grad_proj[:, :query_cols],
        grad_proj[:, query_cols:],
        grad_out,
        norm2_share,
        grad_gate,
        bias_share[:ffn_own],
        grad_up,
        bias_share[ffn_pad : ffn_pad + ffn_own],
        grad_down,
        down_bias_share,
    )


def solution(mesh):
    by_rows, by_entry = P(AXIS, None), P(AXIS)
    in_specs = (
        by_rows,
        by_entry,
        by_rows,
        by_rows,
        by_rows,
        by_entry,
        by_rows,
        by_entry,
        by_rows,
        by_entry,
        by_rows,
        by_entry,
        by_rows,
    )
    out_specs = (
        by_rows,
        by_rows,
        P(None, AXIS),
        by_rows,
        by_entry,
        by_rows,
        by_rows,
        by_rows,
        by_entry,
        by_rows,
        by_entry,
        by_rows,
        by_entry,
        by_rows,
        by_entry,
    )
    return jax.shard_map(body, mesh=mesh, in_specs=in_specs, out_specs=out_specs, check_vma=False)
```

```python
import functools
import math

import jax
import jax.numpy as jnp
from jax import lax
from jax.experimental import pallas as pl
from jax.experimental.pallas import tpu as pltpu
from jax.sharding import PartitionSpec as P

HD = 256
WINDOW = 2048
EPSILON = 1e-06
NEGATIVE = -1e30
ROTARY_BASE = 10000.0
AXIS = "blk"
LANES = 128
DEVICES = 32
PAIR = 2
VMEM_BYTES = 48 * 1024 * 1024
F32 = jnp.float32
BF16 = jnp.bfloat16


def rotary_tables(positions, quarter):
    frequency = ROTARY_BASE ** (-(jnp.arange(quarter, dtype=F32) / quarter))
    angles = positions[:, None] * frequency[None, :]
    return (jnp.cos(angles), jnp.sin(angles))


def rotate(vector, cosine, sine_table, quarter):
    leading = vector[..., :quarter]
    trailing = vector[..., quarter : 2 * quarter]
    return jnp.concatenate(
        [
            leading * cosine - trailing * sine_table,
            trailing * cosine + leading * sine_table,
            vector[..., 2 * quarter :],
        ],
        axis=-1,
    )


def dot(left, right, contract):
    return lax.dot_general(left, right, (contract, ((), ())), preferred_element_type=F32)


def round_up(count, step):
    return (count + step - 1) // step * step


def pad_columns(values, columns):
    pad = [(0, 0)] * (values.ndim - 1) + [(0, columns - values.shape[-1])]
    return jnp.pad(values, pad)


def masked_scores(place_ref, query_rows, keys, tok_rows):
    scores = dot(query_rows, keys, ((1,), (1,)))
    rows = lax.broadcasted_iota(jnp.int32, scores.shape, 0) % tok_rows
    columns = lax.broadcasted_iota(jnp.int32, scores.shape, 1)
    distance = rows - columns + place_ref[0]
    return jnp.where((distance >= 0) & (distance < WINDOW), scores, NEGATIVE)


def stack_heads(block):
    return jnp.concatenate([block[:, i * HD : (i + 1) * HD] for i in range(PAIR)], axis=0)


def unstack_heads(rows):
    tok_rows = rows.shape[0] // PAIR
    return jnp.concatenate([rows[i * tok_rows : (i + 1) * tok_rows] for i in range(PAIR)], axis=1)


def attend_kernel(place_ref, query_ref, kv_ref, out_ref, log_ref):
    tok_rows = query_ref.shape[0]
    scores = masked_scores(place_ref, stack_heads(query_ref[...]), kv_ref[:, :HD], tok_rows)
    row_max = jnp.max(scores, axis=1, keepdims=True)
    probs = jnp.exp(scores - row_max)
    row_sum = jnp.sum(probs, axis=1, keepdims=True)
    probs_low = (probs * (1.0 / row_sum)).astype(BF16)
    attended = dot(probs_low, kv_ref[:, HD:], ((1,), (0,)))
    out_ref[...] = unstack_heads(attended).astype(BF16)
    log_ref[0] = jnp.broadcast_to(row_max + jnp.log(row_sum), log_ref.shape[1:])


def attend_back_kernel(place_ref, query_ref, kv_ref, log_ref, grad_ref, query_grad_ref, kv_grad_ref):
    tok_rows = query_ref.shape[0]
    query_rows = stack_heads(query_ref[...])
    grad_rows = stack_heads(grad_ref[...])
    keys, values = kv_ref[:, :HD], kv_ref[:, HD:]
    scores = masked_scores(place_ref, query_rows, keys, tok_rows)
    probs = jnp.exp(scores - log_ref[0][:, :1])
    prob_grad = dot(grad_rows, values, ((1,), (1,)))
    delta = jnp.sum(probs * prob_grad, axis=1, keepdims=True)
    score_grad = (probs * (prob_grad - delta)).astype(BF16)
    query_grad_ref[...] = unstack_heads(dot(score_grad, keys, ((1,), (0,))))
    key_part = dot(score_grad, query_rows, ((0,), (0,)))
    value_part = dot(probs.astype(BF16), grad_rows, ((0,), (0,)))

    @pl.when(pl.program_id(0) == 0)
    def _():
        kv_grad_ref[:, :HD] = key_part
        kv_grad_ref[:, HD:] = value_part

    @pl.when(pl.program_id(0) > 0)
    def _():
        kv_grad_ref[:, :HD] += key_part
        kv_grad_ref[:, HD:] += value_part


def attention_specs(tok_rows, heads, window_rows):
    place = pl.BlockSpec(memory_space=pltpu.SMEM)
    by_head = pl.BlockSpec((tok_rows, PAIR * HD), lambda i: (0, i))
    whole = pl.BlockSpec((window_rows, 2 * HD), lambda i: (0, 0))
    logs = pl.BlockSpec((1, PAIR * tok_rows, LANES), lambda i: (i, 0, 0))
    return place, by_head, whole, logs


def attend(place, queries, kv_window):
    tok_rows, features = queries.shape
    window_rows = kv_window.shape[0]
    pairs = features // HD // PAIR
    place_spec, by_head, whole, logs = attention_specs(tok_rows, features // HD, window_rows)
    work = tok_rows * features * window_rows
    return pl.pallas_call(
        attend_kernel,
        grid=(pairs,),
        out_shape=(
            jax.ShapeDtypeStruct((tok_rows, features), BF16),
            jax.ShapeDtypeStruct((pairs, PAIR * tok_rows, LANES), F32),
        ),
        in_specs=[place_spec, by_head, whole],
        out_specs=(by_head, logs),
        compiler_params=pltpu.CompilerParams(vmem_limit_bytes=VMEM_BYTES),
        cost_estimate=pl.CostEstimate(
            flops=4 * work, bytes_accessed=8 * kv_window.size, transcendentals=work // HD
        ),
        name="attend",
    )(place, queries, kv_window)


def attend_back(place, queries, kv_window, logs_in, grad):
    tok_rows, features = queries.shape
    window_rows = kv_window.shape[0]
    pairs = features // HD // PAIR
    place_spec, by_head, whole, logs = attention_specs(tok_rows, features // HD, window_rows)
    work = tok_rows * features * window_rows
    return pl.pallas_call(
        attend_back_kernel,
        grid=(pairs,),
        out_shape=(
            jax.ShapeDtypeStruct((tok_rows, features), F32),
            jax.ShapeDtypeStruct((window_rows, 2 * HD), F32),
        ),
        in_specs=[place_spec, by_head, whole, logs, by_head],
        out_specs=(by_head, whole),
        compiler_params=pltpu.CompilerParams(vmem_limit_bytes=VMEM_BYTES),
        cost_estimate=pl.CostEstimate(
            flops=10 * work, bytes_accessed=8 * kv_window.size, transcendentals=work // HD
        ),
        name="attend_back",
    )(place, queries, kv_window, logs_in, grad)


MESH=pl.DeviceIdType.MESH

class Place:
    def __init__(self):
        me = lax.axis_index(AXIS)
        self.core = me % 2
        self.x = (me // 2) % 2
        self.y = (me // 4) % 2
        self.z = me // 8
        self.sibling = self.index(self.z, self.y, self.x, 1 - self.core)
        self.next_x = self.index(self.z, self.y, 1 - self.x, self.core)
        self.next_y = self.index(self.z, 1 - self.y, self.x, self.core)
        self.plane = [self.z] + [(self.z + o) % 4 for o in (1, 2, 3)]
        self.line = [self.index(p, self.y, self.x, self.core) for p in self.plane]
    def index(self, z, y, x, core):
        return ((z * 2 + y) * 2 + x) * 2 + core
    def side(self, dy, dx):
        return (1 - self.y if dy else self.y), (1 - self.x if dx else self.x)
    def meet(self):
        barrier = pltpu.get_barrier_semaphore()
        partners = [self.sibling, self.next_x, self.next_y] + self.line[1:]
        for device in partners:
            pl.semaphore_signal(barrier, inc=1, device_id=(device,), device_id_type=MESH)
        pl.semaphore_wait(barrier, len(partners))

def send(src, dst, sems, device):
    copy = pltpu.make_async_remote_copy(src_ref=src, dst_ref=dst, send_sem=sems[0], recv_sem=sems[1], device_id=(device,), device_id_type=MESH)
    copy.start()
    return copy

TILE=16
def add_rows(total, other, first, count):
    planes = other.shape[0]
    steps = count // TILE
    @pl.loop(0, planes * steps)
    def _(i):
        plane, row = i // steps, (i % steps) * TILE
        here = (plane, pl.ds(pl.multiple_of(row + first, TILE), TILE), slice(None))
        there = (plane, pl.ds(pl.multiple_of(row, TILE), TILE), slice(None))
        total[here] = (total[here].astype(F32) + other[there].astype(F32)).astype(BF16)

def sum_kernel(chunk, in_ref, out_ref, acc, got_core, got_diag_x, got_diag_y, got_x, got_y, got_z,
               load_sem, core_sems, diag_sems, side_sems, line_sems):
    place = Place()
    rows, columns = out_ref.shape
    upper = got_diag_x.shape[1]
    lower = rows - upper
    chunks = columns // chunk
    corners = [(1, 1), (0, 1), (1, 0), (0, 0)]
    cols = [pl.ds(k * chunk, chunk) for k in range(chunks)]
    loads, cores, sends = {}, {}, []
    for k in range(chunks):
        for i, (dy, dx) in enumerate(corners):
            y, x = place.side(dy, dx)
            load = pltpu.make_async_copy(in_ref.at[:, y, x, place.core, :, cols[k]], acc.at[i, :, :, cols[k]], load_sem.at[k, i])
            load.start()
            loads[k, i] = load
    place.meet()
    for k in range(chunks):
        for i, (dy, dx) in enumerate(corners):
            y, x = place.side(dy, dx)
            cores[k, i] = send(in_ref.at[:, y, x, 1 - place.core, :, cols[k]], got_core.at[i, :, :, cols[k]],
                               (core_sems.at[0, k, i], core_sems.at[1, k, i]), place.sibling)
    top, bottom = pl.ds(0, upper), pl.ds(upper, lower)
    diag, side, line = {}, {}, {}
    def pair(sems, k, i): return (sems.at[0, k, i], sems.at[1, k, i])
    def stage0(k):
        for i in range(4):
            loads[k, i].wait(); cores[k, i].wait_recv()
            add_rows(acc.at[i, :, :, cols[k]], got_core.at[i, :, :, cols[k]], 0, rows)
            if i == 0:
                diag[k, 0] = send(acc.at[0, :, top, cols[k]], got_diag_x.at[:, :, cols[k]], pair(diag_sems, k, 0), place.next_x)
                diag[k, 1] = send(acc.at[0, :, bottom, cols[k]], got_diag_y.at[:, :, cols[k]], pair(diag_sems, k, 1), place.next_y)
            if i == 1:
                side[k, 0] = send(acc.at[1, :, top, cols[k]], got_x.at[:, top, cols[k]], pair(side_sems, k, 0), place.next_x)
            if i == 2:
                side[k, 1] = send(acc.at[2, :, bottom, cols[k]], got_y.at[:, bottom, cols[k]], pair(side_sems, k, 1), place.next_y)
    def stage1(k):
        diag[k, 0].wait_recv()
        add_rows(acc.at[2, :, :, cols[k]], got_diag_x.at[:, :, cols[k]], 0, upper)
        side[k, 2] = send(acc.at[2, :, top, cols[k]], got_y.at[:, top, cols[k]], pair(side_sems, k, 2), place.next_y)
        diag[k, 1].wait_recv()
        add_rows(acc.at[1, :, :, cols[k]], got_diag_y.at[:, :, cols[k]], upper, lower)
        side[k, 3] = send(acc.at[1, :, bottom, cols[k]], got_x.at[:, bottom, cols[k]], pair(side_sems, k, 3), place.next_x)
    def stage2(k):
        for i in range(4): side[k, i].wait_recv()
        steps = rows // TILE
        @pl.loop(0, 4 * steps)
        def _(i):
            plane, row = i // steps, (i % steps) * TILE
            here = (plane, pl.ds(pl.multiple_of(row, TILE), TILE), cols[k])
            acc[(3,) + here] = (acc[(3,) + here].astype(F32) + got_x[here].astype(F32) + got_y[here].astype(F32)).astype(BF16)
        for o in (1, 2, 3):
            line[k, o] = send(acc.at[3, place.plane[o], :, cols[k]], got_z.at[o - 1, :, cols[k]], pair(line_sems, k, o - 1), place.line[o])
    def stage3(k):
        for o in (1, 2, 3): line[k, o].wait_recv()
        @pl.loop(0, rows // TILE)
        def _(i):
            here = (pl.ds(pl.multiple_of(i * TILE, TILE), TILE), cols[k])
            total = acc[(3, place.z) + here].astype(F32)
            for o in range(3): total += got_z[(o,) + here].astype(F32)
            out_ref[here] = total
    stages = [stage0, stage1, stage2, stage3]
    for step in range(chunks + 3):
        for s in range(3, -1, -1):
            if 0 <= step - s < chunks: stages[s](step - s)
    for group in (cores, diag, side, line):
        for copy in group.values(): copy.wait_send()

def sum_over_devices(partial, chunk, collective_id, name):
    rows, columns = partial.shape[0] // 32, partial.shape[1]
    chunks = columns // chunk
    upper = (rows // 2 + TILE - 1) // TILE * TILE
    def buf(*shape): return pltpu.VMEM(shape, BF16)
    def sems(count): return pltpu.SemaphoreType.DMA((2, chunks, count))
    return pl.pallas_call(
        functools.partial(sum_kernel, chunk),
        out_shape=jax.ShapeDtypeStruct((rows, columns), F32),
        in_specs=[pl.BlockSpec(memory_space=pl.ANY)],
        out_specs=pl.BlockSpec(memory_space=pltpu.VMEM),
        scratch_shapes=[buf(4, 4, rows, columns), buf(4, 4, rows, columns), buf(4, upper, columns), buf(4, rows - upper, columns),
            buf(4, rows, columns), buf(4, rows, columns), buf(3, rows, columns),
            pltpu.SemaphoreType.DMA((chunks, 4)), sems(4), sems(2), sems(4), sems(3)],
        compiler_params=pltpu.CompilerParams(collective_id=collective_id, has_side_effects=True, vmem_limit_bytes=56*1024*1024),
        name=name,
    )(partial.reshape(4, 2, 2, 2, rows, columns))


PLANES=4
def plane_order(z):
    near = jnp.minimum(z, 3 - z)
    flip = z // 2
    order = []
    for k in range(4):
        swapped = 1 - k if k < 2 else k
        plane = near * swapped + (1 - near) * k
        order.append(flip * (3 - plane) + (1 - flip) * plane)
    return order

class Gather:
    COPIES = 11
    def __init__(self, place, own, held, cols, sems):
        self.place, self.held, self.cols, self.sems = place, held, cols, sems
        self.own = own.at[:, cols]
        rows = held.shape[4]
        upper = (rows // 2 + TILE - 1) // TILE * TILE
        self.halves = pl.ds(0, upper), pl.ds(upper, rows - upper)
        self.order = plane_order(place.z)
        self.sent = []
        self.kept = []
    def at(self, plane, y, x, core, part=slice(None)):
        return self.held.at[plane, y, x, core, part, self.cols]
    def pair(self, slot, k):
        return self.sems.at[0, slot, k], self.sems.at[1, slot, k]
    def push(self, src, dst, slot, k, device):
        copy = send(src, dst, self.pair(slot, k), device)
        self.sent.append(copy)
    def arrived(self, ref, slot, k):
        pltpu.make_async_remote_copy(src_ref=ref, dst_ref=ref, send_sem=self.sems.at[0, slot, k], recv_sem=self.sems.at[1, slot, k], device_id=(self.place.sibling,), device_id_type=MESH).wait_recv()
    def start(self):
        p = self.place
        mine = self.at(p.z, p.y, p.x, p.core)
        keep = pltpu.make_async_copy(self.own, mine, self.sems.at[0, 10, 0])
        keep.start()
        self.kept.append(keep)
        for k in (1, 2, 3):
            plane = self.order[k]
            copy = pltpu.make_async_remote_copy(src_ref=self.own, dst_ref=mine, send_sem=self.sems.at[0, 0, k], recv_sem=self.sems.at[1, 0, p.z], device_id=(p.index(plane, p.y, p.x, p.core),), device_id_type=MESH)
            copy.start(); self.sent.append(copy)
    def line(self, k):
        p = self.place
        plane = self.order[k]
        block = self.at(plane, p.y, p.x, p.core)
        source = self.own if k == 0 else block
        if k > 0:
            pltpu.make_async_remote_copy(src_ref=block, dst_ref=block, send_sem=self.sems.at[0, 0, k], recv_sem=self.sems.at[1, 0, plane], device_id=(p.sibling,), device_id_type=MESH).wait_recv()
        self.push(source, block, 1, k, p.next_x)
        self.push(source, block, 2, k, p.next_y)
        self.push(source, block, 5, k, p.sibling)
    def side(self, k):
        p, plane = self.place, self.order[k]
        top, bottom = self.halves
        self.arrived(self.at(plane, p.y, 1 - p.x, p.core), 1, k)
        block = self.at(plane, p.y, 1 - p.x, p.core, top)
        self.push(block, block, 4, k, p.next_y)
        block = self.at(plane, p.y, 1 - p.x, p.core)
        self.push(block, block, 6, k, p.sibling)
        self.arrived(self.at(plane, 1 - p.y, p.x, p.core), 2, k)
        block = self.at(plane, 1 - p.y, p.x, p.core, bottom)
        self.push(block, block, 3, k, p.next_x)
        block = self.at(plane, 1 - p.y, p.x, p.core)
        self.push(block, block, 7, k, p.sibling)
    def diag(self, k):
        p, plane = self.place, self.order[k]
        for slot, part in ((4, self.halves[0]), (3, self.halves[1])):
            block = self.at(plane, 1 - p.y, 1 - p.x, p.core, part)
            self.arrived(block, slot, k)
            self.push(block, block, slot + 5, k, p.sibling)
    def ready(self, k):
        p, plane = self.place, self.order[k]
        top, bottom = self.halves
        if k == 0:
            for keep in self.kept: keep.wait()
        other = 1 - p.core
        self.arrived(self.at(plane, p.y, p.x, other), 5, k)
        self.arrived(self.at(plane, p.y, 1 - p.x, other), 6, k)
        self.arrived(self.at(plane, 1 - p.y, p.x, other), 7, k)
        self.arrived(self.at(plane, 1 - p.y, 1 - p.x, other, top), 9, k)
        self.arrived(self.at(plane, 1 - p.y, 1 - p.x, other, bottom), 8, k)
    def finish(self):
        for copy in self.sent: copy.wait_send()

def pipeline(stages, count):
    for step in range(count + len(stages) - 1):
        for s in range(len(stages) - 1, -1, -1):
            if 0 <= step - s < count:
                stages[s](step - s)

def gather_kernel(chunks, *refs):
    n = len(chunks)
    ins, outs, sems = refs[:n], refs[n:2*n], refs[2*n:]
    place = Place()
    place.meet()
    items = []
    for a in range(n):
        width = ins[a].shape[1] // chunks[a]
        for j in range(chunks[a]):
            items.append(Gather(place, ins[a], outs[a], pl.ds(j * width, width), sems[a].at[j]))
    def line(s):
        if s % PLANES == 0:
            items[s // PLANES].start()
        items[s // PLANES].line(s % PLANES)
    def side(s): items[s // PLANES].side(s % PLANES)
    def diag(s): items[s // PLANES].diag(s % PLANES)
    pipeline([line, side, diag], len(items) * PLANES)
    for item in items:
        for k in range(PLANES): item.ready(k)
    for item in items: item.finish()

def gather_all(arrays, chunks, collective_id, name):
    outs = pl.pallas_call(
        functools.partial(gather_kernel, chunks),
        out_shape=tuple(jax.ShapeDtypeStruct((4,2,2,2)+a.shape, BF16) for a in arrays),
        in_specs=[pl.BlockSpec(memory_space=pl.ANY)]*len(arrays),
        out_specs=tuple(pl.BlockSpec(memory_space=pl.ANY) for _ in arrays),
        scratch_shapes=[pltpu.SemaphoreType.DMA((c, 2, Gather.COPIES, PLANES)) for c in chunks],
        compiler_params=pltpu.CompilerParams(collective_id=collective_id, has_side_effects=True),
        name=name,
    )(*arrays)
    return [o.reshape(32 * a.shape[0], a.shape[1]) for o, a in zip(outs, arrays)]


GELU_SCALE = math.sqrt(2.0 / math.pi)
GELU_CUBE = 0.044715

def gelu_and_slope(v):
    square = v * v
    t = jnp.tanh(GELU_SCALE * v * (1.0 + GELU_CUBE * square))
    half = 0.5 * (1.0 + t)
    slope = half + 0.5 * v * (1.0 - t * t) * (GELU_SCALE * (1.0 + 3.0 * GELU_CUBE * square))
    return v * half, slope

def ffn_kernel(hidden_ref, cotangent_ref, both_ref, down_ref, bias_ref,
               hidden_out, ffn_out, grad_both_ref, grad_down_ref, bias_grad_ref,
               held, cot, both_keep, ffn_keep, stage, gather_sems, cot_sems, out_sems):
    place = Place()
    width = hidden_ref.shape[1]
    pad = down_ref.shape[0]
    rows = 2 * hidden_ref.shape[0]
    order = plane_order(place.z)
    fetch = [pltpu.make_async_copy(cotangent_ref.at[order[k]], cot.at[k % 2], cot_sems.at[k]) for k in range(PLANES)]
    fetch[0].start()
    fetch[1].start()
    place.meet()
    gather = Gather(place, hidden_ref, held, pl.ds(0, width), gather_sems)
    gather.start()
    grad_both_ref[...] = jnp.zeros_like(grad_both_ref)
    grad_down_ref[...] = jnp.zeros_like(grad_down_ref)
    bias_grad_ref[...] = jnp.zeros_like(bias_grad_ref)

    def emit(kind, slot, plane, y, x):
        target = (hidden_out, ffn_out)[kind]
        return pltpu.make_async_copy(stage.at[kind, slot], target.at[plane, y, x], out_sems.at[kind, slot])

    def compute(k):
        plane = order[k]
        fetch[k].wait()
        @pl.loop(0, 4)
        def _(i):
            y, x, slot = i // 2, i % 2, i % 2
            hidden = held[plane, y, x].reshape(rows, width)
            cotangent = cot[k % 2, y, x].reshape(rows, width)
            both_pre = dot(hidden, both_ref[...], ((1,), (0,))) + bias_ref[0:1]
            hidden_grad = dot(cotangent, down_ref[...], ((1,), (1,)))
            activated, slope = gelu_and_slope(both_pre[:, :pad])
            up_pre = both_pre[:, pad:]
            hidden_ffn = (activated * up_pre).astype(BF16)
            both_grad = jnp.concatenate([(hidden_grad * up_pre * slope).astype(BF16), (hidden_grad * activated).astype(BF16)], axis=1)
            here = pl.ds(pl.multiple_of(i * rows, rows), rows)
            both_keep[here] = both_grad
            ffn_keep[here] = hidden_ffn
            bias_grad_ref[...] += jnp.sum(both_grad.astype(F32), axis=0, keepdims=True)
            def drain():
                for kind in range(2): emit(kind, slot, plane, y, x).wait()
            if k > 0: drain()
            else: pl.when(i >= 2)(drain)
            half = stage.shape[3]
            stage[0, slot] = dot(both_grad, both_ref[...], ((1,), (1,))).astype(BF16).reshape(2, half, width)
            emit(0, slot, plane, y, x).start()
            stage[1, slot] = dot(hidden_ffn, down_ref[...], ((1,), (0,))).astype(BF16).reshape(2, half, width)
            emit(1, slot, plane, y, x).start()
        step = 512
        @pl.loop(0, width // step)
        def _(j):
            cols = pl.ds(pl.multiple_of(j * step, step), step)
            hidden = held[plane, :, :, :, :, cols].reshape(4 * rows, step)
            grad_both_ref[:, cols] += dot(both_keep[...], hidden, ((0,), (0,)))
            cotangent = cot[k % 2, :, :, :, :, cols].reshape(4 * rows, step)
            grad_down_ref[:, cols] += dot(ffn_keep[...], cotangent, ((0,), (0,)))
        if k + 2 < PLANES: fetch[k + 2].start()

    gather.line(0)
    gather.line(1)
    gather.side(0)
    gather.line(2)
    gather.side(1)
    gather.diag(0)
    gather.ready(0)
    compute(0)
    gather.line(3)
    gather.side(2)
    gather.diag(1)
    gather.side(3)
    gather.ready(1)
    compute(1)
    gather.diag(2)
    gather.diag(3)
    gather.ready(2)
    compute(2)
    gather.ready(3)
    compute(3)
    for slot in range(2):
        for kind in range(2): emit(kind, slot, 0, 0, 0).wait()
    gather.finish()

def ffn(hidden_two, cotangent_full, both_own, both_bias, down_own, collective_id):
    tok_rows, width = hidden_two.shape
    pad = down_own.shape[0]
    full = (4, 2, 2, 2, tok_rows, width)
    hbm = pl.BlockSpec(memory_space=pl.ANY)
    vmem = pl.BlockSpec(memory_space=pltpu.VMEM)
    dma = pltpu.SemaphoreType.DMA
    hidden_part, ffn_part, grad_both, grad_down, bias_grad = pl.pallas_call(
        ffn_kernel,
        out_shape=(
            jax.ShapeDtypeStruct(full, BF16),
            jax.ShapeDtypeStruct(full, BF16),
            jax.ShapeDtypeStruct((2 * pad, width), F32),
            jax.ShapeDtypeStruct((pad, width), F32),
            jax.ShapeDtypeStruct((8, 2 * pad), F32),
        ),
        in_specs=[hbm, hbm, vmem, vmem, vmem],
        out_specs=(hbm, hbm, vmem, vmem, vmem),
        scratch_shapes=[
            pltpu.VMEM(full, BF16),
            pltpu.VMEM((2,) + full[1:], BF16),
            pltpu.VMEM((8 * tok_rows, 2 * pad), BF16),
            pltpu.VMEM((8 * tok_rows, pad), BF16),
            pltpu.VMEM((2, 2, 2, tok_rows, width), BF16),
            dma((2, Gather.COPIES, PLANES)), dma((PLANES,)), dma((2, 2)),
        ],
        compiler_params=pltpu.CompilerParams(collective_id=collective_id, has_side_effects=True, vmem_limit_bytes=62*1024*1024),
        name="feed_forward",
    )(hidden_two, cotangent_full.reshape(full), both_own, down_own, jnp.broadcast_to(both_bias, (8, 2 * pad)))
    return (hidden_part.reshape(32 * tok_rows, width), ffn_part.reshape(32 * tok_rows, width), grad_both, grad_down, bias_grad[0])


def gather_rows(arrays, collective_id, name):
    if lax.axis_size(AXIS) == DEVICES:
        return gather_all(arrays, [1] * len(arrays), collective_id, name)
    return [lax.all_gather(values, AXIS, axis=0, tiled=True) for values in arrays]


def sum_rows(partial, chunk, collective_id, name):
    if lax.axis_size(AXIS) == DEVICES:
        return sum_over_devices(partial.astype(BF16), chunk, collective_id, name)
    return lax.psum_scatter(
        partial.astype(BF16), AXIS, scatter_dimension=0, tiled=True
    ).astype(F32)


def swap(pieces):
    return lax.all_to_all(pieces, AXIS, 0, 0, tiled=False)


def feed_forward(hidden_two, cotangent_full, both_own, both_bias, down_own, rows):
    peers = lax.axis_size(AXIS)
    device = lax.axis_index(AXIS)
    tok_rows, width = hidden_two.shape
    ffn_pad = down_own.shape[0]
    own_cotangent = lax.dynamic_slice_in_dim(cotangent_full, device * rows, rows, 1)
    down_bias_share = jnp.sum(own_cotangent.astype(F32), axis=0)
    if peers == DEVICES:
        hidden_part, ffn_part, grad_both, grad_down, bias_share = ffn(
            hidden_two, cotangent_full, both_own, both_bias, down_own, 7
        )
        normed_grad = sum_rows(hidden_part, 512, 1, "sum_hidden")
        ffn_out = sum_rows(ffn_part, 512, 1, "sum_hidden")
        return normed_grad, ffn_out, grad_both.T, grad_down, bias_share, down_bias_share

    def piece(sums, here):
        hidden_own, cotangent_piece = here
        hidden_full = gather_rows([hidden_own], None, None)[0]
        both_pre = jnp.dot(hidden_full, both_own, preferred_element_type=F32) + both_bias
        activated, slope = gelu_and_slope(both_pre[:, :ffn_pad])
        up_pre = both_pre[:, ffn_pad:]
        hidden_ffn = (activated * up_pre).astype(BF16)
        hidden_grad = dot(cotangent_piece, down_own, ((1,), (1,)))
        gate_grad = (hidden_grad * up_pre * slope).astype(BF16)
        up_grad = (hidden_grad * activated).astype(BF16)
        both_grad = jnp.concatenate([gate_grad, up_grad], axis=1)
        normed_grad = sum_rows(dot(both_grad, both_own, ((1,), (1,))), None, None, None)
        ffn_out = sum_rows(
            jnp.dot(hidden_ffn, down_own, preferred_element_type=F32), None, None, None
        )
        shares = (
            dot(hidden_full, both_grad, ((0,), (0,))),
            dot(hidden_ffn, cotangent_piece, ((0,), (0,))),
            jnp.sum(both_grad.astype(F32), axis=0),
        )
        return jax.tree.map(jnp.add, sums, shares), (normed_grad, ffn_out)

    pieces = max(1, peers // DEVICES)
    cut = tok_rows // pieces
    zeros = (
        jnp.zeros((width, 2 * ffn_pad), F32),
        jnp.zeros((ffn_pad, width), F32),
        jnp.zeros((2 * ffn_pad,), F32),
    )
    cotangent_pieces = cotangent_full.reshape(peers, pieces, cut, width).transpose(1, 0, 2, 3)
    shares, outs = lax.scan(
        piece,
        zeros,
        (hidden_two.reshape(pieces, cut, width), cotangent_pieces.reshape(pieces, -1, width)),
    )
    normed_grad, ffn_out = (part.reshape(tok_rows, width) for part in outs)
    return (normed_grad, ffn_out) + shares + (down_bias_share,)


def body(
    layer_input,
    norm1_scale,
    query_weight,
    keyvalue_weight,
    out_weight,
    norm2_scale,
    gate_weight,
    gate_bias,
    up_weight,
    up_bias,
    down_weight,
    down_bias,
    out_cotangent,
):
    peers = lax.axis_size(AXIS)
    device = lax.axis_index(AXIS)
    tok_rows, width = layer_input.shape
    rows = query_weight.shape[0]
    query_cols = query_weight.shape[1]
    kv_cols = keyvalue_weight.shape[1]
    heads = query_cols // HD
    quarter = HD // 4
    query_scale = 1.0 / math.sqrt(HD)
    ffn_own = down_weight.shape[0]
    ffn_pad = round_up(ffn_own, LANES)

    vectors = jnp.stack([norm1_scale, norm2_scale, down_bias], axis=1)
    packed = jnp.concatenate(
        [query_weight, keyvalue_weight, pad_columns(vectors, LANES)], axis=1
    )
    first, out_full, cotangent_full = gather_rows(
        [packed, out_weight, out_cotangent], 5, "gather_weights"
    )
    proj_cols = query_cols + kv_cols
    proj_full = first[:, :proj_cols]
    gains = first[:, proj_cols:].astype(F32).T
    gain_one, gain_two, bias_down = gains[0], gains[1], gains[2]

    resid_in = layer_input.astype(F32)
    square_one = jnp.mean(resid_in * resid_in, axis=1, keepdims=True)
    scale_one = lax.rsqrt(square_one + EPSILON)
    normed_one = resid_in * scale_one
    hidden_one = (normed_one * gain_one).astype(BF16)
    projected = jnp.dot(hidden_one, proj_full, preferred_element_type=F32)
    position = device * tok_rows + jnp.arange(tok_rows, dtype=jnp.int32)
    cosine, sine_table = rotary_tables(position.astype(F32), quarter)
    queries = (
        rotate(
            projected[:, :query_cols].reshape(tok_rows, heads, HD),
            cosine[:, None, :],
            sine_table[:, None, :],
            quarter,
        )
        * query_scale
    ).astype(BF16)
    queries = queries.reshape(tok_rows, query_cols)
    keys_rot = rotate(projected[:, query_cols : query_cols + HD], cosine, sine_table, quarter)
    own_kv = jnp.concatenate([keys_rot, projected[:, query_cols + HD :]], axis=1).astype(BF16)

    reach = min((WINDOW + tok_rows - 2) // tok_rows, peers - 1)
    window_rows = (reach + 1) * tok_rows
    window_start = jnp.maximum(device - reach, 0) * tok_rows
    kv_window = lax.dynamic_slice_in_dim(gather_rows([own_kv], 6, "gather_kv")[0], window_start, window_rows, 0)
    place = (device * tok_rows - window_start).astype(jnp.int32).reshape(1)
    attention, logs = attend(place, queries, kv_window)

    residual_mid = resid_in + jnp.dot(attention, out_full, preferred_element_type=F32)
    square_two = jnp.mean(residual_mid * residual_mid, axis=1, keepdims=True)
    scale_two = lax.rsqrt(square_two + EPSILON)
    normed_two = residual_mid * scale_two
    hidden_two = (normed_two * gain_two).astype(BF16)

    gate_pieces = pad_columns(gate_weight.reshape(rows, peers, ffn_own), ffn_pad)
    up_pieces = pad_columns(up_weight.reshape(rows, peers, ffn_own), ffn_pad)
    both_own = swap(
        jnp.concatenate([gate_pieces, up_pieces], axis=2).transpose(1, 0, 2)
    ).reshape(peers * rows, 2 * ffn_pad)
    both_bias = jnp.concatenate(
        [pad_columns(gate_bias, ffn_pad), pad_columns(up_bias, ffn_pad)]
    ).astype(F32)
    down_own = jnp.pad(down_weight, ((0, ffn_pad - ffn_own), (0, 0)))

    normed_grad_two, ffn_out, grad_both, grad_down, bias_share, down_bias_share = feed_forward(
        hidden_two, cotangent_full, both_own, both_bias, down_own, rows
    )
    layer_output = (residual_mid + (ffn_out + bias_down)).astype(BF16)
    rms_values = jnp.stack(
        [jnp.sqrt(square_one[:, 0] + EPSILON), jnp.sqrt(square_two[:, 0] + EPSILON)], axis=0
    )
    grad_down = grad_down[:ffn_own]
    grad_both = swap(grad_both.astype(BF16).reshape(peers, rows, 2 * ffn_pad)).transpose(1, 0, 2)
    grad_both = grad_both.astype(F32)
    grad_gate = grad_both[:, :, :ffn_own].reshape(rows, peers * ffn_own)
    grad_up = grad_both[:, :, ffn_pad : ffn_pad + ffn_own].reshape(rows, peers * ffn_own)

    norm2_part = jnp.sum(normed_grad_two * normed_two, axis=0)
    weighted_two = normed_grad_two * gain_two
    mid_grad = out_cotangent.astype(F32) + scale_two * (
        weighted_two - normed_two * jnp.mean(weighted_two * normed_two, axis=1, keepdims=True)
    )
    mid_grad_low = mid_grad.astype(BF16)
    attention_grad = dot(mid_grad_low, out_full, ((1,), (1,))).astype(BF16)
    grad_out = sum_rows(dot(attention, mid_grad_low, ((0,), (0,))), 640, 2, "sum_grad_out")

    query_grad, kv_part = attend_back(place, queries, kv_window, logs, attention_grad)
    kv_partial = lax.dynamic_update_slice_in_dim(
        jnp.zeros((peers * tok_rows, 2 * HD), BF16), kv_part.astype(BF16), window_start, 0
    )
    kv_grad = sum_rows(kv_partial, 256, 3, "sum_grad_kv")
    query_raw_grad = (
        rotate(
            query_grad.reshape(tok_rows, heads, HD) * query_scale,
            cosine[:, None, :],
            -sine_table[:, None, :],
            quarter,
        )
        .reshape(tok_rows, query_cols)
        .astype(BF16)
    )
    key_raw_grad = rotate(kv_grad[:, :HD], cosine, -sine_table, quarter)
    kv_raw_grad = jnp.concatenate([key_raw_grad, kv_grad[:, HD:]], axis=1).astype(BF16)
    proj_grad = jnp.concatenate([query_raw_grad, kv_raw_grad], axis=1)
    normed_grad_one = dot(proj_grad, proj_full, ((1,), (1,)))
    norm1_part = jnp.sum(normed_grad_one * normed_one, axis=0)
    weighted_one = normed_grad_one * gain_one
    input_grad = (
        mid_grad
        + scale_one
        * (weighted_one - normed_one * jnp.mean(weighted_one * normed_one, axis=1, keepdims=True))
    ).astype(BF16)

    parts = pad_columns(jnp.stack([norm1_part, norm2_part], axis=1), LANES)
    tail = jnp.concatenate([dot(hidden_one, proj_grad, ((0,), (0,))), parts], axis=1)
    tail = sum_rows(tail, 640, 4, "sum_grad_proj")
    grad_proj = tail[:, :proj_cols]
    norm1_share = tail[:, proj_cols]
    norm2_share = tail[:, proj_cols + 1]
    return (
        layer_output,
        residual_mid,
        rms_values,
        input_grad,
        norm1_share,
        grad_proj[:, :query_cols],
        grad_proj[:, query_cols:],
        grad_out,
        norm2_share,
        grad_gate,
        bias_share[:ffn_own],
        grad_up,
        bias_share[ffn_pad : ffn_pad + ffn_own],
        grad_down,
        down_bias_share,
    )


def solution(mesh):
    by_rows, by_entry = P(AXIS, None), P(AXIS)
    in_specs = (
        by_rows,
        by_entry,
        by_rows,
        by_rows,
        by_rows,
        by_entry,
        by_rows,
        by_entry,
        by_rows,
        by_entry,
        by_rows,
        by_entry,
        by_rows,
    )
    out_specs = (
        by_rows,
        by_rows,
        P(None, AXIS),
        by_rows,
        by_entry,
        by_rows,
        by_rows,
        by_rows,
        by_entry,
        by_rows,
        by_entry,
        by_rows,
        by_entry,
        by_rows,
        by_entry,
    )
    return jax.shard_map(body, mesh=mesh, in_specs=in_specs, out_specs=out_specs, check_vma=False)
```

```python
import functools
import math

import jax
import jax.numpy as jnp
from jax import lax
from jax.experimental import pallas as pl
from jax.experimental.pallas import tpu as pltpu
from jax.sharding import PartitionSpec as P

HD = 256
WINDOW = 2048
EPSILON = 1e-06
NEGATIVE = -1e30
ROTARY_BASE = 10000.0
AXIS = "blk"
LANES = 128
DEVICES = 32
PAIR = 2
VMEM_BYTES = 48 * 1024 * 1024
F32 = jnp.float32
BF16 = jnp.bfloat16


def rotary_tables(positions, quarter):
    frequency = ROTARY_BASE ** (-(jnp.arange(quarter, dtype=F32) / quarter))
    angles = positions[:, None] * frequency[None, :]
    return (jnp.cos(angles), jnp.sin(angles))


def rotate(vector, cosine, sine_table, quarter):
    leading = vector[..., :quarter]
    trailing = vector[..., quarter : 2 * quarter]
    return jnp.concatenate(
        [
            leading * cosine - trailing * sine_table,
            trailing * cosine + leading * sine_table,
            vector[..., 2 * quarter :],
        ],
        axis=-1,
    )


def dot(left, right, contract):
    return lax.dot_general(left, right, (contract, ((), ())), preferred_element_type=F32)


def round_up(count, step):
    return (count + step - 1) // step * step


def pad_columns(values, columns):
    pad = [(0, 0)] * (values.ndim - 1) + [(0, columns - values.shape[-1])]
    return jnp.pad(values, pad)


def masked_scores(place_ref, query_rows, keys, tok_rows):
    scores = dot(query_rows, keys, ((1,), (1,)))
    rows = lax.broadcasted_iota(jnp.int32, scores.shape, 0) % tok_rows
    columns = lax.broadcasted_iota(jnp.int32, scores.shape, 1)
    distance = rows - columns + place_ref[0]
    return jnp.where((distance >= 0) & (distance < WINDOW), scores, NEGATIVE)


def stack_heads(block):
    return jnp.concatenate([block[:, i * HD : (i + 1) * HD] for i in range(PAIR)], axis=0)


def unstack_heads(rows):
    tok_rows = rows.shape[0] // PAIR
    return jnp.concatenate([rows[i * tok_rows : (i + 1) * tok_rows] for i in range(PAIR)], axis=1)


def attend_kernel(place_ref, query_ref, kv_ref, out_ref, log_ref):
    tok_rows = query_ref.shape[0]
    scores = masked_scores(place_ref, stack_heads(query_ref[...]), kv_ref[:, :HD], tok_rows)
    row_max = jnp.max(scores, axis=1, keepdims=True)
    probs = jnp.exp(scores - row_max)
    row_sum = jnp.sum(probs, axis=1, keepdims=True)
    probs_low = (probs * (1.0 / row_sum)).astype(BF16)
    attended = dot(probs_low, kv_ref[:, HD:], ((1,), (0,)))
    out_ref[...] = unstack_heads(attended).astype(BF16)
    log_ref[0] = jnp.broadcast_to(row_max + jnp.log(row_sum), log_ref.shape[1:])


def attend_back_kernel(place_ref, query_ref, kv_ref, log_ref, grad_ref, query_grad_ref, kv_grad_ref):
    tok_rows = query_ref.shape[0]
    query_rows = stack_heads(query_ref[...])
    grad_rows = stack_heads(grad_ref[...])
    keys, values = kv_ref[:, :HD], kv_ref[:, HD:]
    scores = masked_scores(place_ref, query_rows, keys, tok_rows)
    probs = jnp.exp(scores - log_ref[0][:, :1])
    prob_grad = dot(grad_rows, values, ((1,), (1,)))
    delta = jnp.sum(probs * prob_grad, axis=1, keepdims=True)
    score_grad = (probs * (prob_grad - delta)).astype(BF16)
    query_grad_ref[...] = unstack_heads(dot(score_grad, keys, ((1,), (0,))))
    key_part = dot(score_grad, query_rows, ((0,), (0,)))
    value_part = dot(probs.astype(BF16), grad_rows, ((0,), (0,)))

    @pl.when(pl.program_id(0) == 0)
    def _():
        kv_grad_ref[:, :HD] = key_part
        kv_grad_ref[:, HD:] = value_part

    @pl.when(pl.program_id(0) > 0)
    def _():
        kv_grad_ref[:, :HD] += key_part
        kv_grad_ref[:, HD:] += value_part


def attention_specs(tok_rows, heads, window_rows):
    place = pl.BlockSpec(memory_space=pltpu.SMEM)
    by_head = pl.BlockSpec((tok_rows, PAIR * HD), lambda i: (0, i))
    whole = pl.BlockSpec((window_rows, 2 * HD), lambda i: (0, 0))
    logs = pl.BlockSpec((1, PAIR * tok_rows, LANES), lambda i: (i, 0, 0))
    return place, by_head, whole, logs


def attend(place, queries, kv_window):
    tok_rows, features = queries.shape
    window_rows = kv_window.shape[0]
    pairs = features // HD // PAIR
    place_spec, by_head, whole, logs = attention_specs(tok_rows, features // HD, window_rows)
    work = tok_rows * features * window_rows
    return pl.pallas_call(
        attend_kernel,
        grid=(pairs,),
        out_shape=(
            jax.ShapeDtypeStruct((tok_rows, features), BF16),
            jax.ShapeDtypeStruct((pairs, PAIR * tok_rows, LANES), F32),
        ),
        in_specs=[place_spec, by_head, whole],
        out_specs=(by_head, logs),
        compiler_params=pltpu.CompilerParams(vmem_limit_bytes=VMEM_BYTES),
        cost_estimate=pl.CostEstimate(
            flops=4 * work, bytes_accessed=8 * kv_window.size, transcendentals=work // HD
        ),
        name="attend",
    )(place, queries, kv_window)


def attend_back(place, queries, kv_window, logs_in, grad):
    tok_rows, features = queries.shape
    window_rows = kv_window.shape[0]
    pairs = features // HD // PAIR
    place_spec, by_head, whole, logs = attention_specs(tok_rows, features // HD, window_rows)
    work = tok_rows * features * window_rows
    return pl.pallas_call(
        attend_back_kernel,
        grid=(pairs,),
        out_shape=(
            jax.ShapeDtypeStruct((tok_rows, features), F32),
            jax.ShapeDtypeStruct((window_rows, 2 * HD), F32),
        ),
        in_specs=[place_spec, by_head, whole, logs, by_head],
        out_specs=(by_head, whole),
        compiler_params=pltpu.CompilerParams(vmem_limit_bytes=VMEM_BYTES),
        cost_estimate=pl.CostEstimate(
            flops=10 * work, bytes_accessed=8 * kv_window.size, transcendentals=work // HD
        ),
        name="attend_back",
    )(place, queries, kv_window, logs_in, grad)


MESH=pl.DeviceIdType.MESH

class Place:
    def __init__(self):
        me = lax.axis_index(AXIS)
        self.core = me % 2
        self.x = (me // 2) % 2
        self.y = (me // 4) % 2
        self.z = me // 8
        self.sibling = self.index(self.z, self.y, self.x, 1 - self.core)
        self.next_x = self.index(self.z, self.y, 1 - self.x, self.core)
        self.next_y = self.index(self.z, 1 - self.y, self.x, self.core)
        self.plane = [self.z] + [(self.z + o) % 4 for o in (1, 2, 3)]
        self.line = [self.index(p, self.y, self.x, self.core) for p in self.plane]
    def index(self, z, y, x, core):
        return ((z * 2 + y) * 2 + x) * 2 + core
    def side(self, dy, dx):
        return (1 - self.y if dy else self.y), (1 - self.x if dx else self.x)
    def meet(self):
        barrier = pltpu.get_barrier_semaphore()
        partners = [self.sibling, self.next_x, self.next_y] + self.line[1:]
        for device in partners:
            pl.semaphore_signal(barrier, inc=1, device_id=(device,), device_id_type=MESH)
        pl.semaphore_wait(barrier, len(partners))

def send(src, dst, sems, device):
    copy = pltpu.make_async_remote_copy(src_ref=src, dst_ref=dst, send_sem=sems[0], recv_sem=sems[1], device_id=(device,), device_id_type=MESH)
    copy.start()
    return copy

TILE=16
def add_rows(total, other, first, count):
    planes = other.shape[0]
    steps = count // TILE
    @pl.loop(0, planes * steps)
    def _(i):
        plane, row = i // steps, (i % steps) * TILE
        here = (plane, pl.ds(pl.multiple_of(row + first, TILE), TILE), slice(None))
        there = (plane, pl.ds(pl.multiple_of(row, TILE), TILE), slice(None))
        total[here] = (total[here].astype(F32) + other[there].astype(F32)).astype(BF16)

def sum_kernel(chunk, in_ref, out_ref, acc, got_core, got_diag_x, got_diag_y, got_x, got_y, got_z,
               load_sem, core_sems, diag_sems, side_sems, line_sems):
    place = Place()
    rows, columns = out_ref.shape
    upper = got_diag_x.shape[1]
    lower = rows - upper
    chunks = columns // chunk
    corners = [(1, 1), (0, 1), (1, 0), (0, 0)]
    cols = [pl.ds(k * chunk, chunk) for k in range(chunks)]
    loads, cores, sends = {}, {}, []
    for k in range(chunks):
        for i, (dy, dx) in enumerate(corners):
            y, x = place.side(dy, dx)
            load = pltpu.make_async_copy(in_ref.at[:, y, x, place.core, :, cols[k]], acc.at[i, :, :, cols[k]], load_sem.at[k, i])
            load.start()
            loads[k, i] = load
    place.meet()
    for k in range(chunks):
        for i, (dy, dx) in enumerate(corners):
            y, x = place.side(dy, dx)
            cores[k, i] = send(in_ref.at[:, y, x, 1 - place.core, :, cols[k]], got_core.at[i, :, :, cols[k]],
                               (core_sems.at[0, k, i], core_sems.at[1, k, i]), place.sibling)
    top, bottom = pl.ds(0, upper), pl.ds(upper, lower)
    diag, side, line = {}, {}, {}
    def pair(sems, k, i): return (sems.at[0, k, i], sems.at[1, k, i])
    def stage0(k):
        for i in range(4):
            loads[k, i].wait(); cores[k, i].wait_recv()
            add_rows(acc.at[i, :, :, cols[k]], got_core.at[i, :, :, cols[k]], 0, rows)
            if i == 0:
                diag[k, 0] = send(acc.at[0, :, top, cols[k]], got_diag_x.at[:, :, cols[k]], pair(diag_sems, k, 0), place.next_x)
                diag[k, 1] = send(acc.at[0, :, bottom, cols[k]], got_diag_y.at[:, :, cols[k]], pair(diag_sems, k, 1), place.next_y)
            if i == 1:
                side[k, 0] = send(acc.at[1, :, top, cols[k]], got_x.at[:, top, cols[k]], pair(side_sems, k, 0), place.next_x)
            if i == 2:
                side[k, 1] = send(acc.at[2, :, bottom, cols[k]], got_y.at[:, bottom, cols[k]], pair(side_sems, k, 1), place.next_y)
    def stage1(k):
        diag[k, 0].wait_recv()
        add_rows(acc.at[2, :, :, cols[k]], got_diag_x.at[:, :, cols[k]], 0, upper)
        side[k, 2] = send(acc.at[2, :, top, cols[k]], got_y.at[:, top, cols[k]], pair(side_sems, k, 2), place.next_y)
        diag[k, 1].wait_recv()
        add_rows(acc.at[1, :, :, cols[k]], got_diag_y.at[:, :, cols[k]], upper, lower)
        side[k, 3] = send(acc.at[1, :, bottom, cols[k]], got_x.at[:, bottom, cols[k]], pair(side_sems, k, 3), place.next_x)
    def stage2(k):
        for i in range(4): side[k, i].wait_recv()
        steps = rows // TILE
        @pl.loop(0, 4 * steps)
        def _(i):
            plane, row = i // steps, (i % steps) * TILE
            here = (plane, pl.ds(pl.multiple_of(row, TILE), TILE), cols[k])
            acc[(3,) + here] = (acc[(3,) + here].astype(F32) + got_x[here].astype(F32) + got_y[here].astype(F32)).astype(BF16)
        for o in (1, 2, 3):
            line[k, o] = send(acc.at[3, place.plane[o], :, cols[k]], got_z.at[o - 1, :, cols[k]], pair(line_sems, k, o - 1), place.line[o])
    def stage3(k):
        for o in (1, 2, 3): line[k, o].wait_recv()
        @pl.loop(0, rows // TILE)
        def _(i):
            here = (pl.ds(pl.multiple_of(i * TILE, TILE), TILE), cols[k])
            total = acc[(3, place.z) + here].astype(F32)
            for o in range(3): total += got_z[(o,) + here].astype(F32)
            out_ref[here] = total
    stages = [stage0, stage1, stage2, stage3]
    for step in range(chunks + 3):
        for s in range(3, -1, -1):
            if 0 <= step - s < chunks: stages[s](step - s)
    for group in (cores, diag, side, line):
        for copy in group.values(): copy.wait_send()

def sum_over_devices(partial, chunk, collective_id, name):
    rows, columns = partial.shape[0] // 32, partial.shape[1]
    chunks = columns // chunk
    upper = (rows // 2 + TILE - 1) // TILE * TILE
    def buf(*shape): return pltpu.VMEM(shape, BF16)
    def sems(count): return pltpu.SemaphoreType.DMA((2, chunks, count))
    return pl.pallas_call(
        functools.partial(sum_kernel, chunk),
        out_shape=jax.ShapeDtypeStruct((rows, columns), F32),
        in_specs=[pl.BlockSpec(memory_space=pl.ANY)],
        out_specs=pl.BlockSpec(memory_space=pltpu.VMEM),
        scratch_shapes=[buf(4, 4, rows, columns), buf(4, 4, rows, columns), buf(4, upper, columns), buf(4, rows - upper, columns),
            buf(4, rows, columns), buf(4, rows, columns), buf(3, rows, columns),
            pltpu.SemaphoreType.DMA((chunks, 4)), sems(4), sems(2), sems(4), sems(3)],
        compiler_params=pltpu.CompilerParams(collective_id=collective_id, has_side_effects=True, vmem_limit_bytes=56*1024*1024),
        name=name,
    )(partial.reshape(4, 2, 2, 2, rows, columns))


CORNERS = ((1, 1), (0, 1), (1, 0), (0, 0))

def add_tiles(count, rows, target, parts):
    steps = rows // TILE
    @pl.loop(0, count * steps)
    def _(i):
        index, here = i // steps, pl.ds(pl.multiple_of((i % steps) * TILE, TILE), TILE)
        total = None
        for ref, first in parts:
            at = here if first == 0 else pl.ds(pl.multiple_of((i % steps) * TILE + first, TILE), TILE)
            part = ref[index, at].astype(F32)
            total = part if total is None else total + part
        ref, first = target
        at = here if first == 0 else pl.ds(pl.multiple_of((i % steps) * TILE + first, TILE), TILE)
        ref[index, at] = total.astype(BF16)

class SumBuffers:
    def __init__(self, refs):
        self.acc, self.core, self.diag_x, self.diag_y, self.x, self.y, self.z, self.sems = refs
    @staticmethod
    def shapes(rows, columns, units):
        upper = (rows // 2 + TILE - 1) // TILE * TILE
        buf = lambda *shape: pltpu.VMEM(shape + (columns,), BF16)
        return [buf(4, 4, rows), buf(4, 4, rows), buf(4, upper), buf(4, rows - upper), buf(4, rows), buf(4, rows), buf(3, rows),
                pltpu.SemaphoreType.DMA((units, 2, Sum.COPIES))]
    COUNT = 8

class Sum:
    COPIES = 14
    def __init__(self, place, bufs, unit, cols, own, other, out):
        self.p, self.b, self.unit, self.own, self.other, self.out = place, bufs, unit, own, other, out
        self.rows = bufs.acc.shape[2]
        self.upper = bufs.diag_x.shape[1]
        self.lower = self.rows - self.upper
        self.acc = bufs.acc.at[:, :, :, cols]
        self.core = bufs.core.at[:, :, :, cols]
        self.diag_x, self.diag_y = bufs.diag_x.at[:, :, cols], bufs.diag_y.at[:, :, cols]
        self.x, self.y, self.z = bufs.x.at[:, :, cols], bufs.y.at[:, :, cols], bufs.z.at[:, :, cols]
        self.copies = {}
    def push(self, slot, src, dst, device):
        sems = self.b.sems
        self.copies[slot] = send(src, dst, (sems.at[self.unit, 0, slot], sems.at[self.unit, 1, slot]), device)
    def begin(self):
        for i in range(4):
            self.push(i, self.other(i), self.core.at[i], self.p.sibling)
    def stage0(self):
        top, bottom = pl.ds(0, self.upper), pl.ds(self.upper, self.lower)
        for i in range(4):
            self.copies[i].wait_recv()
            add_tiles(4, self.rows, (self.acc.at[i], 0), [(self.own(i), 0), (self.core.at[i], 0)])
            if i == 0:
                self.push(4, self.acc.at[0, :, top], self.diag_x, self.p.next_x)
                self.push(5, self.acc.at[0, :, bottom], self.diag_y, self.p.next_y)
            if i == 1:
                self.push(6, self.acc.at[1, :, top], self.x.at[:, top], self.p.next_x)
            if i == 2:
                self.push(7, self.acc.at[2, :, bottom], self.y.at[:, bottom], self.p.next_y)
    def stage1(self):
        top, bottom = pl.ds(0, self.upper), pl.ds(self.upper, self.lower)
        self.copies[4].wait_recv()
        add_tiles(4, self.upper, (self.acc.at[2], 0), [(self.acc.at[2], 0), (self.diag_x, 0)])
        self.push(8, self.acc.at[2, :, top], self.y.at[:, top], self.p.next_y)
        self.copies[5].wait_recv()
        add_tiles(4, self.lower, (self.acc.at[1], self.upper), [(self.acc.at[1], self.upper), (self.diag_y, 0)])
        self.push(9, self.acc.at[1, :, bottom], self.x.at[:, bottom], self.p.next_x)
    def stage2(self):
        for slot in (6, 7, 8, 9):
            self.copies[slot].wait_recv()
        add_tiles(4, self.rows, (self.acc.at[3], 0), [(self.acc.at[3], 0), (self.x, 0), (self.y, 0)])
        for o in (1, 2, 3):
            self.push(9 + o, self.acc.at[3, self.p.plane[o]], self.z.at[o - 1], self.p.line[o])
    def stage3(self):
        for o in (1, 2, 3):
            self.copies[9 + o].wait_recv()
        @pl.loop(0, self.rows // TILE)
        def _(i):
            here = pl.ds(pl.multiple_of(i * TILE, TILE), TILE)
            total = self.acc[3, self.p.z, here].astype(F32)
            for o in range(3):
                total += self.z[o, here].astype(F32)
            self.out[here] = total
    def core_sent(self):
        for i in range(4): self.copies[i].wait_send()
    def finish(self):
        for slot in range(4, 13): self.copies[slot].wait_send()

def product_sums_kernel(chunk, left_a, right_a, left_b, right_b, extra, out_a, out_b, part, *scratch):
    place = Place()
    bufs = SumBuffers(scratch)
    rows = out_a.shape[0]
    wide = 8 * rows
    units = []
    def add_unit(left, right, out, first, span, more):
        k = len(units)
        slot = k % 2
        def own(i):
            y, x = place.side(*CORNERS[i])
            return part.at[slot, :, y, x, place.core]
        def other(i):
            y, x = place.side(*CORNERS[i])
            return part.at[slot, :, y, x, 1 - place.core]
        cols = pl.ds(k * chunk, chunk)
        unit = Sum(place, bufs, k, cols, own, other, out.at[:, pl.ds(first, chunk)])
        def make():
            if k >= 2: units[k - 2][0].core_sent()
            @pl.loop(0, 4)
            def _(z):
                here = pl.ds(pl.multiple_of(z * wide, wide), wide)
                product = lax.dot_general(left[:, here], right[:, pl.ds(first, span)], (((0,), (0,)), ((), ())), preferred_element_type=F32)
                part[slot, z, :, :, :, :, pl.ds(0, span)] = product.astype(BF16).reshape(2, 2, 2, rows, span)
                if more is not None:
                    part[slot, z, :, :, :, :, pl.ds(span, chunk - span)] = more[here].reshape(2, 2, 2, rows, chunk - span)
            unit.begin()
        units.append((unit, make))
    for first in range(0, out_a.shape[1], chunk):
        add_unit(left_a, right_a, out_a, first, chunk, None)
    for first in range(0, out_b.shape[1], chunk):
        span = min(chunk, right_b.shape[1] - first)
        add_unit(left_b, right_b, out_b, first, span, None if span == chunk else extra)
    place.meet()
    count = len(units)
    stages = [lambda k: units[k][1](), lambda k: units[k][0].stage0(), lambda k: units[k][0].stage1(), lambda k: units[k][0].stage2(), lambda k: units[k][0].stage3()]
    for step in range(count + 4):
        for s in (1, 2, 3, 4, 0):
            if 0 <= step - s < count: stages[s](step - s)
    for unit, _ in units[-2:]: unit.core_sent()
    for unit, _ in units: unit.finish()

def product_sums(left_a, right_a, left_b, right_b, extra, chunk, collective_id, name):
    rows = left_a.shape[1] // 32
    columns_a, columns_b = right_a.shape[1], right_b.shape[1] + extra.shape[1]
    total = columns_a + columns_b
    vmem = pl.BlockSpec(memory_space=pltpu.VMEM)
    return pl.pallas_call(
        functools.partial(product_sums_kernel, chunk),
        out_shape=(jax.ShapeDtypeStruct((rows, columns_a), F32), jax.ShapeDtypeStruct((rows, columns_b), F32)),
        in_specs=[vmem] * 5,
        out_specs=(vmem, vmem),
        scratch_shapes=[pltpu.VMEM((2, 4, 2, 2, 2, rows, chunk), BF16)] + SumBuffers.shapes(rows, total, total // chunk),
        compiler_params=pltpu.CompilerParams(collective_id=collective_id, has_side_effects=True, vmem_limit_bytes=62*1024*1024),
        name=name,
    )(left_a, right_a, left_b, right_b, extra)


PLANES=4
def plane_order(z):
    near = jnp.minimum(z, 3 - z)
    flip = z // 2
    order = []
    for k in range(4):
        swapped = 1 - k if k < 2 else k
        plane = near * swapped + (1 - near) * k
        order.append(flip * (3 - plane) + (1 - flip) * plane)
    return order

class Gather:
    COPIES = 11
    def __init__(self, place, own, held, cols, sems):
        self.place, self.held, self.cols, self.sems = place, held, cols, sems
        self.own = own.at[:, cols]
        rows = held.shape[4]
        upper = (rows // 2 + TILE - 1) // TILE * TILE
        self.halves = pl.ds(0, upper), pl.ds(upper, rows - upper)
        self.order = plane_order(place.z)
        self.sent = []
        self.kept = []
    def at(self, plane, y, x, core, part=slice(None)):
        return self.held.at[plane, y, x, core, part, self.cols]
    def pair(self, slot, k):
        return self.sems.at[0, slot, k], self.sems.at[1, slot, k]
    def push(self, src, dst, slot, k, device):
        copy = send(src, dst, self.pair(slot, k), device)
        self.sent.append(copy)
    def arrived(self, ref, slot, k):
        pltpu.make_async_remote_copy(src_ref=ref, dst_ref=ref, send_sem=self.sems.at[0, slot, k], recv_sem=self.sems.at[1, slot, k], device_id=(self.place.sibling,), device_id_type=MESH).wait_recv()
    def start(self):
        p = self.place
        mine = self.at(p.z, p.y, p.x, p.core)
        keep = pltpu.make_async_copy(self.own, mine, self.sems.at[0, 10, 0])
        keep.start()
        self.kept.append(keep)
        for k in (1, 2, 3):
            plane = self.order[k]
            copy = pltpu.make_async_remote_copy(src_ref=self.own, dst_ref=mine, send_sem=self.sems.at[0, 0, k], recv_sem=self.sems.at[1, 0, p.z], device_id=(p.index(plane, p.y, p.x, p.core),), device_id_type=MESH)
            copy.start(); self.sent.append(copy)
    def line(self, k):
        p = self.place
        plane = self.order[k]
        block = self.at(plane, p.y, p.x, p.core)
        source = self.own if k == 0 else block
        if k > 0:
            pltpu.make_async_remote_copy(src_ref=block, dst_ref=block, send_sem=self.sems.at[0, 0, k], recv_sem=self.sems.at[1, 0, plane], device_id=(p.sibling,), device_id_type=MESH).wait_recv()
        self.push(source, block, 1, k, p.next_x)
        self.push(source, block, 2, k, p.next_y)
        self.push(source, block, 5, k, p.sibling)
    def side(self, k):
        p, plane = self.place, self.order[k]
        top, bottom = self.halves
        self.arrived(self.at(plane, p.y, 1 - p.x, p.core), 1, k)
        block = self.at(plane, p.y, 1 - p.x, p.core, top)
        self.push(block, block, 4, k, p.next_y)
        block = self.at(plane, p.y, 1 - p.x, p.core)
        self.push(block, block, 6, k, p.sibling)
        self.arrived(self.at(plane, 1 - p.y, p.x, p.core), 2, k)
        block = self.at(plane, 1 - p.y, p.x, p.core, bottom)
        self.push(block, block, 3, k, p.next_x)
        block = self.at(plane, 1 - p.y, p.x, p.core)
        self.push(block, block, 7, k, p.sibling)
    def diag(self, k):
        p, plane = self.place, self.order[k]
        for slot, part in ((4, self.halves[0]), (3, self.halves[1])):
            block = self.at(plane, 1 - p.y, 1 - p.x, p.core, part)
            self.arrived(block, slot, k)
            self.push(block, block, slot + 5, k, p.sibling)
    def ready(self, k):
        p, plane = self.place, self.order[k]
        top, bottom = self.halves
        if k == 0:
            for keep in self.kept: keep.wait()
        other = 1 - p.core
        self.arrived(self.at(plane, p.y, p.x, other), 5, k)
        self.arrived(self.at(plane, p.y, 1 - p.x, other), 6, k)
        self.arrived(self.at(plane, 1 - p.y, p.x, other), 7, k)
        self.arrived(self.at(plane, 1 - p.y, 1 - p.x, other, top), 9, k)
        self.arrived(self.at(plane, 1 - p.y, 1 - p.x, other, bottom), 8, k)
    def finish(self):
        for copy in self.sent: copy.wait_send()

def pipeline(stages, count):
    for step in range(count + len(stages) - 1):
        for s in range(len(stages) - 1, -1, -1):
            if 0 <= step - s < count:
                stages[s](step - s)

def gather_kernel(chunks, *refs):
    n = len(chunks)
    ins, outs, sems = refs[:n], refs[n:2*n], refs[2*n:]
    place = Place()
    place.meet()
    items = []
    for a in range(n):
        width = ins[a].shape[1] // chunks[a]
        for j in range(chunks[a]):
            items.append(Gather(place, ins[a], outs[a], pl.ds(j * width, width), sems[a].at[j]))
    def line(s):
        if s % PLANES == 0:
            items[s // PLANES].start()
        items[s // PLANES].line(s % PLANES)
    def side(s): items[s // PLANES].side(s % PLANES)
    def diag(s): items[s // PLANES].diag(s % PLANES)
    pipeline([line, side, diag], len(items) * PLANES)
    for item in items:
        for k in range(PLANES): item.ready(k)
    for item in items: item.finish()

def gather_all(arrays, chunks, collective_id, name):
    outs = pl.pallas_call(
        functools.partial(gather_kernel, chunks),
        out_shape=tuple(jax.ShapeDtypeStruct((4,2,2,2)+a.shape, BF16) for a in arrays),
        in_specs=[pl.BlockSpec(memory_space=pl.ANY)]*len(arrays),
        out_specs=tuple(pl.BlockSpec(memory_space=pl.ANY) for _ in arrays),
        scratch_shapes=[pltpu.SemaphoreType.DMA((c, 2, Gather.COPIES, PLANES)) for c in chunks],
        compiler_params=pltpu.CompilerParams(collective_id=collective_id, has_side_effects=True),
        name=name,
    )(*arrays)
    return [o.reshape(32 * a.shape[0], a.shape[1]) for o, a in zip(outs, arrays)]


GELU_SCALE = math.sqrt(2.0 / math.pi)
GELU_CUBE = 0.044715

def gelu_and_slope(v):
    square = v * v
    t = jnp.tanh(GELU_SCALE * v * (1.0 + GELU_CUBE * square))
    half = 0.5 * (1.0 + t)
    slope = half + 0.5 * v * (1.0 - t * t) * (GELU_SCALE * (1.0 + 3.0 * GELU_CUBE * square))
    return v * half, slope

class PlaneSum:
    SLOTS = 10
    def __init__(self, place, order, kind, k, acc, outgoing, out, land, load, sems, line_sems, load_sems):
        self.p, self.k, self.order = place, k, order
        self.acc, self.outgoing = acc.at[kind, k], outgoing.at[kind]
        self.out = out
        core, diag_x, diag_y, side_x, side_y, line = land
        self.core, self.side_x, self.side_y = core.at[kind, k], side_x.at[kind, k], side_y.at[kind, k]
        self.diag_x, self.diag_y, self.land = diag_x.at[kind, k], diag_y.at[kind, k], line.at[kind]
        self.load, self.load_sems = load, load_sems
        self.sems, self.line_sems = sems.at[kind, k], line_sems.at[kind]
        self.rows = self.acc.shape[1]
        self.upper = self.diag_x.shape[0]
        self.top, self.bottom = pl.ds(0, self.upper), pl.ds(self.upper, self.rows - self.upper)
    def mine(self, i): return self.acc.at[i]
    def copy(self, src, dst, slot, device):
        return pltpu.make_async_remote_copy(src_ref=src, dst_ref=dst, send_sem=self.sems.at[0, slot], recv_sem=self.sems.at[1, slot], device_id=(device,), device_id_type=MESH)
    def across(self, i):
        return self.copy(self.outgoing.at[i % 2], self.core.at[i], i, self.p.sibling)
    def make(self, slot):
        p, mine = self.p, self.mine
        src, dst, device = {
            4: (mine(0).at[self.top], self.diag_x, p.next_x),
            5: (mine(0).at[self.bottom], self.diag_y, p.next_y),
            6: (mine(1).at[self.top], self.side_x.at[self.top], p.next_x),
            7: (mine(2).at[self.bottom], self.side_y.at[self.bottom], p.next_y),
            8: (mine(2).at[self.top], self.side_y.at[self.top], p.next_y),
            9: (mine(1).at[self.bottom], self.side_x.at[self.bottom], p.next_x),
        }[slot]
        return self.copy(src, dst, slot, device)
    def line_copy(self):
        p, plane = self.p, self.order[self.k]
        return pltpu.make_async_remote_copy(src_ref=self.mine(3), dst_ref=self.land.at[p.z], send_sem=self.line_sems.at[0, self.k], recv_sem=self.line_sems.at[1, p.z], device_id=(p.index(plane, p.y, p.x, p.core),), device_id_type=MESH)
    def fetch(self, src, slot):
        rows = src.shape[0]
        copy = pltpu.make_async_copy(src, self.load.at[slot, pl.ds(0, rows)], self.load_sems.at[slot])
        copy.start()
        return copy
    def add(self, target, slots, rows):
        @pl.loop(0, rows // TILE)
        def _(i):
            here = pl.ds(pl.multiple_of(i * TILE, TILE), TILE)
            total = target[here].astype(F32)
            for slot in slots: total += self.load[slot, here].astype(F32)
            target[here] = total.astype(target.dtype)
    def stage0(self):
        self.across(0).wait_recv()
        fetched = self.fetch(self.core.at[0], 0)
        for i in range(4):
            current = fetched
            if i < 3:
                self.across(i + 1).wait_recv()
                fetched = self.fetch(self.core.at[i + 1], (i + 1) % 2)
            current.wait()
            self.add(self.mine(i), [i % 2], self.rows)
            for slot in ((4, 5), (6,), (7,), ())[i]:
                self.make(slot).start()
    def stage1(self):
        self.make(4).wait_recv()
        self.fetch(self.diag_x, 0).wait()
        self.add(self.mine(2).at[self.top], [0], self.upper)
        self.make(8).start()
        self.make(5).wait_recv()
        self.fetch(self.diag_y, 1).wait()
        self.add(self.mine(1).at[self.bottom], [1], self.rows - self.upper)
        self.make(9).start()
    def stage2(self):
        for slot in (6, 9): self.make(slot).wait_recv()
        first = self.fetch(self.side_x, 0)
        for slot in (7, 8): self.make(slot).wait_recv()
        second = self.fetch(self.side_y, 1)
        first.wait(); second.wait()
        if self.k > 0:
            self.add(self.mine(3), [0, 1], self.rows)
            self.line_copy().start()
        else:
            mine, out = self.mine(3), self.out
            @pl.loop(0, self.rows // TILE)
            def _(i):
                here = pl.ds(pl.multiple_of(i * TILE, TILE), TILE)
                out[here] = mine[here].astype(F32) + self.load[0, here].astype(F32) + self.load[1, here].astype(F32)
    def sent(self):
        for slot in range(4, 10): self.make(slot).wait_send()
        if self.k > 0: self.line_copy().wait_send()
    def last(self):
        p, plane = self.p, self.order[self.k]
        land = self.land.at[plane]
        pltpu.make_async_remote_copy(src_ref=land, dst_ref=land, send_sem=self.line_sems.at[0, self.k], recv_sem=self.line_sems.at[1, plane], device_id=(p.sibling,), device_id_type=MESH).wait_recv()
        self.fetch(land, self.k % 2).wait()
        self.add(self.out, [self.k % 2], self.rows)

def ffn_kernel(hidden_ref, cotangent_ref, both_ref, down_ref, bias_ref,
               hidden_sum, ffn_sum, grad_both_ref, grad_down_ref, bias_grad_ref,
               held, land_core, land_dx, land_dy, land_x, land_y, land_z,
               tokens, cot, both_keep, ffn_keep, acc, outgoing, load, gather_sems, cot_sems, sum_sems, line_sems, load_sems):
    place = Place()
    width = hidden_ref.shape[1]
    pad = down_ref.shape[0]
    rows = 2 * hidden_ref.shape[0]
    order = plane_order(place.z)
    def fetch_cot(k): return pltpu.make_async_copy(cotangent_ref.at[order[k]], cot, cot_sems.at[0, k])
    def fetch_tokens(k): return pltpu.make_async_copy(held.at[order[k]], tokens, cot_sems.at[1, k])
    fetch_cot(0).start()
    place.meet()
    gather = Gather(place, hidden_ref, held, pl.ds(0, width), gather_sems)
    gather.start()
    grad_both_ref[...] = jnp.zeros_like(grad_both_ref)
    grad_down_ref[...] = jnp.zeros_like(grad_down_ref)
    bias_grad_ref[...] = jnp.zeros_like(bias_grad_ref)
    land = (land_core, land_dx, land_dy, land_x, land_y, land_z)
    sums = [[PlaneSum(place, order, kind, k, acc, outgoing, (hidden_sum, ffn_sum)[kind], land, load, sum_sems, line_sems, load_sems) for k in range(PLANES)] for kind in range(2)]

    def compute(k):
        gather.ready(k)
        fetch_tokens(k).start()
        fetch_tokens(k).wait()
        fetch_cot(k).wait()
        half = rows // 2
        @pl.loop(0, 4)
        def _(i):
            dy, dx = 1 - i % 2, 1 - i // 2
            y, x = place.y + dy * (1 - 2 * place.y), place.x + dx * (1 - 2 * place.x)
            hidden = tokens[y, x].reshape(rows, width)
            cotangent = cot[y, x].reshape(rows, width)
            both_pre = dot(hidden, both_ref[...], ((1,), (0,))) + bias_ref[0:1]
            hidden_grad = dot(cotangent, down_ref[...], ((1,), (1,)))
            activated, slope = gelu_and_slope(both_pre[:, :pad])
            up_pre = both_pre[:, pad:]
            hidden_ffn = (activated * up_pre).astype(BF16)
            both_grad = jnp.concatenate([(hidden_grad * up_pre * slope).astype(BF16), (hidden_grad * activated).astype(BF16)], axis=1)
            here = pl.ds(pl.multiple_of((y * 2 + x) * rows, rows), rows)
            both_keep[here] = both_grad
            ffn_keep[here] = hidden_ffn
            bias_grad_ref[...] += jnp.sum(both_grad.astype(F32), axis=0, keepdims=True)
            def drain():
                for kind in range(2): sums[kind][k].across(i - 2).wait_send()
            def drain_before():
                for kind in range(2): sums[kind][k - 1].across(i + 2).wait_send()
            pl.when(i >= 2)(drain)
            if k > 0: pl.when(i < 2)(drain_before)
            for kind, part in ((0, lambda: dot(both_grad, both_ref[...], ((1,), (1,)))), (1, lambda: dot(hidden_ffn, down_ref[...], ((1,), (0,))))):
                result = part().astype(BF16)
                low, high = result[:half], result[half:]
                acc[kind, k, i] = jnp.where(place.core == 0, low, high)
                outgoing[kind, i % 2] = jnp.where(place.core == 0, high, low)
                sums[kind][k].across(i).start()
        step = 512
        @pl.loop(0, width // step)
        def _(j):
            cols = pl.ds(pl.multiple_of(j * step, step), step)
            hidden = tokens[:, :, :, :, cols].reshape(4 * rows, step)
            grad_both_ref[:, cols] += dot(both_keep[...], hidden, ((0,), (0,)))
            cotangent = cot[:, :, :, :, cols].reshape(4 * rows, step)
            grad_down_ref[:, cols] += dot(ffn_keep[...], cotangent, ((0,), (0,)))
        if k + 1 < PLANES: fetch_cot(k + 1).start()

    def both(name, k):
        for kind in range(2): getattr(sums[kind][k], name)()

    gather.line(0)
    gather.line(1)
    gather.side(0)
    gather.line(2)
    gather.side(1)
    gather.diag(0)
    compute(0)
    gather.line(3)
    gather.side(2)
    gather.diag(1)
    gather.side(3)
    compute(1)
    gather.diag(2)
    gather.diag(3)
    both("stage0", 1)
    compute(2)
    both("stage1", 1)
    both("stage0", 2)
    compute(3)
    both("stage2", 1)
    both("stage1", 2)
    both("stage0", 3)
    both("stage2", 2)
    both("stage1", 3)
    both("stage0", 0)
    both("stage2", 3)
    both("stage1", 0)
    both("stage2", 0)
    for kind in range(2):
        for i in (2, 3): sums[kind][3].across(i).wait_send()
    for kind in range(2):
        for k in (1, 2, 3): sums[kind][k].last()
    for k in range(PLANES): both("sent", k)
    gather.finish()

def ffn(hidden_two, cotangent_full, both_own, both_bias, down_own, collective_id):
    tok_rows, width = hidden_two.shape
    pad = down_own.shape[0]
    full = (4, 2, 2, 2, tok_rows, width)
    upper = (tok_rows // 2 + TILE - 1) // TILE * TILE
    hbm = pl.BlockSpec(memory_space=pl.ANY)
    vmem = pl.BlockSpec(memory_space=pltpu.VMEM)
    dma = pltpu.SemaphoreType.DMA
    low = lambda *shape: jax.ShapeDtypeStruct(shape + (width,), BF16)
    outs = pl.pallas_call(
        ffn_kernel,
        out_shape=(
            jax.ShapeDtypeStruct((tok_rows, width), F32),
            jax.ShapeDtypeStruct((tok_rows, width), F32),
            jax.ShapeDtypeStruct((2 * pad, width), F32),
            jax.ShapeDtypeStruct((pad, width), F32),
            jax.ShapeDtypeStruct((8, 2 * pad), F32),
            low(4, 2, 2, 2, tok_rows),
            low(2, 4, 4, tok_rows), low(2, 4, upper), low(2, 4, tok_rows - upper),
            low(2, 4, tok_rows), low(2, 4, tok_rows), low(2, 4, tok_rows),
        ),
        in_specs=[hbm, hbm, vmem, vmem, vmem],
        out_specs=(vmem,) * 5 + (hbm,) * 7,
        scratch_shapes=[
            pltpu.VMEM(full[1:], BF16),
            pltpu.VMEM(full[1:], BF16),
            pltpu.VMEM((8 * tok_rows, 2 * pad), BF16),
            pltpu.VMEM((8 * tok_rows, pad), BF16),
            pltpu.VMEM((2, 4, 4, tok_rows, width), BF16),
            pltpu.VMEM((2, 2, tok_rows, width), BF16),
            pltpu.VMEM((2, tok_rows, width), BF16),
            dma((2, Gather.COPIES, PLANES)), dma((2, PLANES)), dma((2, PLANES, 2, PlaneSum.SLOTS)), dma((2, 2, PLANES)), dma((2,)),
        ],
        compiler_params=pltpu.CompilerParams(collective_id=collective_id, has_side_effects=True, vmem_limit_bytes=63*1024*1024),
        name="feed_forward",
    )(hidden_two, cotangent_full.reshape(full), both_own, down_own, jnp.broadcast_to(both_bias, (8, 2 * pad)))
    return outs[0], outs[1], outs[2], outs[3], outs[4][0]


def gather_rows(arrays, collective_id, name):
    if lax.axis_size(AXIS) == DEVICES:
        return gather_all(arrays, [1] * len(arrays), collective_id, name)
    return [lax.all_gather(values, AXIS, axis=0, tiled=True) for values in arrays]


def sum_rows(partial, chunk, collective_id, name):
    if lax.axis_size(AXIS) == DEVICES:
        return sum_over_devices(partial.astype(BF16), chunk, collective_id, name)
    return lax.psum_scatter(
        partial.astype(BF16), AXIS, scatter_dimension=0, tiled=True
    ).astype(F32)


def sum_products(left_a, right_a, left_b, right_b, extra):
    if lax.axis_size(AXIS) == DEVICES:
        return product_sums(left_a, right_a, left_b, right_b, extra, 640, 2, "sum_products")
    product_a = dot(left_a, right_a, ((0,), (0,)))
    product_b = dot(left_b, right_b, ((0,), (0,))).astype(BF16)
    return (
        sum_rows(product_a, None, None, None),
        sum_rows(jnp.concatenate([product_b, extra], axis=1), None, None, None),
    )


def swap(pieces):
    return lax.all_to_all(pieces, AXIS, 0, 0, tiled=False)


def feed_forward(hidden_two, cotangent_full, both_own, both_bias, down_own, rows):
    peers = lax.axis_size(AXIS)
    device = lax.axis_index(AXIS)
    tok_rows, width = hidden_two.shape
    ffn_pad = down_own.shape[0]
    own_cotangent = lax.dynamic_slice_in_dim(cotangent_full, device * rows, rows, 1)
    down_bias_share = jnp.sum(own_cotangent.astype(F32), axis=0)
    if peers == DEVICES:
        normed_grad, ffn_out, grad_both, grad_down, bias_share = ffn(
            hidden_two, cotangent_full, both_own, both_bias, down_own, 7
        )
        return normed_grad, ffn_out, grad_both.T, grad_down, bias_share, down_bias_share

    def piece(sums, here):
        hidden_own, cotangent_piece = here
        hidden_full = gather_rows([hidden_own], None, None)[0]
        both_pre = jnp.dot(hidden_full, both_own, preferred_element_type=F32) + both_bias
        activated, slope = gelu_and_slope(both_pre[:, :ffn_pad])
        up_pre = both_pre[:, ffn_pad:]
        hidden_ffn = (activated * up_pre).astype(BF16)
        hidden_grad = dot(cotangent_piece, down_own, ((1,), (1,)))
        gate_grad = (hidden_grad * up_pre * slope).astype(BF16)
        up_grad = (hidden_grad * activated).astype(BF16)
        both_grad = jnp.concatenate([gate_grad, up_grad], axis=1)
        normed_grad = sum_rows(dot(both_grad, both_own, ((1,), (1,))), None, None, None)
        ffn_out = sum_rows(
            jnp.dot(hidden_ffn, down_own, preferred_element_type=F32), None, None, None
        )
        shares = (
            dot(hidden_full, both_grad, ((0,), (0,))),
            dot(hidden_ffn, cotangent_piece, ((0,), (0,))),
            jnp.sum(both_grad.astype(F32), axis=0),
        )
        return jax.tree.map(jnp.add, sums, shares), (normed_grad, ffn_out)

    pieces = max(1, peers // DEVICES)
    cut = tok_rows // pieces
    zeros = (
        jnp.zeros((width, 2 * ffn_pad), F32),
        jnp.zeros((ffn_pad, width), F32),
        jnp.zeros((2 * ffn_pad,), F32),
    )
    cotangent_pieces = cotangent_full.reshape(peers, pieces, cut, width).transpose(1, 0, 2, 3)
    shares, outs = lax.scan(
        piece,
        zeros,
        (hidden_two.reshape(pieces, cut, width), cotangent_pieces.reshape(pieces, -1, width)),
    )
    normed_grad, ffn_out = (part.reshape(tok_rows, width) for part in outs)
    return (normed_grad, ffn_out) + shares + (down_bias_share,)


def body(
    layer_input,
    norm1_scale,
    query_weight,
    keyvalue_weight,
    out_weight,
    norm2_scale,
    gate_weight,
    gate_bias,
    up_weight,
    up_bias,
    down_weight,
    down_bias,
    out_cotangent,
):
    peers = lax.axis_size(AXIS)
    device = lax.axis_index(AXIS)
    tok_rows, width = layer_input.shape
    rows = query_weight.shape[0]
    query_cols = query_weight.shape[1]
    kv_cols = keyvalue_weight.shape[1]
    heads = query_cols // HD
    quarter = HD // 4
    query_scale = 1.0 / math.sqrt(HD)
    ffn_own = down_weight.shape[0]
    ffn_pad = round_up(ffn_own, LANES)

    vectors = jnp.stack([norm1_scale, norm2_scale, down_bias], axis=1)
    packed = jnp.concatenate(
        [query_weight, keyvalue_weight, pad_columns(vectors, LANES)], axis=1
    )
    first, out_full, cotangent_full = gather_rows(
        [packed, out_weight, out_cotangent], 5, "gather_weights"
    )
    proj_cols = query_cols + kv_cols
    proj_full = first[:, :proj_cols]
    gains = first[:, proj_cols:].astype(F32).T
    gain_one, gain_two, bias_down = gains[0], gains[1], gains[2]

    resid_in = layer_input.astype(F32)
    square_one = jnp.mean(resid_in * resid_in, axis=1, keepdims=True)
    scale_one = lax.rsqrt(square_one + EPSILON)
    normed_one = resid_in * scale_one
    hidden_one = (normed_one * gain_one).astype(BF16)
    projected = jnp.dot(hidden_one, proj_full, preferred_element_type=F32)
    position = device * tok_rows + jnp.arange(tok_rows, dtype=jnp.int32)
    cosine, sine_table = rotary_tables(position.astype(F32), quarter)
    queries = (
        rotate(
            projected[:, :query_cols].reshape(tok_rows, heads, HD),
            cosine[:, None, :],
            sine_table[:, None, :],
            quarter,
        )
        * query_scale
    ).astype(BF16)
    queries = queries.reshape(tok_rows, query_cols)
    keys_rot = rotate(projected[:, query_cols : query_cols + HD], cosine, sine_table, quarter)
    own_kv = jnp.concatenate([keys_rot, projected[:, query_cols + HD :]], axis=1).astype(BF16)

    reach = min((WINDOW + tok_rows - 2) // tok_rows, peers - 1)
    window_rows = (reach + 1) * tok_rows
    window_start = jnp.maximum(device - reach, 0) * tok_rows
    kv_window = lax.dynamic_slice_in_dim(gather_rows([own_kv], 6, "gather_kv")[0], window_start, window_rows, 0)
    place = (device * tok_rows - window_start).astype(jnp.int32).reshape(1)
    attention, logs = attend(place, queries, kv_window)

    residual_mid = resid_in + jnp.dot(attention, out_full, preferred_element_type=F32)
    square_two = jnp.mean(residual_mid * residual_mid, axis=1, keepdims=True)
    scale_two = lax.rsqrt(square_two + EPSILON)
    normed_two = residual_mid * scale_two
    hidden_two = (normed_two * gain_two).astype(BF16)

    gate_pieces = pad_columns(gate_weight.reshape(rows, peers, ffn_own), ffn_pad)
    up_pieces = pad_columns(up_weight.reshape(rows, peers, ffn_own), ffn_pad)
    both_own = swap(
        jnp.concatenate([gate_pieces, up_pieces], axis=2).transpose(1, 0, 2)
    ).reshape(peers * rows, 2 * ffn_pad)
    both_bias = jnp.concatenate(
        [pad_columns(gate_bias, ffn_pad), pad_columns(up_bias, ffn_pad)]
    ).astype(F32)
    down_own = jnp.pad(down_weight, ((0, ffn_pad - ffn_own), (0, 0)))

    normed_grad_two, ffn_out, grad_both, grad_down, bias_share, down_bias_share = feed_forward(
        hidden_two, cotangent_full, both_own, both_bias, down_own, rows
    )
    layer_output = (residual_mid + (ffn_out + bias_down)).astype(BF16)
    rms_values = jnp.stack(
        [jnp.sqrt(square_one[:, 0] + EPSILON), jnp.sqrt(square_two[:, 0] + EPSILON)], axis=0
    )
    grad_down = grad_down[:ffn_own]
    grad_both = swap(grad_both.astype(BF16).reshape(peers, rows, 2 * ffn_pad)).transpose(1, 0, 2)
    grad_both = grad_both.astype(F32)
    grad_gate = grad_both[:, :, :ffn_own].reshape(rows, peers * ffn_own)
    grad_up = grad_both[:, :, ffn_pad : ffn_pad + ffn_own].reshape(rows, peers * ffn_own)

    norm2_part = jnp.sum(normed_grad_two * normed_two, axis=0)
    weighted_two = normed_grad_two * gain_two
    mid_grad = out_cotangent.astype(F32) + scale_two * (
        weighted_two - normed_two * jnp.mean(weighted_two * normed_two, axis=1, keepdims=True)
    )
    mid_grad_low = mid_grad.astype(BF16)
    attention_grad = dot(mid_grad_low, out_full, ((1,), (1,))).astype(BF16)

    query_grad, kv_part = attend_back(place, queries, kv_window, logs, attention_grad)
    kv_partial = lax.dynamic_update_slice_in_dim(
        jnp.zeros((peers * tok_rows, 2 * HD), BF16), kv_part.astype(BF16), window_start, 0
    )
    kv_grad = sum_rows(kv_partial, 256, 3, "sum_grad_kv")
    query_raw_grad = (
        rotate(
            query_grad.reshape(tok_rows, heads, HD) * query_scale,
            cosine[:, None, :],
            -sine_table[:, None, :],
            quarter,
        )
        .reshape(tok_rows, query_cols)
        .astype(BF16)
    )
    key_raw_grad = rotate(kv_grad[:, :HD], cosine, -sine_table, quarter)
    kv_raw_grad = jnp.concatenate([key_raw_grad, kv_grad[:, HD:]], axis=1).astype(BF16)
    proj_grad = jnp.concatenate([query_raw_grad, kv_raw_grad], axis=1)
    normed_grad_one = dot(proj_grad, proj_full, ((1,), (1,)))
    norm1_part = jnp.sum(normed_grad_one * normed_one, axis=0)
    weighted_one = normed_grad_one * gain_one
    input_grad = (
        mid_grad
        + scale_one
        * (weighted_one - normed_one * jnp.mean(weighted_one * normed_one, axis=1, keepdims=True))
    ).astype(BF16)

    parts = pad_columns(jnp.stack([norm1_part, norm2_part], axis=1), LANES)
    grad_out, tail = sum_products(
        attention, mid_grad_low, hidden_one, proj_grad, parts.astype(BF16)
    )
    grad_proj = tail[:, :proj_cols]
    norm1_share = tail[:, proj_cols]
    norm2_share = tail[:, proj_cols + 1]
    return (
        layer_output,
        residual_mid,
        rms_values,
        input_grad,
        norm1_share,
        grad_proj[:, :query_cols],
        grad_proj[:, query_cols:],
        grad_out,
        norm2_share,
        grad_gate,
        bias_share[:ffn_own],
        grad_up,
        bias_share[ffn_pad : ffn_pad + ffn_own],
        grad_down,
        down_bias_share,
    )


def solution(mesh):
    by_rows, by_entry = P(AXIS, None), P(AXIS)
    in_specs = (
        by_rows,
        by_entry,
        by_rows,
        by_rows,
        by_rows,
        by_entry,
        by_rows,
        by_entry,
        by_rows,
        by_entry,
        by_rows,
        by_entry,
        by_rows,
    )
    out_specs = (
        by_rows,
        by_rows,
        P(None, AXIS),
        by_rows,
        by_entry,
        by_rows,
        by_rows,
        by_rows,
        by_entry,
        by_rows,
        by_entry,
        by_rows,
        by_entry,
        by_rows,
        by_entry,
    )
    return jax.shard_map(body, mesh=mesh, in_specs=in_specs, out_specs=out_specs, check_vma=False)
```

```python
import functools
import math

import jax
import jax.numpy as jnp
from jax import lax
from jax.experimental import pallas as pl
from jax.experimental.pallas import tpu as pltpu
from jax.sharding import PartitionSpec as P

HD = 256
WINDOW = 2048
EPSILON = 1e-06
NEGATIVE = -1e30
ROTARY_BASE = 10000.0
AXIS = "blk"
LANES = 128
DEVICES = 32
PAIR = 2
VMEM_BYTES = 48 * 1024 * 1024
F32 = jnp.float32
BF16 = jnp.bfloat16


def rotary_tables(positions, quarter):
    frequency = ROTARY_BASE ** (-(jnp.arange(quarter, dtype=F32) / quarter))
    angles = positions[:, None] * frequency[None, :]
    return (jnp.cos(angles), jnp.sin(angles))


def rotate(vector, cosine, sine_table, quarter):
    leading = vector[..., :quarter]
    trailing = vector[..., quarter : 2 * quarter]
    return jnp.concatenate(
        [
            leading * cosine - trailing * sine_table,
            trailing * cosine + leading * sine_table,
            vector[..., 2 * quarter :],
        ],
        axis=-1,
    )


def dot(left, right, contract):
    return lax.dot_general(left, right, (contract, ((), ())), preferred_element_type=F32)


def round_up(count, step):
    return (count + step - 1) // step * step


def pad_columns(values, columns):
    pad = [(0, 0)] * (values.ndim - 1) + [(0, columns - values.shape[-1])]
    return jnp.pad(values, pad)


def masked_scores(ahead, query_rows, keys, tok_rows):
    scores = dot(query_rows, keys, ((1,), (1,)))
    rows = lax.broadcasted_iota(jnp.int32, scores.shape, 0) % tok_rows
    columns = lax.broadcasted_iota(jnp.int32, scores.shape, 1)
    distance = rows - columns + ahead
    return jnp.where((distance >= 0) & (distance < WINDOW), scores, NEGATIVE)


def stack_heads(block):
    return jnp.concatenate([block[:, i * HD : (i + 1) * HD] for i in range(PAIR)], axis=0)


def unstack_heads(rows):
    tok_rows = rows.shape[0] // PAIR
    return jnp.concatenate([rows[i * tok_rows : (i + 1) * tok_rows] for i in range(PAIR)], axis=1)


def attend_pair(ahead, query, keys, values):
    tok_rows = query.shape[0]
    scores = masked_scores(ahead, stack_heads(query), keys, tok_rows)
    row_max = jnp.max(scores, axis=1, keepdims=True)
    probs = jnp.exp(scores - row_max)
    row_sum = jnp.sum(probs, axis=1, keepdims=True)
    probs_low = (probs * (1.0 / row_sum)).astype(BF16)
    attended = dot(probs_low, values, ((1,), (0,)))
    return unstack_heads(attended).astype(BF16), row_max + jnp.log(row_sum)


def attend_kernel(place_ref, query_ref, kv_ref, out_ref, log_ref):
    attended, logs = attend_pair(place_ref[0], query_ref[...], kv_ref[:, :HD], kv_ref[:, HD:])
    out_ref[...] = attended
    log_ref[0] = jnp.broadcast_to(logs, log_ref.shape[1:])


def attend_back_kernel(place_ref, query_ref, kv_ref, log_ref, grad_ref, query_grad_ref, kv_grad_ref):
    tok_rows = query_ref.shape[0]
    query_rows = stack_heads(query_ref[...])
    grad_rows = stack_heads(grad_ref[...])
    keys, values = kv_ref[:, :HD], kv_ref[:, HD:]
    scores = masked_scores(place_ref[0], query_rows, keys, tok_rows)
    probs = jnp.exp(scores - log_ref[0][:, :1])
    prob_grad = dot(grad_rows, values, ((1,), (1,)))
    delta = jnp.sum(probs * prob_grad, axis=1, keepdims=True)
    score_grad = (probs * (prob_grad - delta)).astype(BF16)
    query_grad_ref[...] = unstack_heads(dot(score_grad, keys, ((1,), (0,))))
    key_part = dot(score_grad, query_rows, ((0,), (0,)))
    value_part = dot(probs.astype(BF16), grad_rows, ((0,), (0,)))

    @pl.when(pl.program_id(0) == 0)
    def _():
        kv_grad_ref[:, :HD] = key_part
        kv_grad_ref[:, HD:] = value_part

    @pl.when(pl.program_id(0) > 0)
    def _():
        kv_grad_ref[:, :HD] += key_part
        kv_grad_ref[:, HD:] += value_part


def attention_specs(tok_rows, heads, window_rows):
    place = pl.BlockSpec(memory_space=pltpu.SMEM)
    by_head = pl.BlockSpec((tok_rows, PAIR * HD), lambda i: (0, i))
    whole = pl.BlockSpec((window_rows, 2 * HD), lambda i: (0, 0))
    logs = pl.BlockSpec((1, PAIR * tok_rows, LANES), lambda i: (i, 0, 0))
    return place, by_head, whole, logs


def attend(place, queries, kv_window):
    tok_rows, features = queries.shape
    window_rows = kv_window.shape[0]
    pairs = features // HD // PAIR
    place_spec, by_head, whole, logs = attention_specs(tok_rows, features // HD, window_rows)
    work = tok_rows * features * window_rows
    return pl.pallas_call(
        attend_kernel,
        grid=(pairs,),
        out_shape=(
            jax.ShapeDtypeStruct((tok_rows, features), BF16),
            jax.ShapeDtypeStruct((pairs, PAIR * tok_rows, LANES), F32),
        ),
        in_specs=[place_spec, by_head, whole],
        out_specs=(by_head, logs),
        compiler_params=pltpu.CompilerParams(vmem_limit_bytes=VMEM_BYTES),
        cost_estimate=pl.CostEstimate(
            flops=4 * work, bytes_accessed=8 * kv_window.size, transcendentals=work // HD
        ),
        name="attend",
    )(place, queries, kv_window)


def attend_back(place, queries, kv_window, logs_in, grad):
    tok_rows, features = queries.shape
    window_rows = kv_window.shape[0]
    pairs = features // HD // PAIR
    place_spec, by_head, whole, logs = attention_specs(tok_rows, features // HD, window_rows)
    work = tok_rows * features * window_rows
    return pl.pallas_call(
        attend_back_kernel,
        grid=(pairs,),
        out_shape=(
            jax.ShapeDtypeStruct((tok_rows, features), F32),
            jax.ShapeDtypeStruct((window_rows, 2 * HD), F32),
        ),
        in_specs=[place_spec, by_head, whole, logs, by_head],
        out_specs=(by_head, whole),
        compiler_params=pltpu.CompilerParams(vmem_limit_bytes=VMEM_BYTES),
        cost_estimate=pl.CostEstimate(
            flops=10 * work, bytes_accessed=8 * kv_window.size, transcendentals=work // HD
        ),
        name="attend_back",
    )(place, queries, kv_window, logs_in, grad)


MESH=pl.DeviceIdType.MESH

class Place:
    def __init__(self):
        me = lax.axis_index(AXIS)
        self.core = me % 2
        self.x = (me // 2) % 2
        self.y = (me // 4) % 2
        self.z = me // 8
        self.sibling = self.index(self.z, self.y, self.x, 1 - self.core)
        self.next_x = self.index(self.z, self.y, 1 - self.x, self.core)
        self.next_y = self.index(self.z, 1 - self.y, self.x, self.core)
        self.plane = [self.z] + [(self.z + o) % 4 for o in (1, 2, 3)]
        self.line = [self.index(p, self.y, self.x, self.core) for p in self.plane]
    def index(self, z, y, x, core):
        return ((z * 2 + y) * 2 + x) * 2 + core
    def side(self, dy, dx):
        return (1 - self.y if dy else self.y), (1 - self.x if dx else self.x)
    def meet(self):
        barrier = pltpu.get_barrier_semaphore()
        partners = [self.sibling, self.next_x, self.next_y] + self.line[1:]
        for device in partners:
            pl.semaphore_signal(barrier, inc=1, device_id=(device,), device_id_type=MESH)
        pl.semaphore_wait(barrier, len(partners))

def send(src, dst, sems, device):
    copy = pltpu.make_async_remote_copy(src_ref=src, dst_ref=dst, send_sem=sems[0], recv_sem=sems[1], device_id=(device,), device_id_type=MESH)
    copy.start()
    return copy

TILE=16
def add_rows(total, other, first, count):
    planes = other.shape[0]
    steps = count // TILE
    @pl.loop(0, planes * steps)
    def _(i):
        plane, row = i // steps, (i % steps) * TILE
        here = (plane, pl.ds(pl.multiple_of(row + first, TILE), TILE), slice(None))
        there = (plane, pl.ds(pl.multiple_of(row, TILE), TILE), slice(None))
        total[here] = (total[here].astype(F32) + other[there].astype(F32)).astype(BF16)

def sum_kernel(chunk, in_ref, out_ref, acc, got_core, got_diag_x, got_diag_y, got_x, got_y, got_z,
               load_sem, core_sems, diag_sems, side_sems, line_sems):
    place = Place()
    rows, columns = out_ref.shape
    upper = got_diag_x.shape[1]
    lower = rows - upper
    chunks = columns // chunk
    corners = [(1, 1), (0, 1), (1, 0), (0, 0)]
    cols = [pl.ds(k * chunk, chunk) for k in range(chunks)]
    loads, cores, sends = {}, {}, []
    for k in range(chunks):
        for i, (dy, dx) in enumerate(corners):
            y, x = place.side(dy, dx)
            load = pltpu.make_async_copy(in_ref.at[:, y, x, place.core, :, cols[k]], acc.at[i, :, :, cols[k]], load_sem.at[k, i])
            load.start()
            loads[k, i] = load
    place.meet()
    for k in range(chunks):
        for i, (dy, dx) in enumerate(corners):
            y, x = place.side(dy, dx)
            cores[k, i] = send(in_ref.at[:, y, x, 1 - place.core, :, cols[k]], got_core.at[i, :, :, cols[k]],
                               (core_sems.at[0, k, i], core_sems.at[1, k, i]), place.sibling)
    top, bottom = pl.ds(0, upper), pl.ds(upper, lower)
    diag, side, line = {}, {}, {}
    def pair(sems, k, i): return (sems.at[0, k, i], sems.at[1, k, i])
    def stage0(k):
        for i in range(4):
            loads[k, i].wait(); cores[k, i].wait_recv()
            add_rows(acc.at[i, :, :, cols[k]], got_core.at[i, :, :, cols[k]], 0, rows)
            if i == 0:
                diag[k, 0] = send(acc.at[0, :, top, cols[k]], got_diag_x.at[:, :, cols[k]], pair(diag_sems, k, 0), place.next_x)
                diag[k, 1] = send(acc.at[0, :, bottom, cols[k]], got_diag_y.at[:, :, cols[k]], pair(diag_sems, k, 1), place.next_y)
            if i == 1:
                side[k, 0] = send(acc.at[1, :, top, cols[k]], got_x.at[:, top, cols[k]], pair(side_sems, k, 0), place.next_x)
            if i == 2:
                side[k, 1] = send(acc.at[2, :, bottom, cols[k]], got_y.at[:, bottom, cols[k]], pair(side_sems, k, 1), place.next_y)
    def stage1(k):
        diag[k, 0].wait_recv()
        add_rows(acc.at[2, :, :, cols[k]], got_diag_x.at[:, :, cols[k]], 0, upper)
        side[k, 2] = send(acc.at[2, :, top, cols[k]], got_y.at[:, top, cols[k]], pair(side_sems, k, 2), place.next_y)
        diag[k, 1].wait_recv()
        add_rows(acc.at[1, :, :, cols[k]], got_diag_y.at[:, :, cols[k]], upper, lower)
        side[k, 3] = send(acc.at[1, :, bottom, cols[k]], got_x.at[:, bottom, cols[k]], pair(side_sems, k, 3), place.next_x)
    def stage2(k):
        for i in range(4): side[k, i].wait_recv()
        steps = rows // TILE
        @pl.loop(0, 4 * steps)
        def _(i):
            plane, row = i // steps, (i % steps) * TILE
            here = (plane, pl.ds(pl.multiple_of(row, TILE), TILE), cols[k])
            acc[(3,) + here] = (acc[(3,) + here].astype(F32) + got_x[here].astype(F32) + got_y[here].astype(F32)).astype(BF16)
        for o in (1, 2, 3):
            line[k, o] = send(acc.at[3, place.plane[o], :, cols[k]], got_z.at[o - 1, :, cols[k]], pair(line_sems, k, o - 1), place.line[o])
    def stage3(k):
        for o in (1, 2, 3): line[k, o].wait_recv()
        @pl.loop(0, rows // TILE)
        def _(i):
            here = (pl.ds(pl.multiple_of(i * TILE, TILE), TILE), cols[k])
            total = acc[(3, place.z) + here].astype(F32)
            for o in range(3): total += got_z[(o,) + here].astype(F32)
            out_ref[here] = total
    stages = [stage0, stage1, stage2, stage3]
    for step in range(chunks + 3):
        for s in range(3, -1, -1):
            if 0 <= step - s < chunks: stages[s](step - s)
    for group in (cores, diag, side, line):
        for copy in group.values(): copy.wait_send()

def sum_over_devices(partial, chunk, collective_id, name):
    rows, columns = partial.shape[0] // 32, partial.shape[1]
    chunks = columns // chunk
    upper = (rows // 2 + TILE - 1) // TILE * TILE
    def buf(*shape): return pltpu.VMEM(shape, BF16)
    def sems(count): return pltpu.SemaphoreType.DMA((2, chunks, count))
    return pl.pallas_call(
        functools.partial(sum_kernel, chunk),
        out_shape=jax.ShapeDtypeStruct((rows, columns), F32),
        in_specs=[pl.BlockSpec(memory_space=pl.ANY)],
        out_specs=pl.BlockSpec(memory_space=pltpu.VMEM),
        scratch_shapes=[buf(4, 4, rows, columns), buf(4, 4, rows, columns), buf(4, upper, columns), buf(4, rows - upper, columns),
            buf(4, rows, columns), buf(4, rows, columns), buf(3, rows, columns),
            pltpu.SemaphoreType.DMA((chunks, 4)), sems(4), sems(2), sems(4), sems(3)],
        compiler_params=pltpu.CompilerParams(collective_id=collective_id, has_side_effects=True, vmem_limit_bytes=56*1024*1024),
        name=name,
    )(partial.reshape(4, 2, 2, 2, rows, columns))


CORNERS = ((1, 1), (0, 1), (1, 0), (0, 0))

def add_tiles(count, rows, target, parts):
    steps = rows // TILE
    @pl.loop(0, count * steps)
    def _(i):
        index, here = i // steps, pl.ds(pl.multiple_of((i % steps) * TILE, TILE), TILE)
        total = None
        for ref, first in parts:
            at = here if first == 0 else pl.ds(pl.multiple_of((i % steps) * TILE + first, TILE), TILE)
            part = ref[index, at].astype(F32)
            total = part if total is None else total + part
        ref, first = target
        at = here if first == 0 else pl.ds(pl.multiple_of((i % steps) * TILE + first, TILE), TILE)
        ref[index, at] = total.astype(BF16)

class SumBuffers:
    def __init__(self, refs):
        self.acc, self.core, self.diag_x, self.diag_y, self.x, self.y, self.z, self.sems = refs
    @staticmethod
    def shapes(rows, columns, units):
        upper = (rows // 2 + TILE - 1) // TILE * TILE
        buf = lambda *shape: pltpu.VMEM(shape + (columns,), BF16)
        return [buf(4, 4, rows), buf(4, 4, rows), buf(4, upper), buf(4, rows - upper), buf(4, rows), buf(4, rows), buf(3, rows),
                pltpu.SemaphoreType.DMA((units, 2, Sum.COPIES))]
    COUNT = 8

class Sum:
    COPIES = 14
    def __init__(self, place, bufs, unit, cols, own, other, out):
        self.p, self.b, self.unit, self.own, self.other, self.out = place, bufs, unit, own, other, out
        self.rows = bufs.acc.shape[2]
        self.upper = bufs.diag_x.shape[1]
        self.lower = self.rows - self.upper
        self.acc = bufs.acc.at[:, :, :, cols]
        self.core = bufs.core.at[:, :, :, cols]
        self.diag_x, self.diag_y = bufs.diag_x.at[:, :, cols], bufs.diag_y.at[:, :, cols]
        self.x, self.y, self.z = bufs.x.at[:, :, cols], bufs.y.at[:, :, cols], bufs.z.at[:, :, cols]
        self.copies = {}
    def push(self, slot, src, dst, device):
        sems = self.b.sems
        self.copies[slot] = send(src, dst, (sems.at[self.unit, 0, slot], sems.at[self.unit, 1, slot]), device)
    def begin(self):
        for i in range(4):
            self.push(i, self.other(i), self.core.at[i], self.p.sibling)
    def stage0(self):
        top, bottom = pl.ds(0, self.upper), pl.ds(self.upper, self.lower)
        for i in range(4):
            self.copies[i].wait_recv()
            add_tiles(4, self.rows, (self.acc.at[i], 0), [(self.own(i), 0), (self.core.at[i], 0)])
            if i == 0:
                self.push(4, self.acc.at[0, :, top], self.diag_x, self.p.next_x)
                self.push(5, self.acc.at[0, :, bottom], self.diag_y, self.p.next_y)
            if i == 1:
                self.push(6, self.acc.at[1, :, top], self.x.at[:, top], self.p.next_x)
            if i == 2:
                self.push(7, self.acc.at[2, :, bottom], self.y.at[:, bottom], self.p.next_y)
    def stage1(self):
        top, bottom = pl.ds(0, self.upper), pl.ds(self.upper, self.lower)
        self.copies[4].wait_recv()
        add_tiles(4, self.upper, (self.acc.at[2], 0), [(self.acc.at[2], 0), (self.diag_x, 0)])
        self.push(8, self.acc.at[2, :, top], self.y.at[:, top], self.p.next_y)
        self.copies[5].wait_recv()
        add_tiles(4, self.lower, (self.acc.at[1], self.upper), [(self.acc.at[1], self.upper), (self.diag_y, 0)])
        self.push(9, self.acc.at[1, :, bottom], self.x.at[:, bottom], self.p.next_x)
    def stage2(self):
        for slot in (6, 7, 8, 9):
            self.copies[slot].wait_recv()
        add_tiles(4, self.rows, (self.acc.at[3], 0), [(self.acc.at[3], 0), (self.x, 0), (self.y, 0)])
        for o in (1, 2, 3):
            self.push(9 + o, self.acc.at[3, self.p.plane[o]], self.z.at[o - 1], self.p.line[o])
    def stage3(self):
        for o in (1, 2, 3):
            self.copies[9 + o].wait_recv()
        @pl.loop(0, self.rows // TILE)
        def _(i):
            here = pl.ds(pl.multiple_of(i * TILE, TILE), TILE)
            total = self.acc[3, self.p.z, here].astype(F32)
            for o in range(3):
                total += self.z[o, here].astype(F32)
            self.out[here] = total
    def core_sent(self):
        for i in range(4): self.copies[i].wait_send()
    def finish(self):
        for slot in range(4, 13): self.copies[slot].wait_send()

def product_sums_kernel(chunk, left_a, right_a, left_b, right_b, extra, out_a, out_b, part, *scratch):
    place = Place()
    bufs = SumBuffers(scratch)
    rows = out_a.shape[0]
    wide = 8 * rows
    units = []
    def add_unit(left, right, out, first, span, more):
        k = len(units)
        slot = k % 2
        def own(i):
            y, x = place.side(*CORNERS[i])
            return part.at[slot, :, y, x, place.core]
        def other(i):
            y, x = place.side(*CORNERS[i])
            return part.at[slot, :, y, x, 1 - place.core]
        cols = pl.ds(k * chunk, chunk)
        unit = Sum(place, bufs, k, cols, own, other, out.at[:, pl.ds(first, chunk)])
        def make():
            if k >= 2: units[k - 2][0].core_sent()
            @pl.loop(0, 4)
            def _(z):
                here = pl.ds(pl.multiple_of(z * wide, wide), wide)
                product = lax.dot_general(left[:, here], right[:, pl.ds(first, span)], (((0,), (0,)), ((), ())), preferred_element_type=F32)
                part[slot, z, :, :, :, :, pl.ds(0, span)] = product.astype(BF16).reshape(2, 2, 2, rows, span)
                if more is not None:
                    part[slot, z, :, :, :, :, pl.ds(span, chunk - span)] = more[here].reshape(2, 2, 2, rows, chunk - span)
            unit.begin()
        units.append((unit, make))
    for first in range(0, out_a.shape[1], chunk):
        add_unit(left_a, right_a, out_a, first, chunk, None)
    for first in range(0, out_b.shape[1], chunk):
        span = min(chunk, right_b.shape[1] - first)
        add_unit(left_b, right_b, out_b, first, span, None if span == chunk else extra)
    place.meet()
    count = len(units)
    stages = [lambda k: units[k][1](), lambda k: units[k][0].stage0(), lambda k: units[k][0].stage1(), lambda k: units[k][0].stage2(), lambda k: units[k][0].stage3()]
    for step in range(count + 4):
        for s in (1, 2, 3, 4, 0):
            if 0 <= step - s < count: stages[s](step - s)
    for unit, _ in units[-2:]: unit.core_sent()
    for unit, _ in units: unit.finish()

def product_sums(left_a, right_a, left_b, right_b, extra, chunk, collective_id, name):
    rows = left_a.shape[1] // 32
    columns_a, columns_b = right_a.shape[1], right_b.shape[1] + extra.shape[1]
    total = columns_a + columns_b
    vmem = pl.BlockSpec(memory_space=pltpu.VMEM)
    return pl.pallas_call(
        functools.partial(product_sums_kernel, chunk),
        out_shape=(jax.ShapeDtypeStruct((rows, columns_a), F32), jax.ShapeDtypeStruct((rows, columns_b), F32)),
        in_specs=[vmem] * 5,
        out_specs=(vmem, vmem),
        scratch_shapes=[pltpu.VMEM((2, 4, 2, 2, 2, rows, chunk), BF16)] + SumBuffers.shapes(rows, total, total // chunk),
        compiler_params=pltpu.CompilerParams(collective_id=collective_id, has_side_effects=True, vmem_limit_bytes=62*1024*1024),
        name=name,
    )(left_a, right_a, left_b, right_b, extra)


PLANES=4
def plane_order(z):
    near = jnp.minimum(z, 3 - z)
    flip = z // 2
    order = []
    for k in range(4):
        swapped = 1 - k if k < 2 else k
        plane = near * swapped + (1 - near) * k
        order.append(flip * (3 - plane) + (1 - flip) * plane)
    return order

class Gather:
    COPIES = 11
    def __init__(self, place, own, held, cols, sems):
        self.place, self.held, self.cols, self.sems = place, held, cols, sems
        self.own = own.at[:, cols]
        rows = held.shape[4]
        upper = (rows // 2 + TILE - 1) // TILE * TILE
        self.halves = pl.ds(0, upper), pl.ds(upper, rows - upper)
        self.order = plane_order(place.z)
        self.sent = []
        self.kept = []
    def at(self, plane, y, x, core, part=slice(None)):
        return self.held.at[plane, y, x, core, part, self.cols]
    def pair(self, slot, k):
        return self.sems.at[0, slot, k], self.sems.at[1, slot, k]
    def push(self, src, dst, slot, k, device):
        copy = send(src, dst, self.pair(slot, k), device)
        self.sent.append(copy)
    def arrived(self, ref, slot, k):
        pltpu.make_async_remote_copy(src_ref=ref, dst_ref=ref, send_sem=self.sems.at[0, slot, k], recv_sem=self.sems.at[1, slot, k], device_id=(self.place.sibling,), device_id_type=MESH).wait_recv()
    def start(self):
        p = self.place
        mine = self.at(p.z, p.y, p.x, p.core)
        keep = pltpu.make_async_copy(self.own, mine, self.sems.at[0, 10, 0])
        keep.start()
        self.kept.append(keep)
        for k in (1, 2, 3):
            plane = self.order[k]
            copy = pltpu.make_async_remote_copy(src_ref=self.own, dst_ref=mine, send_sem=self.sems.at[0, 0, k], recv_sem=self.sems.at[1, 0, p.z], device_id=(p.index(plane, p.y, p.x, p.core),), device_id_type=MESH)
            copy.start(); self.sent.append(copy)
    def line(self, k):
        p = self.place
        plane = self.order[k]
        block = self.at(plane, p.y, p.x, p.core)
        source = self.own if k == 0 else block
        if k > 0:
            pltpu.make_async_remote_copy(src_ref=block, dst_ref=block, send_sem=self.sems.at[0, 0, k], recv_sem=self.sems.at[1, 0, plane], device_id=(p.sibling,), device_id_type=MESH).wait_recv()
        self.push(source, block, 1, k, p.next_x)
        self.push(source, block, 2, k, p.next_y)
        self.push(source, block, 5, k, p.sibling)
    def side(self, k):
        p, plane = self.place, self.order[k]
        top, bottom = self.halves
        self.arrived(self.at(plane, p.y, 1 - p.x, p.core), 1, k)
        block = self.at(plane, p.y, 1 - p.x, p.core, top)
        self.push(block, block, 4, k, p.next_y)
        block = self.at(plane, p.y, 1 - p.x, p.core)
        self.push(block, block, 6, k, p.sibling)
        self.arrived(self.at(plane, 1 - p.y, p.x, p.core), 2, k)
        block = self.at(plane, 1 - p.y, p.x, p.core, bottom)
        self.push(block, block, 3, k, p.next_x)
        block = self.at(plane, 1 - p.y, p.x, p.core)
        self.push(block, block, 7, k, p.sibling)
    def diag(self, k):
        p, plane = self.place, self.order[k]
        for slot, part in ((4, self.halves[0]), (3, self.halves[1])):
            block = self.at(plane, 1 - p.y, 1 - p.x, p.core, part)
            self.arrived(block, slot, k)
            self.push(block, block, slot + 5, k, p.sibling)
    def ready(self, k):
        p, plane = self.place, self.order[k]
        top, bottom = self.halves
        if k == 0:
            for keep in self.kept: keep.wait()
        other = 1 - p.core
        self.arrived(self.at(plane, p.y, p.x, other), 5, k)
        self.arrived(self.at(plane, p.y, 1 - p.x, other), 6, k)
        self.arrived(self.at(plane, 1 - p.y, p.x, other), 7, k)
        self.arrived(self.at(plane, 1 - p.y, 1 - p.x, other, top), 9, k)
        self.arrived(self.at(plane, 1 - p.y, 1 - p.x, other, bottom), 8, k)
    def finish(self):
        for copy in self.sent: copy.wait_send()

def pipeline(stages, count):
    for step in range(count + len(stages) - 1):
        for s in range(len(stages) - 1, -1, -1):
            if 0 <= step - s < count:
                stages[s](step - s)

def gather_kernel(chunks, *refs):
    n = len(chunks)
    ins, outs, sems = refs[:n], refs[n:2*n], refs[2*n:]
    place = Place()
    place.meet()
    items = []
    for a in range(n):
        width = ins[a].shape[1] // chunks[a]
        for j in range(chunks[a]):
            items.append(Gather(place, ins[a], outs[a], pl.ds(j * width, width), sems[a].at[j]))
    def line(s):
        if s % PLANES == 0:
            items[s // PLANES].start()
        items[s // PLANES].line(s % PLANES)
    def side(s): items[s // PLANES].side(s % PLANES)
    def diag(s): items[s // PLANES].diag(s % PLANES)
    pipeline([line, side, diag], len(items) * PLANES)
    for item in items:
        for k in range(PLANES): item.ready(k)
    for item in items: item.finish()

def gather_all(arrays, chunks, collective_id, name):
    outs = pl.pallas_call(
        functools.partial(gather_kernel, chunks),
        out_shape=tuple(jax.ShapeDtypeStruct((4,2,2,2)+a.shape, BF16) for a in arrays),
        in_specs=[pl.BlockSpec(memory_space=pl.ANY)]*len(arrays),
        out_specs=tuple(pl.BlockSpec(memory_space=pl.ANY) for _ in arrays),
        scratch_shapes=[pltpu.SemaphoreType.DMA((c, 2, Gather.COPIES, PLANES)) for c in chunks],
        compiler_params=pltpu.CompilerParams(collective_id=collective_id, has_side_effects=True),
        name=name,
    )(*arrays)
    return [o.reshape(32 * a.shape[0], a.shape[1]) for o, a in zip(outs, arrays)]


GELU_SCALE = math.sqrt(2.0 / math.pi)
GELU_CUBE = 0.044715

def gelu_and_slope(v):
    square = v * v
    t = jnp.tanh(GELU_SCALE * v * (1.0 + GELU_CUBE * square))
    half = 0.5 * (1.0 + t)
    slope = half + 0.5 * v * (1.0 - t * t) * (GELU_SCALE * (1.0 + 3.0 * GELU_CUBE * square))
    return v * half, slope

def gather_attend_kernel(
    kv_ref, weight_ref, cotangent_ref, query_ref,
    kv_held, weight_held, cotangent_held, window, out_ref, log_ref,
    kv_sems, weight_sems, cotangent_sems, load_sems,
):
    place = Place()
    me = lax.axis_index(AXIS)
    tok_rows, features = query_ref.shape
    blocks = window.shape[0] // tok_rows
    start = jnp.maximum(me - (blocks - 1), 0)
    place.meet()

    def item(own, held, sems):
        return Gather(place, own, held, pl.ds(0, own.shape[1]), sems)

    kv = item(kv_ref, kv_held, kv_sems)
    weight = item(weight_ref, weight_held, weight_sems)
    cotangent = item(cotangent_ref, cotangent_held, cotangent_sems)
    for one in (kv, weight, cotangent):
        one.start()

    def run(*steps):
        for one, name, k in steps:
            getattr(one, name)(k)

    run(
        (kv, "line", 0), (weight, "line", 0), (kv, "line", 1), (kv, "side", 0),
        (kv, "line", 2), (kv, "side", 1), (kv, "diag", 0), (kv, "line", 3),
        (kv, "side", 2), (kv, "diag", 1), (kv, "side", 3), (kv, "diag", 2), (kv, "diag", 3),
        (weight, "line", 1), (cotangent, "line", 0), (weight, "side", 0), (weight, "line", 2),
        (weight, "side", 1), (weight, "diag", 0), (weight, "line", 3), (cotangent, "line", 1),
        (kv, "ready", 0), (kv, "ready", 1), (kv, "ready", 2), (kv, "ready", 3),
    )
    loads = []
    for j in range(blocks):
        block = start + j
        load = pltpu.make_async_copy(
            kv_held.at[block // 8, (block // 4) % 2, (block // 2) % 2, block % 2],
            window.at[pl.ds(j * tok_rows, tok_rows)],
            load_sems.at[j],
        )
        load.start()
        loads.append(load)
    for load in loads:
        load.wait()
    run((weight, "side", 2), (weight, "diag", 1))
    ahead = (me - start) * tok_rows

    @pl.loop(0, features // (PAIR * HD))
    def _(i):
        here = pl.ds(pl.multiple_of(i * PAIR * HD, PAIR * HD), PAIR * HD)
        attended, logs = attend_pair(ahead, query_ref[:, here], window[:, :HD], window[:, HD:])
        out_ref[:, here] = attended
        log_ref[i] = jnp.broadcast_to(logs, log_ref.shape[1:])

    run(
        (cotangent, "side", 0), (weight, "side", 3), (weight, "diag", 2), (cotangent, "line", 2),
        (weight, "diag", 3), (cotangent, "side", 1), (cotangent, "diag", 0),
        (cotangent, "line", 3), (cotangent, "side", 2), (cotangent, "diag", 1),
        (cotangent, "side", 3), (cotangent, "diag", 2), (cotangent, "diag", 3),
    )
    for one in (weight, cotangent):
        for k in range(PLANES):
            one.ready(k)
    for one in (kv, weight, cotangent):
        one.finish()


def gather_attend(own_kv, out_weight, out_cotangent, queries, collective_id):
    tok_rows, features = queries.shape
    blocks = (WINDOW + tok_rows - 2) // tok_rows + 1
    pairs = features // HD // PAIR
    arrays = (own_kv, out_weight, out_cotangent)
    hbm = pl.BlockSpec(memory_space=pl.ANY)
    vmem = pl.BlockSpec(memory_space=pltpu.VMEM)
    outs = pl.pallas_call(
        gather_attend_kernel,
        out_shape=tuple(jax.ShapeDtypeStruct((4, 2, 2, 2) + a.shape, BF16) for a in arrays)
        + (
            jax.ShapeDtypeStruct((blocks * tok_rows, own_kv.shape[1]), BF16),
            jax.ShapeDtypeStruct((tok_rows, features), BF16),
            jax.ShapeDtypeStruct((pairs, PAIR * tok_rows, LANES), F32),
        ),
        in_specs=[hbm] * 3 + [vmem],
        out_specs=(hbm,) * 3 + (vmem,) * 3,
        scratch_shapes=[pltpu.SemaphoreType.DMA((2, Gather.COPIES, PLANES)) for _ in arrays]
        + [pltpu.SemaphoreType.DMA((blocks,))],
        compiler_params=pltpu.CompilerParams(
            collective_id=collective_id, has_side_effects=True, vmem_limit_bytes=VMEM_BYTES
        ),
        name="gather_attend",
    )(*arrays, queries)
    full = [o.reshape(32 * a.shape[0], a.shape[1]) for o, a in zip(outs[1:3], arrays[1:])]
    return full[0], full[1], outs[3], outs[4], outs[5]


class PlaneSum:
    SLOTS = 10
    def __init__(self, place, order, kind, k, acc, outgoing, out, land, load, sems, line_sems, load_sems):
        self.p, self.k, self.order = place, k, order
        self.acc, self.outgoing = acc.at[kind, k], outgoing.at[kind]
        self.out = out
        core, diag_x, diag_y, side_x, side_y, line = land
        self.core, self.side_x, self.side_y = core.at[kind, k], side_x.at[kind, k], side_y.at[kind, k]
        self.diag_x, self.diag_y, self.land = diag_x.at[kind, k], diag_y.at[kind, k], line.at[kind]
        self.load, self.load_sems = load, load_sems
        self.sems, self.line_sems = sems.at[kind, k], line_sems.at[kind]
        self.rows = self.acc.shape[1]
        self.upper = self.diag_x.shape[0]
        self.top, self.bottom = pl.ds(0, self.upper), pl.ds(self.upper, self.rows - self.upper)
    def mine(self, i): return self.acc.at[i]
    def copy(self, src, dst, slot, device):
        return pltpu.make_async_remote_copy(src_ref=src, dst_ref=dst, send_sem=self.sems.at[0, slot], recv_sem=self.sems.at[1, slot], device_id=(device,), device_id_type=MESH)
    def across(self, i):
        return self.copy(self.outgoing.at[i % 2], self.core.at[i], i, self.p.sibling)
    def make(self, slot):
        p, mine = self.p, self.mine
        src, dst, device = {
            4: (mine(0).at[self.top], self.diag_x, p.next_x),
            5: (mine(0).at[self.bottom], self.diag_y, p.next_y),
            6: (mine(1).at[self.top], self.side_x.at[self.top], p.next_x),
            7: (mine(2).at[self.bottom], self.side_y.at[self.bottom], p.next_y),
            8: (mine(2).at[self.top], self.side_y.at[self.top], p.next_y),
            9: (mine(1).at[self.bottom], self.side_x.at[self.bottom], p.next_x),
        }[slot]
        return self.copy(src, dst, slot, device)
    def line_copy(self):
        p, plane = self.p, self.order[self.k]
        return pltpu.make_async_remote_copy(src_ref=self.mine(3), dst_ref=self.land.at[p.z], send_sem=self.line_sems.at[0, self.k], recv_sem=self.line_sems.at[1, p.z], device_id=(p.index(plane, p.y, p.x, p.core),), device_id_type=MESH)
    def fetch(self, src, slot):
        rows = src.shape[0]
        copy = pltpu.make_async_copy(src, self.load.at[slot, pl.ds(0, rows)], self.load_sems.at[slot])
        copy.start()
        return copy
    def add(self, target, slots, rows):
        @pl.loop(0, rows // TILE)
        def _(i):
            here = pl.ds(pl.multiple_of(i * TILE, TILE), TILE)
            total = target[here].astype(F32)
            for slot in slots: total += self.load[slot, here].astype(F32)
            target[here] = total.astype(target.dtype)
    def stage0(self):
        self.across(0).wait_recv()
        fetched = self.fetch(self.core.at[0], 0)
        for i in range(4):
            current = fetched
            if i < 3:
                self.across(i + 1).wait_recv()
                fetched = self.fetch(self.core.at[i + 1], (i + 1) % 2)
            current.wait()
            self.add(self.mine(i), [i % 2], self.rows)
            for slot in ((4, 5), (6,), (7,), ())[i]:
                self.make(slot).start()
    def stage1(self):
        self.make(4).wait_recv()
        self.fetch(self.diag_x, 0).wait()
        self.add(self.mine(2).at[self.top], [0], self.upper)
        self.make(8).start()
        self.make(5).wait_recv()
        self.fetch(self.diag_y, 1).wait()
        self.add(self.mine(1).at[self.bottom], [1], self.rows - self.upper)
        self.make(9).start()
    def stage2(self):
        for slot in (6, 9): self.make(slot).wait_recv()
        first = self.fetch(self.side_x, 0)
        for slot in (7, 8): self.make(slot).wait_recv()
        second = self.fetch(self.side_y, 1)
        first.wait(); second.wait()
        if self.k > 0:
            self.add(self.mine(3), [0, 1], self.rows)
            self.line_copy().start()
        else:
            mine, out = self.mine(3), self.out
            @pl.loop(0, self.rows // TILE)
            def _(i):
                here = pl.ds(pl.multiple_of(i * TILE, TILE), TILE)
                out[here] = mine[here].astype(F32) + self.load[0, here].astype(F32) + self.load[1, here].astype(F32)
    def sent(self):
        for slot in range(4, 10): self.make(slot).wait_send()
        if self.k > 0: self.line_copy().wait_send()
    def last(self):
        p, plane = self.p, self.order[self.k]
        land = self.land.at[plane]
        pltpu.make_async_remote_copy(src_ref=land, dst_ref=land, send_sem=self.line_sems.at[0, self.k], recv_sem=self.line_sems.at[1, plane], device_id=(p.sibling,), device_id_type=MESH).wait_recv()
        self.fetch(land, self.k % 2).wait()
        self.add(self.out, [self.k % 2], self.rows)

def ffn_kernel(hidden_ref, cotangent_ref, both_ref, down_ref, bias_ref,
               hidden_sum, ffn_sum, grad_both_ref, grad_down_ref, bias_grad_ref,
               held, land_core, land_dx, land_dy, land_x, land_y, land_z,
               tokens, cot, both_keep, ffn_keep, acc, outgoing, load, gather_sems, cot_sems, sum_sems, line_sems, load_sems):
    place = Place()
    width = hidden_ref.shape[1]
    pad = down_ref.shape[0]
    rows = 2 * hidden_ref.shape[0]
    order = plane_order(place.z)
    def fetch_cot(k): return pltpu.make_async_copy(cotangent_ref.at[order[k]], cot, cot_sems.at[0, k])
    def fetch_tokens(k): return pltpu.make_async_copy(held.at[order[k]], tokens, cot_sems.at[1, k])
    fetch_cot(0).start()
    place.meet()
    gather = Gather(place, hidden_ref, held, pl.ds(0, width), gather_sems)
    gather.start()
    grad_both_ref[...] = jnp.zeros_like(grad_both_ref)
    grad_down_ref[...] = jnp.zeros_like(grad_down_ref)
    bias_grad_ref[...] = jnp.zeros_like(bias_grad_ref)
    land = (land_core, land_dx, land_dy, land_x, land_y, land_z)
    sums = [[PlaneSum(place, order, kind, k, acc, outgoing, (hidden_sum, ffn_sum)[kind], land, load, sum_sems, line_sems, load_sems) for k in range(PLANES)] for kind in range(2)]

    def compute(k):
        gather.ready(k)
        fetch_tokens(k).start()
        fetch_tokens(k).wait()
        fetch_cot(k).wait()
        half = rows // 2
        @pl.loop(0, 4)
        def _(i):
            dy, dx = 1 - i % 2, 1 - i // 2
            y, x = place.y + dy * (1 - 2 * place.y), place.x + dx * (1 - 2 * place.x)
            hidden = tokens[y, x].reshape(rows, width)
            cotangent = cot[y, x].reshape(rows, width)
            both_pre = dot(hidden, both_ref[...], ((1,), (0,))) + bias_ref[0:1]
            hidden_grad = dot(cotangent, down_ref[...], ((1,), (1,)))
            activated, slope = gelu_and_slope(both_pre[:, :pad])
            up_pre = both_pre[:, pad:]
            hidden_ffn = (activated * up_pre).astype(BF16)
            both_grad = jnp.concatenate([(hidden_grad * up_pre * slope).astype(BF16), (hidden_grad * activated).astype(BF16)], axis=1)
            here = pl.ds(pl.multiple_of((y * 2 + x) * rows, rows), rows)
            both_keep[here] = both_grad
            ffn_keep[here] = hidden_ffn
            bias_grad_ref[...] += jnp.sum(both_grad.astype(F32), axis=0, keepdims=True)
            def drain():
                for kind in range(2): sums[kind][k].across(i - 2).wait_send()
            def drain_before():
                for kind in range(2): sums[kind][k - 1].across(i + 2).wait_send()
            pl.when(i >= 2)(drain)
            if k > 0: pl.when(i < 2)(drain_before)
            for kind, part in ((0, lambda: dot(both_grad, both_ref[...], ((1,), (1,)))), (1, lambda: dot(hidden_ffn, down_ref[...], ((1,), (0,))))):
                result = part().astype(BF16)
                low, high = result[:half], result[half:]
                acc[kind, k, i] = jnp.where(place.core == 0, low, high)
                outgoing[kind, i % 2] = jnp.where(place.core == 0, high, low)
                sums[kind][k].across(i).start()
        step = 512
        @pl.loop(0, width // step)
        def _(j):
            cols = pl.ds(pl.multiple_of(j * step, step), step)
            hidden = tokens[:, :, :, :, cols].reshape(4 * rows, step)
            grad_both_ref[:, cols] += dot(both_keep[...], hidden, ((0,), (0,)))
            cotangent = cot[:, :, :, :, cols].reshape(4 * rows, step)
            grad_down_ref[:, cols] += dot(ffn_keep[...], cotangent, ((0,), (0,)))
        if k + 1 < PLANES: fetch_cot(k + 1).start()

    def both(name, k):
        for kind in range(2): getattr(sums[kind][k], name)()

    gather.line(0)
    gather.line(1)
    gather.side(0)
    gather.line(2)
    gather.side(1)
    gather.diag(0)
    compute(0)
    gather.line(3)
    gather.side(2)
    gather.diag(1)
    gather.side(3)
    compute(1)
    gather.diag(2)
    gather.diag(3)
    both("stage0", 1)
    compute(2)
    both("stage1", 1)
    both("stage0", 2)
    compute(3)
    both("stage2", 1)
    both("stage1", 2)
    both("stage0", 3)
    both("stage2", 2)
    both("stage1", 3)
    both("stage0", 0)
    both("stage2", 3)
    both("stage1", 0)
    both("stage2", 0)
    for kind in range(2):
        for i in (2, 3): sums[kind][3].across(i).wait_send()
    for kind in range(2):
        for k in (1, 2, 3): sums[kind][k].last()
    for k in range(PLANES): both("sent", k)
    gather.finish()

def ffn(hidden_two, cotangent_full, both_own, both_bias, down_own, collective_id):
    tok_rows, width = hidden_two.shape
    pad = down_own.shape[0]
    full = (4, 2, 2, 2, tok_rows, width)
    upper = (tok_rows // 2 + TILE - 1) // TILE * TILE
    hbm = pl.BlockSpec(memory_space=pl.ANY)
    vmem = pl.BlockSpec(memory_space=pltpu.VMEM)
    dma = pltpu.SemaphoreType.DMA
    low = lambda *shape: jax.ShapeDtypeStruct(shape + (width,), BF16)
    outs = pl.pallas_call(
        ffn_kernel,
        out_shape=(
            jax.ShapeDtypeStruct((tok_rows, width), F32),
            jax.ShapeDtypeStruct((tok_rows, width), F32),
            jax.ShapeDtypeStruct((2 * pad, width), F32),
            jax.ShapeDtypeStruct((pad, width), F32),
            jax.ShapeDtypeStruct((8, 2 * pad), F32),
            low(4, 2, 2, 2, tok_rows),
            low(2, 4, 4, tok_rows), low(2, 4, upper), low(2, 4, tok_rows - upper),
            low(2, 4, tok_rows), low(2, 4, tok_rows), low(2, 4, tok_rows),
        ),
        in_specs=[hbm, hbm, vmem, vmem, vmem],
        out_specs=(vmem,) * 5 + (hbm,) * 7,
        scratch_shapes=[
            pltpu.VMEM(full[1:], BF16),
            pltpu.VMEM(full[1:], BF16),
            pltpu.VMEM((8 * tok_rows, 2 * pad), BF16),
            pltpu.VMEM((8 * tok_rows, pad), BF16),
            pltpu.VMEM((2, 4, 4, tok_rows, width), BF16),
            pltpu.VMEM((2, 2, tok_rows, width), BF16),
            pltpu.VMEM((2, tok_rows, width), BF16),
            dma((2, Gather.COPIES, PLANES)), dma((2, PLANES)), dma((2, PLANES, 2, PlaneSum.SLOTS)), dma((2, 2, PLANES)), dma((2,)),
        ],
        compiler_params=pltpu.CompilerParams(collective_id=collective_id, has_side_effects=True, vmem_limit_bytes=63*1024*1024),
        name="feed_forward",
    )(hidden_two, cotangent_full.reshape(full), both_own, down_own, jnp.broadcast_to(both_bias, (8, 2 * pad)))
    return outs[0], outs[1], outs[2], outs[3], outs[4][0]


def gather_rows(arrays, collective_id, name):
    if lax.axis_size(AXIS) == DEVICES:
        return gather_all(arrays, [1] * len(arrays), collective_id, name)
    return [lax.all_gather(values, AXIS, axis=0, tiled=True) for values in arrays]


def sum_rows(partial, chunk, collective_id, name):
    if lax.axis_size(AXIS) == DEVICES:
        return sum_over_devices(partial.astype(BF16), chunk, collective_id, name)
    return lax.psum_scatter(
        partial.astype(BF16), AXIS, scatter_dimension=0, tiled=True
    ).astype(F32)


def sum_products(left_a, right_a, left_b, right_b, extra):
    if lax.axis_size(AXIS) == DEVICES:
        return product_sums(left_a, right_a, left_b, right_b, extra, 640, 2, "sum_products")
    product_a = dot(left_a, right_a, ((0,), (0,)))
    product_b = dot(left_b, right_b, ((0,), (0,))).astype(BF16)
    return (
        sum_rows(product_a, None, None, None),
        sum_rows(jnp.concatenate([product_b, extra], axis=1), None, None, None),
    )


def swap(pieces):
    return lax.all_to_all(pieces, AXIS, 0, 0, tiled=False)


def feed_forward(hidden_two, cotangent_full, both_own, both_bias, down_own, rows):
    peers = lax.axis_size(AXIS)
    device = lax.axis_index(AXIS)
    tok_rows, width = hidden_two.shape
    ffn_pad = down_own.shape[0]
    own_cotangent = lax.dynamic_slice_in_dim(cotangent_full, device * rows, rows, 1)
    down_bias_share = jnp.sum(own_cotangent.astype(F32), axis=0)
    if peers == DEVICES:
        normed_grad, ffn_out, grad_both, grad_down, bias_share = ffn(
            hidden_two, cotangent_full, both_own, both_bias, down_own, 7
        )
        return normed_grad, ffn_out, grad_both.T, grad_down, bias_share, down_bias_share

    def piece(sums, here):
        hidden_own, cotangent_piece = here
        hidden_full = gather_rows([hidden_own], None, None)[0]
        both_pre = jnp.dot(hidden_full, both_own, preferred_element_type=F32) + both_bias
        activated, slope = gelu_and_slope(both_pre[:, :ffn_pad])
        up_pre = both_pre[:, ffn_pad:]
        hidden_ffn = (activated * up_pre).astype(BF16)
        hidden_grad = dot(cotangent_piece, down_own, ((1,), (1,)))
        gate_grad = (hidden_grad * up_pre * slope).astype(BF16)
        up_grad = (hidden_grad * activated).astype(BF16)
        both_grad = jnp.concatenate([gate_grad, up_grad], axis=1)
        normed_grad = sum_rows(dot(both_grad, both_own, ((1,), (1,))), None, None, None)
        ffn_out = sum_rows(
            jnp.dot(hidden_ffn, down_own, preferred_element_type=F32), None, None, None
        )
        shares = (
            dot(hidden_full, both_grad, ((0,), (0,))),
            dot(hidden_ffn, cotangent_piece, ((0,), (0,))),
            jnp.sum(both_grad.astype(F32), axis=0),
        )
        return jax.tree.map(jnp.add, sums, shares), (normed_grad, ffn_out)

    pieces = max(1, peers // DEVICES)
    cut = tok_rows // pieces
    zeros = (
        jnp.zeros((width, 2 * ffn_pad), F32),
        jnp.zeros((ffn_pad, width), F32),
        jnp.zeros((2 * ffn_pad,), F32),
    )
    cotangent_pieces = cotangent_full.reshape(peers, pieces, cut, width).transpose(1, 0, 2, 3)
    shares, outs = lax.scan(
        piece,
        zeros,
        (hidden_two.reshape(pieces, cut, width), cotangent_pieces.reshape(pieces, -1, width)),
    )
    normed_grad, ffn_out = (part.reshape(tok_rows, width) for part in outs)
    return (normed_grad, ffn_out) + shares + (down_bias_share,)


def body(
    layer_input,
    norm1_scale,
    query_weight,
    keyvalue_weight,
    out_weight,
    norm2_scale,
    gate_weight,
    gate_bias,
    up_weight,
    up_bias,
    down_weight,
    down_bias,
    out_cotangent,
):
    peers = lax.axis_size(AXIS)
    device = lax.axis_index(AXIS)
    tok_rows, width = layer_input.shape
    rows = query_weight.shape[0]
    query_cols = query_weight.shape[1]
    kv_cols = keyvalue_weight.shape[1]
    heads = query_cols // HD
    quarter = HD // 4
    query_scale = 1.0 / math.sqrt(HD)
    ffn_own = down_weight.shape[0]
    ffn_pad = round_up(ffn_own, LANES)

    vectors = jnp.stack([norm1_scale, norm2_scale, down_bias], axis=1)
    packed = jnp.concatenate(
        [query_weight, keyvalue_weight, pad_columns(vectors, LANES)], axis=1
    )
    first = gather_rows([packed], 5, "gather_weights")[0]
    proj_cols = query_cols + kv_cols
    proj_full = first[:, :proj_cols]
    gains = first[:, proj_cols:].astype(F32).T
    gain_one, gain_two, bias_down = gains[0], gains[1], gains[2]

    resid_in = layer_input.astype(F32)
    square_one = jnp.mean(resid_in * resid_in, axis=1, keepdims=True)
    scale_one = lax.rsqrt(square_one + EPSILON)
    normed_one = resid_in * scale_one
    hidden_one = (normed_one * gain_one).astype(BF16)
    projected = jnp.dot(hidden_one, proj_full, preferred_element_type=F32)
    position = device * tok_rows + jnp.arange(tok_rows, dtype=jnp.int32)
    cosine, sine_table = rotary_tables(position.astype(F32), quarter)
    queries = (
        rotate(
            projected[:, :query_cols].reshape(tok_rows, heads, HD),
            cosine[:, None, :],
            sine_table[:, None, :],
            quarter,
        )
        * query_scale
    ).astype(BF16)
    queries = queries.reshape(tok_rows, query_cols)
    keys_rot = rotate(projected[:, query_cols : query_cols + HD], cosine, sine_table, quarter)
    own_kv = jnp.concatenate([keys_rot, projected[:, query_cols + HD :]], axis=1).astype(BF16)

    reach = min((WINDOW + tok_rows - 2) // tok_rows, peers - 1)
    window_rows = (reach + 1) * tok_rows
    window_start = jnp.maximum(device - reach, 0) * tok_rows
    place = (device * tok_rows - window_start).astype(jnp.int32).reshape(1)
    if peers == DEVICES:
        out_full, cotangent_full, kv_window, attention, logs = gather_attend(
            own_kv, out_weight, out_cotangent, queries, 6
        )
    else:
        kv_full, out_full, cotangent_full = gather_rows(
            [own_kv, out_weight, out_cotangent], None, None
        )
        kv_window = lax.dynamic_slice_in_dim(kv_full, window_start, window_rows, 0)
        attention, logs = attend(place, queries, kv_window)

    residual_mid = resid_in + jnp.dot(attention, out_full, preferred_element_type=F32)
    square_two = jnp.mean(residual_mid * residual_mid, axis=1, keepdims=True)
    scale_two = lax.rsqrt(square_two + EPSILON)
    normed_two = residual_mid * scale_two
    hidden_two = (normed_two * gain_two).astype(BF16)

    gate_pieces = pad_columns(gate_weight.reshape(rows, peers, ffn_own), ffn_pad)
    up_pieces = pad_columns(up_weight.reshape(rows, peers, ffn_own), ffn_pad)
    both_own = swap(
        jnp.concatenate([gate_pieces, up_pieces], axis=2).transpose(1, 0, 2)
    ).reshape(peers * rows, 2 * ffn_pad)
    both_bias = jnp.concatenate(
        [pad_columns(gate_bias, ffn_pad), pad_columns(up_bias, ffn_pad)]
    ).astype(F32)
    down_own = jnp.pad(down_weight, ((0, ffn_pad - ffn_own), (0, 0)))

    normed_grad_two, ffn_out, grad_both, grad_down, bias_share, down_bias_share = feed_forward(
        hidden_two, cotangent_full, both_own, both_bias, down_own, rows
    )
    layer_output = (residual_mid + (ffn_out + bias_down)).astype(BF16)
    rms_values = jnp.stack(
        [jnp.sqrt(square_one[:, 0] + EPSILON), jnp.sqrt(square_two[:, 0] + EPSILON)], axis=0
    )
    grad_down = grad_down[:ffn_own]
    grad_both = swap(grad_both.astype(BF16).reshape(peers, rows, 2 * ffn_pad)).transpose(1, 0, 2)
    grad_both = grad_both.astype(F32)
    grad_gate = grad_both[:, :, :ffn_own].reshape(rows, peers * ffn_own)
    grad_up = grad_both[:, :, ffn_pad : ffn_pad + ffn_own].reshape(rows, peers * ffn_own)

    norm2_part = jnp.sum(normed_grad_two * normed_two, axis=0)
    weighted_two = normed_grad_two * gain_two
    mid_grad = out_cotangent.astype(F32) + scale_two * (
        weighted_two - normed_two * jnp.mean(weighted_two * normed_two, axis=1, keepdims=True)
    )
    mid_grad_low = mid_grad.astype(BF16)
    attention_grad = dot(mid_grad_low, out_full, ((1,), (1,))).astype(BF16)

    query_grad, kv_part = attend_back(place, queries, kv_window, logs, attention_grad)
    kv_partial = lax.dynamic_update_slice_in_dim(
        jnp.zeros((peers * tok_rows, 2 * HD), BF16), kv_part.astype(BF16), window_start, 0
    )
    kv_grad = sum_rows(kv_partial, 256, 3, "sum_grad_kv")
    query_raw_grad = (
        rotate(
            query_grad.reshape(tok_rows, heads, HD) * query_scale,
            cosine[:, None, :],
            -sine_table[:, None, :],
            quarter,
        )
        .reshape(tok_rows, query_cols)
        .astype(BF16)
    )
    key_raw_grad = rotate(kv_grad[:, :HD], cosine, -sine_table, quarter)
    kv_raw_grad = jnp.concatenate([key_raw_grad, kv_grad[:, HD:]], axis=1).astype(BF16)
    proj_grad = jnp.concatenate([query_raw_grad, kv_raw_grad], axis=1)
    normed_grad_one = dot(proj_grad, proj_full, ((1,), (1,)))
    norm1_part = jnp.sum(normed_grad_one * normed_one, axis=0)
    weighted_one = normed_grad_one * gain_one
    input_grad = (
        mid_grad
        + scale_one
        * (weighted_one - normed_one * jnp.mean(weighted_one * normed_one, axis=1, keepdims=True))
    ).astype(BF16)

    parts = pad_columns(jnp.stack([norm1_part, norm2_part], axis=1), LANES)
    grad_out, tail = sum_products(
        attention, mid_grad_low, hidden_one, proj_grad, parts.astype(BF16)
    )
    grad_proj = tail[:, :proj_cols]
    norm1_share = tail[:, proj_cols]
    norm2_share = tail[:, proj_cols + 1]
    return (
        layer_output,
        residual_mid,
        rms_values,
        input_grad,
        norm1_share,
        grad_proj[:, :query_cols],
        grad_proj[:, query_cols:],
        grad_out,
        norm2_share,
        grad_gate,
        bias_share[:ffn_own],
        grad_up,
        bias_share[ffn_pad : ffn_pad + ffn_own],
        grad_down,
        down_bias_share,
    )


def solution(mesh):
    by_rows, by_entry = P(AXIS, None), P(AXIS)
    in_specs = (
        by_rows,
        by_entry,
        by_rows,
        by_rows,
        by_rows,
        by_entry,
        by_rows,
        by_entry,
        by_rows,
        by_entry,
        by_rows,
        by_entry,
        by_rows,
    )
    out_specs = (
        by_rows,
        by_rows,
        P(None, AXIS),
        by_rows,
        by_entry,
        by_rows,
        by_rows,
        by_rows,
        by_entry,
        by_rows,
        by_entry,
        by_rows,
        by_entry,
        by_rows,
        by_entry,
    )
    return jax.shard_map(body, mesh=mesh, in_specs=in_specs, out_specs=out_specs, check_vma=False)
```

```python
import functools
import math

import jax
import jax.numpy as jnp
from jax import lax
from jax.experimental import pallas as pl
from jax.experimental.pallas import tpu as pltpu
from jax.sharding import PartitionSpec as P

HD = 256
WINDOW = 2048
EPSILON = 1e-06
NEGATIVE = -1e30
ROTARY_BASE = 10000.0
AXIS = "blk"
LANES = 128
DEVICES = 32
PAIR = 2
VMEM_BYTES = 48 * 1024 * 1024
F32 = jnp.float32
BF16 = jnp.bfloat16


def rotary_tables(positions, quarter):
    frequency = ROTARY_BASE ** (-(jnp.arange(quarter, dtype=F32) / quarter))
    angles = positions[:, None] * frequency[None, :]
    return (jnp.cos(angles), jnp.sin(angles))


def rotate(vector, cosine, sine_table, quarter):
    leading = vector[..., :quarter]
    trailing = vector[..., quarter : 2 * quarter]
    return jnp.concatenate(
        [
            leading * cosine - trailing * sine_table,
            trailing * cosine + leading * sine_table,
            vector[..., 2 * quarter :],
        ],
        axis=-1,
    )


def dot(left, right, contract):
    return lax.dot_general(left, right, (contract, ((), ())), preferred_element_type=F32)


def round_up(count, step):
    return (count + step - 1) // step * step


def pad_columns(values, columns):
    pad = [(0, 0)] * (values.ndim - 1) + [(0, columns - values.shape[-1])]
    return jnp.pad(values, pad)


def masked_scores(ahead, query_rows, keys, tok_rows):
    scores = dot(query_rows, keys, ((1,), (1,)))
    rows = lax.broadcasted_iota(jnp.int32, scores.shape, 0) % tok_rows
    columns = lax.broadcasted_iota(jnp.int32, scores.shape, 1)
    distance = rows - columns + ahead
    return jnp.where((distance >= 0) & (distance < WINDOW), scores, NEGATIVE)


def stack_heads(block):
    return jnp.concatenate([block[:, i * HD : (i + 1) * HD] for i in range(PAIR)], axis=0)


def unstack_heads(rows):
    tok_rows = rows.shape[0] // PAIR
    return jnp.concatenate([rows[i * tok_rows : (i + 1) * tok_rows] for i in range(PAIR)], axis=1)


def attend_pair(ahead, query, keys, values):
    tok_rows = query.shape[0]
    scores = masked_scores(ahead, stack_heads(query), keys, tok_rows)
    row_max = jnp.max(scores, axis=1, keepdims=True)
    probs = jnp.exp(scores - row_max)
    row_sum = jnp.sum(probs, axis=1, keepdims=True)
    probs_low = (probs * (1.0 / row_sum)).astype(BF16)
    attended = dot(probs_low, values, ((1,), (0,)))
    return unstack_heads(attended).astype(BF16), row_max + jnp.log(row_sum)


def attend_kernel(place_ref, query_ref, kv_ref, out_ref, log_ref):
    attended, logs = attend_pair(place_ref[0], query_ref[...], kv_ref[:, :HD], kv_ref[:, HD:])
    out_ref[...] = attended
    log_ref[0] = jnp.broadcast_to(logs, log_ref.shape[1:])


def attend_back_pair(ahead, query, grad, keys, values, logs):
    tok_rows = query.shape[0]
    query_rows, grad_rows = stack_heads(query), stack_heads(grad)
    scores = masked_scores(ahead, query_rows, keys, tok_rows)
    probs = jnp.exp(scores - logs)
    prob_grad = dot(grad_rows, values, ((1,), (1,)))
    delta = jnp.sum(probs * prob_grad, axis=1, keepdims=True)
    score_grad = (probs * (prob_grad - delta)).astype(BF16)
    query_grad = unstack_heads(dot(score_grad, keys, ((1,), (0,))))
    key_part = dot(score_grad, query_rows, ((0,), (0,)))
    value_part = dot(probs.astype(BF16), grad_rows, ((0,), (0,)))
    return query_grad, key_part, value_part


def attend_back_kernel(place_ref, query_ref, kv_ref, log_ref, grad_ref, query_grad_ref, kv_grad_ref):
    query_grad_ref[...], key_part, value_part = attend_back_pair(
        place_ref[0], query_ref[...], grad_ref[...], kv_ref[:, :HD], kv_ref[:, HD:], log_ref[0][:, :1]
    )

    @pl.when(pl.program_id(0) == 0)
    def _():
        kv_grad_ref[:, :HD] = key_part
        kv_grad_ref[:, HD:] = value_part

    @pl.when(pl.program_id(0) > 0)
    def _():
        kv_grad_ref[:, :HD] += key_part
        kv_grad_ref[:, HD:] += value_part


def attention_specs(tok_rows, heads, window_rows):
    place = pl.BlockSpec(memory_space=pltpu.SMEM)
    by_head = pl.BlockSpec((tok_rows, PAIR * HD), lambda i: (0, i))
    whole = pl.BlockSpec((window_rows, 2 * HD), lambda i: (0, 0))
    logs = pl.BlockSpec((1, PAIR * tok_rows, LANES), lambda i: (i, 0, 0))
    return place, by_head, whole, logs


def attend(place, queries, kv_window):
    tok_rows, features = queries.shape
    window_rows = kv_window.shape[0]
    pairs = features // HD // PAIR
    place_spec, by_head, whole, logs = attention_specs(tok_rows, features // HD, window_rows)
    work = tok_rows * features * window_rows
    return pl.pallas_call(
        attend_kernel,
        grid=(pairs,),
        out_shape=(
            jax.ShapeDtypeStruct((tok_rows, features), BF16),
            jax.ShapeDtypeStruct((pairs, PAIR * tok_rows, LANES), F32),
        ),
        in_specs=[place_spec, by_head, whole],
        out_specs=(by_head, logs),
        compiler_params=pltpu.CompilerParams(vmem_limit_bytes=VMEM_BYTES),
        cost_estimate=pl.CostEstimate(
            flops=4 * work, bytes_accessed=8 * kv_window.size, transcendentals=work // HD
        ),
        name="attend",
    )(place, queries, kv_window)


def attend_back(place, queries, kv_window, logs_in, grad):
    tok_rows, features = queries.shape
    window_rows = kv_window.shape[0]
    pairs = features // HD // PAIR
    place_spec, by_head, whole, logs = attention_specs(tok_rows, features // HD, window_rows)
    work = tok_rows * features * window_rows
    return pl.pallas_call(
        attend_back_kernel,
        grid=(pairs,),
        out_shape=(
            jax.ShapeDtypeStruct((tok_rows, features), F32),
            jax.ShapeDtypeStruct((window_rows, 2 * HD), F32),
        ),
        in_specs=[place_spec, by_head, whole, logs, by_head],
        out_specs=(by_head, whole),
        compiler_params=pltpu.CompilerParams(vmem_limit_bytes=VMEM_BYTES),
        cost_estimate=pl.CostEstimate(
            flops=10 * work, bytes_accessed=8 * kv_window.size, transcendentals=work // HD
        ),
        name="attend_back",
    )(place, queries, kv_window, logs_in, grad)


MESH=pl.DeviceIdType.MESH

class Place:
    def __init__(self):
        me = lax.axis_index(AXIS)
        self.core = me % 2
        self.x = (me // 2) % 2
        self.y = (me // 4) % 2
        self.z = me // 8
        self.sibling = self.index(self.z, self.y, self.x, 1 - self.core)
        self.next_x = self.index(self.z, self.y, 1 - self.x, self.core)
        self.next_y = self.index(self.z, 1 - self.y, self.x, self.core)
        self.plane = [self.z] + [(self.z + o) % 4 for o in (1, 2, 3)]
        self.line = [self.index(p, self.y, self.x, self.core) for p in self.plane]
    def index(self, z, y, x, core):
        return ((z * 2 + y) * 2 + x) * 2 + core
    def side(self, dy, dx):
        return (1 - self.y if dy else self.y), (1 - self.x if dx else self.x)
    def meet(self):
        barrier = pltpu.get_barrier_semaphore()
        partners = [self.sibling, self.next_x, self.next_y] + self.line[1:]
        for device in partners:
            pl.semaphore_signal(barrier, inc=1, device_id=(device,), device_id_type=MESH)
        pl.semaphore_wait(barrier, len(partners))

def send(src, dst, sems, device):
    copy = pltpu.make_async_remote_copy(src_ref=src, dst_ref=dst, send_sem=sems[0], recv_sem=sems[1], device_id=(device,), device_id_type=MESH)
    copy.start()
    return copy

TILE=16

CORNERS = ((1, 1), (0, 1), (1, 0), (0, 0))

def add_tiles(count, rows, target, parts):
    steps = rows // TILE
    @pl.loop(0, count * steps)
    def _(i):
        index, here = i // steps, pl.ds(pl.multiple_of((i % steps) * TILE, TILE), TILE)
        total = None
        for ref, first in parts:
            at = here if first == 0 else pl.ds(pl.multiple_of((i % steps) * TILE + first, TILE), TILE)
            part = ref[index, at].astype(F32)
            total = part if total is None else total + part
        ref, first = target
        at = here if first == 0 else pl.ds(pl.multiple_of((i % steps) * TILE + first, TILE), TILE)
        ref[index, at] = total.astype(BF16)

class SumBuffers:
    def __init__(self, refs):
        self.acc, self.core, self.diag_x, self.diag_y, self.x, self.y, self.z, self.sems = refs
    @staticmethod
    def shapes(rows, columns, units):
        upper = (rows // 2 + TILE - 1) // TILE * TILE
        buf = lambda *shape: pltpu.VMEM(shape + (columns,), BF16)
        return [buf(4, 4, rows), buf(4, 4, rows), buf(4, upper), buf(4, rows - upper), buf(4, rows), buf(4, rows), buf(3, rows),
                pltpu.SemaphoreType.DMA((units, 2, Sum.COPIES))]
    COUNT = 8

class Sum:
    COPIES = 14
    def __init__(self, place, bufs, unit, cols, own, other, out):
        self.p, self.b, self.unit, self.own, self.other, self.out = place, bufs, unit, own, other, out
        self.rows = bufs.acc.shape[2]
        self.upper = bufs.diag_x.shape[1]
        self.lower = self.rows - self.upper
        self.acc = bufs.acc.at[:, :, :, cols]
        self.core = bufs.core.at[:, :, :, cols]
        self.diag_x, self.diag_y = bufs.diag_x.at[:, :, cols], bufs.diag_y.at[:, :, cols]
        self.x, self.y, self.z = bufs.x.at[:, :, cols], bufs.y.at[:, :, cols], bufs.z.at[:, :, cols]
        self.copies = {}
    def push(self, slot, src, dst, device):
        sems = self.b.sems
        self.copies[slot] = send(src, dst, (sems.at[self.unit, 0, slot], sems.at[self.unit, 1, slot]), device)
    def begin(self):
        for i in range(4):
            self.push(i, self.other(i), self.core.at[i], self.p.sibling)
    def stage0(self):
        top, bottom = pl.ds(0, self.upper), pl.ds(self.upper, self.lower)
        for i in range(4):
            self.copies[i].wait_recv()
            add_tiles(4, self.rows, (self.acc.at[i], 0), [(self.own(i), 0), (self.core.at[i], 0)])
            if i == 0:
                self.push(4, self.acc.at[0, :, top], self.diag_x, self.p.next_x)
                self.push(5, self.acc.at[0, :, bottom], self.diag_y, self.p.next_y)
            if i == 1:
                self.push(6, self.acc.at[1, :, top], self.x.at[:, top], self.p.next_x)
            if i == 2:
                self.push(7, self.acc.at[2, :, bottom], self.y.at[:, bottom], self.p.next_y)
    def stage1(self):
        top, bottom = pl.ds(0, self.upper), pl.ds(self.upper, self.lower)
        self.copies[4].wait_recv()
        add_tiles(4, self.upper, (self.acc.at[2], 0), [(self.acc.at[2], 0), (self.diag_x, 0)])
        self.push(8, self.acc.at[2, :, top], self.y.at[:, top], self.p.next_y)
        self.copies[5].wait_recv()
        add_tiles(4, self.lower, (self.acc.at[1], self.upper), [(self.acc.at[1], self.upper), (self.diag_y, 0)])
        self.push(9, self.acc.at[1, :, bottom], self.x.at[:, bottom], self.p.next_x)
    def stage2(self):
        for slot in (6, 7, 8, 9):
            self.copies[slot].wait_recv()
        add_tiles(4, self.rows, (self.acc.at[3], 0), [(self.acc.at[3], 0), (self.x, 0), (self.y, 0)])
        for o in (1, 2, 3):
            self.push(9 + o, self.acc.at[3, self.p.plane[o]], self.z.at[o - 1], self.p.line[o])
    def stage3(self):
        for o in (1, 2, 3):
            self.copies[9 + o].wait_recv()
        @pl.loop(0, self.rows // TILE)
        def _(i):
            here = pl.ds(pl.multiple_of(i * TILE, TILE), TILE)
            total = self.acc[3, self.p.z, here].astype(F32)
            for o in range(3):
                total += self.z[o, here].astype(F32)
            self.out[here] = total
    def core_sent(self):
        for i in range(4): self.copies[i].wait_send()
    def finish(self):
        for slot in range(4, 13): self.copies[slot].wait_send()

def product_units(place, bufs, part, chunk, left, right, out, extra):
    rows = out.shape[0]
    wide = 8 * rows
    units = []

    def add_unit(k, first):
        slot = k % 2
        span = min(chunk, right.shape[1] - first)

        def half(i, core):
            y, x = place.side(*CORNERS[i])
            return part.at[slot, :, y, x, core]

        unit = Sum(
            place, bufs, k, pl.ds(k * chunk, chunk),
            lambda i: half(i, place.core), lambda i: half(i, 1 - place.core),
            out.at[:, pl.ds(first, chunk)],
        )

        def make():
            if k >= 2:
                units[k - 2][0].core_sent()

            @pl.loop(0, 4)
            def _(z):
                here = pl.ds(pl.multiple_of(z * wide, wide), wide)
                product = dot(left[:, here], right[:, pl.ds(first, span)], ((0,), (0,)))
                block = (2, 2, 2, rows)
                part[slot, z, :, :, :, :, pl.ds(0, span)] = product.astype(BF16).reshape(block + (span,))
                if span < chunk:
                    part[slot, z, :, :, :, :, pl.ds(span, chunk - span)] = extra[here].reshape(
                        block + (chunk - span,)
                    )

            unit.begin()

        units.append((unit, make))

    for k, first in enumerate(range(0, out.shape[1], chunk)):
        add_unit(k, first)
    return units


def product_sum_kernel(chunk, left, right, extra, out, part, *scratch):
    place = Place()
    units = product_units(place, SumBuffers(scratch), part, chunk, left, right, out, extra)
    place.meet()
    count = len(units)
    stages = [lambda k: units[k][1]()] + [
        lambda k, name=name: getattr(units[k][0], name)()
        for name in ("stage0", "stage1", "stage2", "stage3")
    ]
    for step in range(count + 4):
        for s in (1, 2, 3, 4, 0):
            if 0 <= step - s < count:
                stages[s](step - s)
    for unit, _ in units[-2:]:
        unit.core_sent()
    for unit, _ in units:
        unit.finish()


def product_sum(left, right, extra, chunk, collective_id, name):
    rows = left.shape[1] // 32
    columns = right.shape[1] + extra.shape[1]
    vmem = pl.BlockSpec(memory_space=pltpu.VMEM)
    return pl.pallas_call(
        functools.partial(product_sum_kernel, chunk),
        out_shape=jax.ShapeDtypeStruct((rows, columns), F32),
        in_specs=[vmem] * 3,
        out_specs=vmem,
        scratch_shapes=[pltpu.VMEM((2, 4, 2, 2, 2, rows, chunk), BF16)]
        + SumBuffers.shapes(rows, columns, columns // chunk),
        compiler_params=pltpu.CompilerParams(
            collective_id=collective_id, has_side_effects=True, vmem_limit_bytes=62 * 1024 * 1024
        ),
        name=name,
    )(left, right, extra)


def back_sums_kernel(
    chunk, left, right, query_ref, window, log_ref, grad_ref,
    out, query_grad_ref, kv_grad_ref, part, kv_total, kv_part, *scratch,
):
    place = Place()
    me = lax.axis_index(AXIS)
    tok_rows, features = query_ref.shape
    blocks = window.shape[0] // tok_rows
    start = jnp.maximum(me - (blocks - 1), 0)
    ahead = (me - start) * tok_rows
    units = product_units(
        place, SumBuffers(scratch[: SumBuffers.COUNT]), part, chunk, left, right, out, None
    )
    sums = [unit for unit, _ in units]

    def half(i, core):
        y, x = place.side(*CORNERS[i])
        return kv_part.at[:, y, x, core]

    kv = Sum(
        place, SumBuffers(scratch[SumBuffers.COUNT :]), 0, pl.ds(0, 2 * HD),
        lambda i: half(i, place.core), lambda i: half(i, 1 - place.core), kv_grad_ref,
    )
    place.meet()
    units[0][1]()
    units[1][1]()
    sums[0].stage0()
    sums[1].stage0()
    kv_total[...] = jnp.zeros_like(kv_total)
    kv_part[...] = jnp.zeros_like(kv_part)

    @pl.loop(0, features // (PAIR * HD))
    def _(i):
        here = pl.ds(pl.multiple_of(i * PAIR * HD, PAIR * HD), PAIR * HD)
        query_grad, key_part, value_part = attend_back_pair(
            ahead, query_ref[:, here], grad_ref[:, here], window[:, :HD], window[:, HD:],
            log_ref[i][:, :1],
        )
        query_grad_ref[:, here] = query_grad
        kv_total[:, :HD] += key_part
        kv_total[:, HD:] += value_part

    for j in range(blocks):
        block = start + j
        kv_part[block // 8, (block // 4) % 2, (block // 2) % 2, block % 2] = kv_total[
            j * tok_rows : (j + 1) * tok_rows
        ].astype(BF16)
    kv.begin()
    sums[0].stage1()
    kv.stage0()
    sums[1].stage1()
    units[2][1]()
    kv.stage1()
    sums[0].stage2()
    sums[2].stage0()
    kv.stage2()
    sums[1].stage2()
    units[3][1]()
    sums[2].stage1()
    sums[3].stage0()
    kv.stage3()
    sums[0].stage3()
    sums[2].stage2()
    sums[3].stage1()
    sums[1].stage3()
    sums[3].stage2()
    sums[2].stage3()
    sums[3].stage3()
    for unit in sums[2:] + [kv]:
        unit.core_sent()
    for unit in sums + [kv]:
        unit.finish()


def back_sums(left, right, queries, kv_window, logs, grad, collective_id):
    rows, columns = left.shape[1] // 32, right.shape[1]
    tok_rows, features = queries.shape
    chunk = columns // 4
    vmem = pl.BlockSpec(memory_space=pltpu.VMEM)
    return pl.pallas_call(
        functools.partial(back_sums_kernel, chunk),
        out_shape=(
            jax.ShapeDtypeStruct((rows, columns), F32),
            jax.ShapeDtypeStruct((tok_rows, features), F32),
            jax.ShapeDtypeStruct((tok_rows, 2 * HD), F32),
        ),
        in_specs=[vmem] * 6,
        out_specs=(vmem,) * 3,
        scratch_shapes=[
            pltpu.VMEM((2, 4, 2, 2, 2, rows, chunk), BF16),
            pltpu.VMEM(kv_window.shape, F32),
            pltpu.VMEM((4, 2, 2, 2, tok_rows, 2 * HD), BF16),
        ]
        + SumBuffers.shapes(rows, columns, 4)
        + SumBuffers.shapes(tok_rows, 2 * HD, 1),
        compiler_params=pltpu.CompilerParams(
            collective_id=collective_id, has_side_effects=True, vmem_limit_bytes=62 * 1024 * 1024
        ),
        name="back_sums",
    )(left, right, queries, kv_window, logs, grad)


PLANES=4
def plane_order(z):
    near = jnp.minimum(z, 3 - z)
    flip = z // 2
    order = []
    for k in range(4):
        swapped = 1 - k if k < 2 else k
        plane = near * swapped + (1 - near) * k
        order.append(flip * (3 - plane) + (1 - flip) * plane)
    return order

class Gather:
    COPIES = 11
    def __init__(self, place, own, held, cols, sems):
        self.place, self.held, self.cols, self.sems = place, held, cols, sems
        self.own = own.at[:, cols]
        rows = held.shape[4]
        upper = (rows // 2 + TILE - 1) // TILE * TILE
        self.halves = pl.ds(0, upper), pl.ds(upper, rows - upper)
        self.order = plane_order(place.z)
        self.sent = []
        self.kept = []
    def at(self, plane, y, x, core, part=slice(None)):
        return self.held.at[plane, y, x, core, part, self.cols]
    def pair(self, slot, k):
        return self.sems.at[0, slot, k], self.sems.at[1, slot, k]
    def push(self, src, dst, slot, k, device):
        copy = send(src, dst, self.pair(slot, k), device)
        self.sent.append(copy)
    def arrived(self, ref, slot, k):
        pltpu.make_async_remote_copy(src_ref=ref, dst_ref=ref, send_sem=self.sems.at[0, slot, k], recv_sem=self.sems.at[1, slot, k], device_id=(self.place.sibling,), device_id_type=MESH).wait_recv()
    def start(self):
        p = self.place
        mine = self.at(p.z, p.y, p.x, p.core)
        keep = pltpu.make_async_copy(self.own, mine, self.sems.at[0, 10, 0])
        keep.start()
        self.kept.append(keep)
        for k in (1, 2, 3):
            plane = self.order[k]
            copy = pltpu.make_async_remote_copy(src_ref=self.own, dst_ref=mine, send_sem=self.sems.at[0, 0, k], recv_sem=self.sems.at[1, 0, p.z], device_id=(p.index(plane, p.y, p.x, p.core),), device_id_type=MESH)
            copy.start(); self.sent.append(copy)
    def line(self, k):
        p = self.place
        plane = self.order[k]
        block = self.at(plane, p.y, p.x, p.core)
        source = self.own if k == 0 else block
        if k > 0:
            pltpu.make_async_remote_copy(src_ref=block, dst_ref=block, send_sem=self.sems.at[0, 0, k], recv_sem=self.sems.at[1, 0, plane], device_id=(p.sibling,), device_id_type=MESH).wait_recv()
        self.push(source, block, 1, k, p.next_x)
        self.push(source, block, 2, k, p.next_y)
        self.push(source, block, 5, k, p.sibling)
    def side(self, k):
        p, plane = self.place, self.order[k]
        top, bottom = self.halves
        self.arrived(self.at(plane, p.y, 1 - p.x, p.core), 1, k)
        block = self.at(plane, p.y, 1 - p.x, p.core, top)
        self.push(block, block, 4, k, p.next_y)
        block = self.at(plane, p.y, 1 - p.x, p.core)
        self.push(block, block, 6, k, p.sibling)
        self.arrived(self.at(plane, 1 - p.y, p.x, p.core), 2, k)
        block = self.at(plane, 1 - p.y, p.x, p.core, bottom)
        self.push(block, block, 3, k, p.next_x)
        block = self.at(plane, 1 - p.y, p.x, p.core)
        self.push(block, block, 7, k, p.sibling)
    def diag(self, k):
        p, plane = self.place, self.order[k]
        for slot, part in ((4, self.halves[0]), (3, self.halves[1])):
            block = self.at(plane, 1 - p.y, 1 - p.x, p.core, part)
            self.arrived(block, slot, k)
            self.push(block, block, slot + 5, k, p.sibling)
    def ready(self, k):
        p, plane = self.place, self.order[k]
        top, bottom = self.halves
        if k == 0:
            for keep in self.kept: keep.wait()
        other = 1 - p.core
        self.arrived(self.at(plane, p.y, p.x, other), 5, k)
        self.arrived(self.at(plane, p.y, 1 - p.x, other), 6, k)
        self.arrived(self.at(plane, 1 - p.y, p.x, other), 7, k)
        self.arrived(self.at(plane, 1 - p.y, 1 - p.x, other, top), 9, k)
        self.arrived(self.at(plane, 1 - p.y, 1 - p.x, other, bottom), 8, k)
    def finish(self):
        for copy in self.sent: copy.wait_send()

def pipeline(stages, count):
    for step in range(count + len(stages) - 1):
        for s in range(len(stages) - 1, -1, -1):
            if 0 <= step - s < count:
                stages[s](step - s)

def gather_kernel(chunks, *refs):
    n = len(chunks)
    ins, outs, sems = refs[:n], refs[n:2*n], refs[2*n:]
    place = Place()
    place.meet()
    items = []
    for a in range(n):
        width = ins[a].shape[1] // chunks[a]
        for j in range(chunks[a]):
            items.append(Gather(place, ins[a], outs[a], pl.ds(j * width, width), sems[a].at[j]))
    def line(s):
        if s % PLANES == 0:
            items[s // PLANES].start()
        items[s // PLANES].line(s % PLANES)
    def side(s): items[s // PLANES].side(s % PLANES)
    def diag(s): items[s // PLANES].diag(s % PLANES)
    pipeline([line, side, diag], len(items) * PLANES)
    for item in items:
        for k in range(PLANES): item.ready(k)
    for item in items: item.finish()

def gather_all(arrays, chunks, collective_id, name):
    outs = pl.pallas_call(
        functools.partial(gather_kernel, chunks),
        out_shape=tuple(jax.ShapeDtypeStruct((4,2,2,2)+a.shape, BF16) for a in arrays),
        in_specs=[pl.BlockSpec(memory_space=pl.ANY)]*len(arrays),
        out_specs=tuple(pl.BlockSpec(memory_space=pl.ANY) for _ in arrays),
        scratch_shapes=[pltpu.SemaphoreType.DMA((c, 2, Gather.COPIES, PLANES)) for c in chunks],
        compiler_params=pltpu.CompilerParams(collective_id=collective_id, has_side_effects=True),
        name=name,
    )(*arrays)
    return [o.reshape(32 * a.shape[0], a.shape[1]) for o, a in zip(outs, arrays)]


GELU_SCALE = math.sqrt(2.0 / math.pi)
GELU_CUBE = 0.044715

def gelu_and_slope(v):
    square = v * v
    t = jnp.tanh(GELU_SCALE * v * (1.0 + GELU_CUBE * square))
    half = 0.5 * (1.0 + t)
    slope = half + 0.5 * v * (1.0 - t * t) * (GELU_SCALE * (1.0 + 3.0 * GELU_CUBE * square))
    return v * half, slope

def gather_attend_kernel(
    kv_ref, weight_ref, cotangent_ref, query_ref,
    kv_held, weight_held, cotangent_held, window, out_ref, log_ref,
    kv_sems, weight_sems, cotangent_sems, load_sems,
):
    place = Place()
    me = lax.axis_index(AXIS)
    tok_rows, features = query_ref.shape
    blocks = window.shape[0] // tok_rows
    start = jnp.maximum(me - (blocks - 1), 0)
    place.meet()

    def item(own, held, sems):
        return Gather(place, own, held, pl.ds(0, own.shape[1]), sems)

    kv = item(kv_ref, kv_held, kv_sems)
    weight = item(weight_ref, weight_held, weight_sems)
    cotangent = item(cotangent_ref, cotangent_held, cotangent_sems)
    for one in (kv, weight, cotangent):
        one.start()

    def run(*steps):
        for one, name, k in steps:
            getattr(one, name)(k)

    run(
        (kv, "line", 0), (weight, "line", 0), (kv, "line", 1), (kv, "side", 0),
        (kv, "line", 2), (kv, "side", 1), (kv, "diag", 0), (kv, "line", 3),
        (kv, "side", 2), (kv, "diag", 1), (kv, "side", 3), (kv, "diag", 2), (kv, "diag", 3),
        (weight, "line", 1), (cotangent, "line", 0), (weight, "side", 0), (weight, "line", 2),
        (weight, "side", 1), (weight, "diag", 0), (weight, "line", 3), (cotangent, "line", 1),
        (kv, "ready", 0), (kv, "ready", 1), (kv, "ready", 2), (kv, "ready", 3),
    )
    loads = []
    for j in range(blocks):
        block = start + j
        load = pltpu.make_async_copy(
            kv_held.at[block // 8, (block // 4) % 2, (block // 2) % 2, block % 2],
            window.at[pl.ds(j * tok_rows, tok_rows)],
            load_sems.at[j],
        )
        load.start()
        loads.append(load)
    for load in loads:
        load.wait()
    run((weight, "side", 2), (weight, "diag", 1))
    ahead = (me - start) * tok_rows

    @pl.loop(0, features // (PAIR * HD))
    def _(i):
        here = pl.ds(pl.multiple_of(i * PAIR * HD, PAIR * HD), PAIR * HD)
        attended, logs = attend_pair(ahead, query_ref[:, here], window[:, :HD], window[:, HD:])
        out_ref[:, here] = attended
        log_ref[i] = jnp.broadcast_to(logs, log_ref.shape[1:])

    run(
        (cotangent, "side", 0), (weight, "side", 3), (weight, "diag", 2), (cotangent, "line", 2),
        (weight, "diag", 3), (cotangent, "side", 1), (cotangent, "diag", 0),
        (cotangent, "line", 3), (cotangent, "side", 2), (cotangent, "diag", 1),
        (cotangent, "side", 3), (cotangent, "diag", 2), (cotangent, "diag", 3),
    )
    for one in (weight, cotangent):
        for k in range(PLANES):
            one.ready(k)
    for one in (kv, weight, cotangent):
        one.finish()


def gather_attend(own_kv, out_weight, out_cotangent, queries, collective_id):
    tok_rows, features = queries.shape
    blocks = (WINDOW + tok_rows - 2) // tok_rows + 1
    pairs = features // HD // PAIR
    arrays = (own_kv, out_weight, out_cotangent)
    hbm = pl.BlockSpec(memory_space=pl.ANY)
    vmem = pl.BlockSpec(memory_space=pltpu.VMEM)
    outs = pl.pallas_call(
        gather_attend_kernel,
        out_shape=tuple(jax.ShapeDtypeStruct((4, 2, 2, 2) + a.shape, BF16) for a in arrays)
        + (
            jax.ShapeDtypeStruct((blocks * tok_rows, own_kv.shape[1]), BF16),
            jax.ShapeDtypeStruct((tok_rows, features), BF16),
            jax.ShapeDtypeStruct((pairs, PAIR * tok_rows, LANES), F32),
        ),
        in_specs=[hbm] * 3 + [vmem],
        out_specs=(hbm,) * 3 + (vmem,) * 3,
        scratch_shapes=[pltpu.SemaphoreType.DMA((2, Gather.COPIES, PLANES)) for _ in arrays]
        + [pltpu.SemaphoreType.DMA((blocks,))],
        compiler_params=pltpu.CompilerParams(
            collective_id=collective_id, has_side_effects=True, vmem_limit_bytes=VMEM_BYTES
        ),
        name="gather_attend",
    )(*arrays, queries)
    full = [o.reshape(32 * a.shape[0], a.shape[1]) for o, a in zip(outs[1:3], arrays[1:])]
    return full[0], full[1], outs[3], outs[4], outs[5]


class PlaneSum:
    SLOTS = 10
    def __init__(self, place, order, kind, k, acc, outgoing, out, land, load, sems, line_sems, load_sems):
        self.p, self.k, self.order = place, k, order
        self.acc, self.outgoing = acc.at[kind, k], outgoing.at[kind]
        self.out = out
        core, diag_x, diag_y, side_x, side_y, line = land
        self.core, self.side_x, self.side_y = core.at[kind, k], side_x.at[kind, k], side_y.at[kind, k]
        self.diag_x, self.diag_y, self.land = diag_x.at[kind, k], diag_y.at[kind, k], line.at[kind]
        self.load, self.load_sems = load, load_sems
        self.sems, self.line_sems = sems.at[kind, k], line_sems.at[kind]
        self.rows = self.acc.shape[1]
        self.upper = self.diag_x.shape[0]
        self.top, self.bottom = pl.ds(0, self.upper), pl.ds(self.upper, self.rows - self.upper)
    def mine(self, i): return self.acc.at[i]
    def copy(self, src, dst, slot, device):
        return pltpu.make_async_remote_copy(src_ref=src, dst_ref=dst, send_sem=self.sems.at[0, slot], recv_sem=self.sems.at[1, slot], device_id=(device,), device_id_type=MESH)
    def across(self, i):
        return self.copy(self.outgoing.at[i % 2], self.core.at[i], i, self.p.sibling)
    def make(self, slot):
        p, mine = self.p, self.mine
        src, dst, device = {
            4: (mine(0).at[self.top], self.diag_x, p.next_x),
            5: (mine(0).at[self.bottom], self.diag_y, p.next_y),
            6: (mine(1).at[self.top], self.side_x.at[self.top], p.next_x),
            7: (mine(2).at[self.bottom], self.side_y.at[self.bottom], p.next_y),
            8: (mine(2).at[self.top], self.side_y.at[self.top], p.next_y),
            9: (mine(1).at[self.bottom], self.side_x.at[self.bottom], p.next_x),
        }[slot]
        return self.copy(src, dst, slot, device)
    def line_copy(self):
        p, plane = self.p, self.order[self.k]
        return pltpu.make_async_remote_copy(src_ref=self.mine(3), dst_ref=self.land.at[p.z], send_sem=self.line_sems.at[0, self.k], recv_sem=self.line_sems.at[1, p.z], device_id=(p.index(plane, p.y, p.x, p.core),), device_id_type=MESH)
    def fetch(self, src, slot):
        rows = src.shape[0]
        copy = pltpu.make_async_copy(src, self.load.at[slot, pl.ds(0, rows)], self.load_sems.at[slot])
        copy.start()
        return copy
    def add(self, target, slots, rows):
        @pl.loop(0, rows // TILE)
        def _(i):
            here = pl.ds(pl.multiple_of(i * TILE, TILE), TILE)
            total = target[here].astype(F32)
            for slot in slots: total += self.load[slot, here].astype(F32)
            target[here] = total.astype(target.dtype)
    def stage0(self):
        self.across(0).wait_recv()
        fetched = self.fetch(self.core.at[0], 0)
        for i in range(4):
            current = fetched
            if i < 3:
                self.across(i + 1).wait_recv()
                fetched = self.fetch(self.core.at[i + 1], (i + 1) % 2)
            current.wait()
            self.add(self.mine(i), [i % 2], self.rows)
            for slot in ((4, 5), (6,), (7,), ())[i]:
                self.make(slot).start()
    def stage1(self):
        self.make(4).wait_recv()
        self.fetch(self.diag_x, 0).wait()
        self.add(self.mine(2).at[self.top], [0], self.upper)
        self.make(8).start()
        self.make(5).wait_recv()
        self.fetch(self.diag_y, 1).wait()
        self.add(self.mine(1).at[self.bottom], [1], self.rows - self.upper)
        self.make(9).start()
    def stage2(self):
        for slot in (6, 9): self.make(slot).wait_recv()
        first = self.fetch(self.side_x, 0)
        for slot in (7, 8): self.make(slot).wait_recv()
        second = self.fetch(self.side_y, 1)
        first.wait(); second.wait()
        if self.k > 0:
            self.add(self.mine(3), [0, 1], self.rows)
            self.line_copy().start()
        else:
            mine, out = self.mine(3), self.out
            @pl.loop(0, self.rows // TILE)
            def _(i):
                here = pl.ds(pl.multiple_of(i * TILE, TILE), TILE)
                out[here] = mine[here].astype(F32) + self.load[0, here].astype(F32) + self.load[1, here].astype(F32)
    def sent(self):
        for slot in range(4, 10): self.make(slot).wait_send()
        if self.k > 0: self.line_copy().wait_send()
    def last(self):
        p, plane = self.p, self.order[self.k]
        land = self.land.at[plane]
        pltpu.make_async_remote_copy(src_ref=land, dst_ref=land, send_sem=self.line_sems.at[0, self.k], recv_sem=self.line_sems.at[1, plane], device_id=(p.sibling,), device_id_type=MESH).wait_recv()
        self.fetch(land, self.k % 2).wait()
        self.add(self.out, [self.k % 2], self.rows)

def ffn_kernel(hidden_ref, cotangent_ref, both_ref, down_ref, bias_ref,
               hidden_sum, ffn_sum, grad_both_ref, grad_down_ref, bias_grad_ref,
               held, land_core, land_dx, land_dy, land_x, land_y, land_z,
               tokens, cot, both_keep, ffn_keep, acc, outgoing, load, gather_sems, cot_sems, sum_sems, line_sems, load_sems):
    place = Place()
    width = hidden_ref.shape[1]
    pad = down_ref.shape[0]
    rows = 2 * hidden_ref.shape[0]
    order = plane_order(place.z)
    def fetch_cot(k): return pltpu.make_async_copy(cotangent_ref.at[order[k]], cot, cot_sems.at[0, k])
    def fetch_tokens(k): return pltpu.make_async_copy(held.at[order[k]], tokens, cot_sems.at[1, k])
    fetch_cot(0).start()
    place.meet()
    gather = Gather(place, hidden_ref, held, pl.ds(0, width), gather_sems)
    gather.start()
    grad_both_ref[...] = jnp.zeros_like(grad_both_ref)
    grad_down_ref[...] = jnp.zeros_like(grad_down_ref)
    bias_grad_ref[...] = jnp.zeros_like(bias_grad_ref)
    land = (land_core, land_dx, land_dy, land_x, land_y, land_z)
    sums = [[PlaneSum(place, order, kind, k, acc, outgoing, (hidden_sum, ffn_sum)[kind], land, load, sum_sems, line_sems, load_sems) for k in range(PLANES)] for kind in range(2)]

    def compute(k):
        gather.ready(k)
        fetch_tokens(k).start()
        fetch_tokens(k).wait()
        fetch_cot(k).wait()
        half = rows // 2
        @pl.loop(0, 4)
        def _(i):
            dy, dx = 1 - i % 2, 1 - i // 2
            y, x = place.y + dy * (1 - 2 * place.y), place.x + dx * (1 - 2 * place.x)
            hidden = tokens[y, x].reshape(rows, width)
            cotangent = cot[y, x].reshape(rows, width)
            both_pre = dot(hidden, both_ref[...], ((1,), (0,))) + bias_ref[0:1]
            hidden_grad = dot(cotangent, down_ref[...], ((1,), (1,)))
            activated, slope = gelu_and_slope(both_pre[:, :pad])
            up_pre = both_pre[:, pad:]
            hidden_ffn = (activated * up_pre).astype(BF16)
            both_grad = jnp.concatenate([(hidden_grad * up_pre * slope).astype(BF16), (hidden_grad * activated).astype(BF16)], axis=1)
            here = pl.ds(pl.multiple_of((y * 2 + x) * rows, rows), rows)
            both_keep[here] = both_grad
            ffn_keep[here] = hidden_ffn
            bias_grad_ref[...] += jnp.sum(both_grad.astype(F32), axis=0, keepdims=True)
            def drain():
                for kind in range(2): sums[kind][k].across(i - 2).wait_send()
            def drain_before():
                for kind in range(2): sums[kind][k - 1].across(i + 2).wait_send()
            pl.when(i >= 2)(drain)
            if k > 0: pl.when(i < 2)(drain_before)
            for kind, part in ((0, lambda: dot(both_grad, both_ref[...], ((1,), (1,)))), (1, lambda: dot(hidden_ffn, down_ref[...], ((1,), (0,))))):
                result = part().astype(BF16)
                low, high = result[:half], result[half:]
                acc[kind, k, i] = jnp.where(place.core == 0, low, high)
                outgoing[kind, i % 2] = jnp.where(place.core == 0, high, low)
                sums[kind][k].across(i).start()
        step = 512
        @pl.loop(0, width // step)
        def _(j):
            cols = pl.ds(pl.multiple_of(j * step, step), step)
            hidden = tokens[:, :, :, :, cols].reshape(4 * rows, step)
            grad_both_ref[:, cols] += dot(both_keep[...], hidden, ((0,), (0,)))
            cotangent = cot[:, :, :, :, cols].reshape(4 * rows, step)
            grad_down_ref[:, cols] += dot(ffn_keep[...], cotangent, ((0,), (0,)))
        if k + 1 < PLANES: fetch_cot(k + 1).start()

    def both(name, k):
        for kind in range(2): getattr(sums[kind][k], name)()

    gather.line(0)
    gather.line(1)
    gather.side(0)
    gather.line(2)
    gather.side(1)
    gather.diag(0)
    compute(0)
    gather.line(3)
    gather.side(2)
    gather.diag(1)
    gather.side(3)
    compute(1)
    gather.diag(2)
    gather.diag(3)
    both("stage0", 1)
    compute(2)
    both("stage1", 1)
    both("stage0", 2)
    compute(3)
    both("stage2", 1)
    both("stage1", 2)
    both("stage0", 3)
    both("stage2", 2)
    both("stage1", 3)
    both("stage0", 0)
    both("stage2", 3)
    both("stage1", 0)
    both("stage2", 0)
    for kind in range(2):
        for i in (2, 3): sums[kind][3].across(i).wait_send()
    for kind in range(2):
        for k in (1, 2, 3): sums[kind][k].last()
    for k in range(PLANES): both("sent", k)
    gather.finish()

def ffn(hidden_two, cotangent_full, both_own, both_bias, down_own, collective_id):
    tok_rows, width = hidden_two.shape
    pad = down_own.shape[0]
    full = (4, 2, 2, 2, tok_rows, width)
    upper = (tok_rows // 2 + TILE - 1) // TILE * TILE
    hbm = pl.BlockSpec(memory_space=pl.ANY)
    vmem = pl.BlockSpec(memory_space=pltpu.VMEM)
    dma = pltpu.SemaphoreType.DMA
    low = lambda *shape: jax.ShapeDtypeStruct(shape + (width,), BF16)
    outs = pl.pallas_call(
        ffn_kernel,
        out_shape=(
            jax.ShapeDtypeStruct((tok_rows, width), F32),
            jax.ShapeDtypeStruct((tok_rows, width), F32),
            jax.ShapeDtypeStruct((2 * pad, width), F32),
            jax.ShapeDtypeStruct((pad, width), F32),
            jax.ShapeDtypeStruct((8, 2 * pad), F32),
            low(4, 2, 2, 2, tok_rows),
            low(2, 4, 4, tok_rows), low(2, 4, upper), low(2, 4, tok_rows - upper),
            low(2, 4, tok_rows), low(2, 4, tok_rows), low(2, 4, tok_rows),
        ),
        in_specs=[hbm, hbm, vmem, vmem, vmem],
        out_specs=(vmem,) * 5 + (hbm,) * 7,
        scratch_shapes=[
            pltpu.VMEM(full[1:], BF16),
            pltpu.VMEM(full[1:], BF16),
            pltpu.VMEM((8 * tok_rows, 2 * pad), BF16),
            pltpu.VMEM((8 * tok_rows, pad), BF16),
            pltpu.VMEM((2, 4, 4, tok_rows, width), BF16),
            pltpu.VMEM((2, 2, tok_rows, width), BF16),
            pltpu.VMEM((2, tok_rows, width), BF16),
            dma((2, Gather.COPIES, PLANES)), dma((2, PLANES)), dma((2, PLANES, 2, PlaneSum.SLOTS)), dma((2, 2, PLANES)), dma((2,)),
        ],
        compiler_params=pltpu.CompilerParams(collective_id=collective_id, has_side_effects=True, vmem_limit_bytes=63*1024*1024),
        name="feed_forward",
    )(hidden_two, cotangent_full.reshape(full), both_own, down_own, jnp.broadcast_to(both_bias, (8, 2 * pad)))
    return outs[0], outs[1], outs[2], outs[3], outs[4][0]


def gather_rows(arrays, collective_id, name):
    if lax.axis_size(AXIS) == DEVICES:
        return gather_all(arrays, [1] * len(arrays), collective_id, name)
    return [lax.all_gather(values, AXIS, axis=0, tiled=True) for values in arrays]


def sum_rows(partial):
    return lax.psum_scatter(
        partial.astype(BF16), AXIS, scatter_dimension=0, tiled=True
    ).astype(F32)


def swap(pieces):
    return lax.all_to_all(pieces, AXIS, 0, 0, tiled=False)


def feed_forward(hidden_two, cotangent_full, both_own, both_bias, down_own, rows):
    peers = lax.axis_size(AXIS)
    device = lax.axis_index(AXIS)
    tok_rows, width = hidden_two.shape
    ffn_pad = down_own.shape[0]
    own_cotangent = lax.dynamic_slice_in_dim(cotangent_full, device * rows, rows, 1)
    down_bias_share = jnp.sum(own_cotangent.astype(F32), axis=0)
    if peers == DEVICES:
        normed_grad, ffn_out, grad_both, grad_down, bias_share = ffn(
            hidden_two, cotangent_full, both_own, both_bias, down_own, 7
        )
        return normed_grad, ffn_out, grad_both.T, grad_down, bias_share, down_bias_share

    def piece(sums, here):
        hidden_own, cotangent_piece = here
        hidden_full = gather_rows([hidden_own], None, None)[0]
        both_pre = jnp.dot(hidden_full, both_own, preferred_element_type=F32) + both_bias
        activated, slope = gelu_and_slope(both_pre[:, :ffn_pad])
        up_pre = both_pre[:, ffn_pad:]
        hidden_ffn = (activated * up_pre).astype(BF16)
        hidden_grad = dot(cotangent_piece, down_own, ((1,), (1,)))
        gate_grad = (hidden_grad * up_pre * slope).astype(BF16)
        up_grad = (hidden_grad * activated).astype(BF16)
        both_grad = jnp.concatenate([gate_grad, up_grad], axis=1)
        normed_grad = sum_rows(dot(both_grad, both_own, ((1,), (1,))))
        ffn_out = sum_rows(jnp.dot(hidden_ffn, down_own, preferred_element_type=F32))
        shares = (
            dot(hidden_full, both_grad, ((0,), (0,))),
            dot(hidden_ffn, cotangent_piece, ((0,), (0,))),
            jnp.sum(both_grad.astype(F32), axis=0),
        )
        return jax.tree.map(jnp.add, sums, shares), (normed_grad, ffn_out)

    pieces = max(1, peers // DEVICES)
    cut = tok_rows // pieces
    zeros = (
        jnp.zeros((width, 2 * ffn_pad), F32),
        jnp.zeros((ffn_pad, width), F32),
        jnp.zeros((2 * ffn_pad,), F32),
    )
    cotangent_pieces = cotangent_full.reshape(peers, pieces, cut, width).transpose(1, 0, 2, 3)
    shares, outs = lax.scan(
        piece,
        zeros,
        (hidden_two.reshape(pieces, cut, width), cotangent_pieces.reshape(pieces, -1, width)),
    )
    normed_grad, ffn_out = (part.reshape(tok_rows, width) for part in outs)
    return (normed_grad, ffn_out) + shares + (down_bias_share,)


def body(
    layer_input,
    norm1_scale,
    query_weight,
    keyvalue_weight,
    out_weight,
    norm2_scale,
    gate_weight,
    gate_bias,
    up_weight,
    up_bias,
    down_weight,
    down_bias,
    out_cotangent,
):
    peers = lax.axis_size(AXIS)
    device = lax.axis_index(AXIS)
    tok_rows, width = layer_input.shape
    rows = query_weight.shape[0]
    query_cols = query_weight.shape[1]
    kv_cols = keyvalue_weight.shape[1]
    heads = query_cols // HD
    quarter = HD // 4
    query_scale = 1.0 / math.sqrt(HD)
    ffn_own = down_weight.shape[0]
    ffn_pad = round_up(ffn_own, LANES)

    vectors = jnp.stack([norm1_scale, norm2_scale, down_bias], axis=1)
    packed = jnp.concatenate(
        [query_weight, keyvalue_weight, pad_columns(vectors, LANES)], axis=1
    )
    first = gather_rows([packed], 5, "gather_weights")[0]
    proj_cols = query_cols + kv_cols
    proj_full = first[:, :proj_cols]
    gains = first[:, proj_cols:].astype(F32).T
    gain_one, gain_two, bias_down = gains[0], gains[1], gains[2]

    resid_in = layer_input.astype(F32)
    square_one = jnp.mean(resid_in * resid_in, axis=1, keepdims=True)
    scale_one = lax.rsqrt(square_one + EPSILON)
    normed_one = resid_in * scale_one
    hidden_one = (normed_one * gain_one).astype(BF16)
    projected = jnp.dot(hidden_one, proj_full, preferred_element_type=F32)
    position = device * tok_rows + jnp.arange(tok_rows, dtype=jnp.int32)
    cosine, sine_table = rotary_tables(position.astype(F32), quarter)
    queries = (
        rotate(
            projected[:, :query_cols].reshape(tok_rows, heads, HD),
            cosine[:, None, :],
            sine_table[:, None, :],
            quarter,
        )
        * query_scale
    ).astype(BF16)
    queries = queries.reshape(tok_rows, query_cols)
    keys_rot = rotate(projected[:, query_cols : query_cols + HD], cosine, sine_table, quarter)
    own_kv = jnp.concatenate([keys_rot, projected[:, query_cols + HD :]], axis=1).astype(BF16)

    reach = min((WINDOW + tok_rows - 2) // tok_rows, peers - 1)
    window_rows = (reach + 1) * tok_rows
    window_start = jnp.maximum(device - reach, 0) * tok_rows
    place = (device * tok_rows - window_start).astype(jnp.int32).reshape(1)
    if peers == DEVICES:
        out_full, cotangent_full, kv_window, attention, logs = gather_attend(
            own_kv, out_weight, out_cotangent, queries, 6
        )
    else:
        kv_full, out_full, cotangent_full = gather_rows(
            [own_kv, out_weight, out_cotangent], None, None
        )
        kv_window = lax.dynamic_slice_in_dim(kv_full, window_start, window_rows, 0)
        attention, logs = attend(place, queries, kv_window)

    residual_mid = resid_in + jnp.dot(attention, out_full, preferred_element_type=F32)
    square_two = jnp.mean(residual_mid * residual_mid, axis=1, keepdims=True)
    scale_two = lax.rsqrt(square_two + EPSILON)
    normed_two = residual_mid * scale_two
    hidden_two = (normed_two * gain_two).astype(BF16)

    gate_pieces = pad_columns(gate_weight.reshape(rows, peers, ffn_own), ffn_pad)
    up_pieces = pad_columns(up_weight.reshape(rows, peers, ffn_own), ffn_pad)
    both_own = swap(
        jnp.concatenate([gate_pieces, up_pieces], axis=2).transpose(1, 0, 2)
    ).reshape(peers * rows, 2 * ffn_pad)
    both_bias = jnp.concatenate(
        [pad_columns(gate_bias, ffn_pad), pad_columns(up_bias, ffn_pad)]
    ).astype(F32)
    down_own = jnp.pad(down_weight, ((0, ffn_pad - ffn_own), (0, 0)))

    normed_grad_two, ffn_out, grad_both, grad_down, bias_share, down_bias_share = feed_forward(
        hidden_two, cotangent_full, both_own, both_bias, down_own, rows
    )
    layer_output = (residual_mid + (ffn_out + bias_down)).astype(BF16)
    rms_values = jnp.stack(
        [jnp.sqrt(square_one[:, 0] + EPSILON), jnp.sqrt(square_two[:, 0] + EPSILON)], axis=0
    )
    grad_down = grad_down[:ffn_own]
    grad_both = swap(grad_both.astype(BF16).reshape(peers, rows, 2 * ffn_pad)).transpose(1, 0, 2)
    grad_both = grad_both.astype(F32)
    grad_gate = grad_both[:, :, :ffn_own].reshape(rows, peers * ffn_own)
    grad_up = grad_both[:, :, ffn_pad : ffn_pad + ffn_own].reshape(rows, peers * ffn_own)

    norm2_part = jnp.sum(normed_grad_two * normed_two, axis=0)
    weighted_two = normed_grad_two * gain_two
    mid_grad = out_cotangent.astype(F32) + scale_two * (
        weighted_two - normed_two * jnp.mean(weighted_two * normed_two, axis=1, keepdims=True)
    )
    mid_grad_low = mid_grad.astype(BF16)
    attention_grad = dot(mid_grad_low, out_full, ((1,), (1,))).astype(BF16)

    if peers == DEVICES:
        grad_out, query_grad, kv_grad = back_sums(
            attention, mid_grad_low, queries, kv_window, logs, attention_grad, 3
        )
    else:
        grad_out = sum_rows(dot(attention, mid_grad_low, ((0,), (0,))))
        query_grad, kv_part = attend_back(place, queries, kv_window, logs, attention_grad)
        kv_grad = sum_rows(
            lax.dynamic_update_slice_in_dim(
                jnp.zeros((peers * tok_rows, 2 * HD), BF16), kv_part.astype(BF16), window_start, 0
            )
        )
    query_raw_grad = (
        rotate(
            query_grad.reshape(tok_rows, heads, HD) * query_scale,
            cosine[:, None, :],
            -sine_table[:, None, :],
            quarter,
        )
        .reshape(tok_rows, query_cols)
        .astype(BF16)
    )
    key_raw_grad = rotate(kv_grad[:, :HD], cosine, -sine_table, quarter)
    kv_raw_grad = jnp.concatenate([key_raw_grad, kv_grad[:, HD:]], axis=1).astype(BF16)
    proj_grad = jnp.concatenate([query_raw_grad, kv_raw_grad], axis=1)
    normed_grad_one = dot(proj_grad, proj_full, ((1,), (1,)))
    norm1_part = jnp.sum(normed_grad_one * normed_one, axis=0)
    weighted_one = normed_grad_one * gain_one
    input_grad = (
        mid_grad
        + scale_one
        * (weighted_one - normed_one * jnp.mean(weighted_one * normed_one, axis=1, keepdims=True))
    ).astype(BF16)

    parts = pad_columns(jnp.stack([norm1_part, norm2_part], axis=1), LANES)
    if peers == DEVICES:
        tail = product_sum(hidden_one, proj_grad, parts.astype(BF16), 640, 2, "sum_projections")
    else:
        tail = sum_rows(
            jnp.concatenate(
                [dot(hidden_one, proj_grad, ((0,), (0,))).astype(BF16), parts.astype(BF16)], axis=1
            )
        )
    grad_proj = tail[:, :proj_cols]
    norm1_share = tail[:, proj_cols]
    norm2_share = tail[:, proj_cols + 1]
    return (
        layer_output,
        residual_mid,
        rms_values,
        input_grad,
        norm1_share,
        grad_proj[:, :query_cols],
        grad_proj[:, query_cols:],
        grad_out,
        norm2_share,
        grad_gate,
        bias_share[:ffn_own],
        grad_up,
        bias_share[ffn_pad : ffn_pad + ffn_own],
        grad_down,
        down_bias_share,
    )


def solution(mesh):
    by_rows, by_entry = P(AXIS, None), P(AXIS)
    in_specs = (
        by_rows,
        by_entry,
        by_rows,
        by_rows,
        by_rows,
        by_entry,
        by_rows,
        by_entry,
        by_rows,
        by_entry,
        by_rows,
        by_entry,
        by_rows,
    )
    out_specs = (
        by_rows,
        by_rows,
        P(None, AXIS),
        by_rows,
        by_entry,
        by_rows,
        by_rows,
        by_rows,
        by_entry,
        by_rows,
        by_entry,
        by_rows,
        by_entry,
        by_rows,
        by_entry,
    )
    return jax.shard_map(body, mesh=mesh, in_specs=in_specs, out_specs=out_specs, check_vma=False)
```

```python
import functools
import math

import jax
import jax.numpy as jnp
from jax import lax
from jax.experimental import pallas as pl
from jax.experimental.pallas import tpu as pltpu
from jax.sharding import PartitionSpec as P

HD = 256
WINDOW = 2048
EPSILON = 1e-06
NEGATIVE = -1e30
ROTARY_BASE = 10000.0
AXIS = "blk"
LANES = 128
DEVICES = 32
PAIR = 2
VMEM_BYTES = 48 * 1024 * 1024
F32 = jnp.float32
BF16 = jnp.bfloat16


def rotary_tables(positions, quarter):
    frequency = ROTARY_BASE ** (-(jnp.arange(quarter, dtype=F32) / quarter))
    angles = positions[:, None] * frequency[None, :]
    return (jnp.cos(angles), jnp.sin(angles))


def rotate(vector, cosine, sine_table, quarter):
    leading = vector[..., :quarter]
    trailing = vector[..., quarter : 2 * quarter]
    return jnp.concatenate(
        [
            leading * cosine - trailing * sine_table,
            trailing * cosine + leading * sine_table,
            vector[..., 2 * quarter :],
        ],
        axis=-1,
    )


def dot(left, right, contract):
    return lax.dot_general(left, right, (contract, ((), ())), preferred_element_type=F32)


def round_up(count, step):
    return (count + step - 1) // step * step


def pad_columns(values, columns):
    pad = [(0, 0)] * (values.ndim - 1) + [(0, columns - values.shape[-1])]
    return jnp.pad(values, pad)


def masked_scores(ahead, query_rows, keys, tok_rows):
    scores = dot(query_rows, keys, ((1,), (1,)))
    rows = lax.broadcasted_iota(jnp.int32, scores.shape, 0) % tok_rows
    columns = lax.broadcasted_iota(jnp.int32, scores.shape, 1)
    distance = rows - columns + ahead
    return jnp.where((distance >= 0) & (distance < WINDOW), scores, NEGATIVE)


def stack_heads(block):
    return jnp.concatenate([block[:, i * HD : (i + 1) * HD] for i in range(PAIR)], axis=0)


def unstack_heads(rows):
    tok_rows = rows.shape[0] // PAIR
    return jnp.concatenate([rows[i * tok_rows : (i + 1) * tok_rows] for i in range(PAIR)], axis=1)


def attend_pair(ahead, query, keys, values):
    tok_rows = query.shape[0]
    scores = masked_scores(ahead, stack_heads(query), keys, tok_rows)
    row_max = jnp.max(scores, axis=1, keepdims=True)
    probs = jnp.exp(scores - row_max)
    row_sum = jnp.sum(probs, axis=1, keepdims=True)
    probs_low = (probs * (1.0 / row_sum)).astype(BF16)
    attended = dot(probs_low, values, ((1,), (0,)))
    return unstack_heads(attended).astype(BF16), row_max + jnp.log(row_sum)


def attend_kernel(place_ref, query_ref, kv_ref, out_ref, log_ref):
    attended, logs = attend_pair(place_ref[0], query_ref[...], kv_ref[:, :HD], kv_ref[:, HD:])
    out_ref[...] = attended
    log_ref[0] = jnp.broadcast_to(logs, log_ref.shape[1:])


def attend_back_pair(ahead, query, grad, keys, values, logs):
    tok_rows = query.shape[0]
    query_rows, grad_rows = stack_heads(query), stack_heads(grad)
    scores = masked_scores(ahead, query_rows, keys, tok_rows)
    probs = jnp.exp(scores - logs)
    prob_grad = dot(grad_rows, values, ((1,), (1,)))
    delta = jnp.sum(probs * prob_grad, axis=1, keepdims=True)
    score_grad = (probs * (prob_grad - delta)).astype(BF16)
    query_grad = unstack_heads(dot(score_grad, keys, ((1,), (0,))))
    key_part = dot(score_grad, query_rows, ((0,), (0,)))
    value_part = dot(probs.astype(BF16), grad_rows, ((0,), (0,)))
    return query_grad, key_part, value_part


def attend_back_kernel(place_ref, query_ref, kv_ref, log_ref, grad_ref, query_grad_ref, kv_grad_ref):
    query_grad_ref[...], key_part, value_part = attend_back_pair(
        place_ref[0], query_ref[...], grad_ref[...], kv_ref[:, :HD], kv_ref[:, HD:], log_ref[0][:, :1]
    )

    @pl.when(pl.program_id(0) == 0)
    def _():
        kv_grad_ref[:, :HD] = key_part
        kv_grad_ref[:, HD:] = value_part

    @pl.when(pl.program_id(0) > 0)
    def _():
        kv_grad_ref[:, :HD] += key_part
        kv_grad_ref[:, HD:] += value_part


def attention_specs(tok_rows, heads, window_rows):
    place = pl.BlockSpec(memory_space=pltpu.SMEM)
    by_head = pl.BlockSpec((tok_rows, PAIR * HD), lambda i: (0, i))
    whole = pl.BlockSpec((window_rows, 2 * HD), lambda i: (0, 0))
    logs = pl.BlockSpec((1, PAIR * tok_rows, LANES), lambda i: (i, 0, 0))
    return place, by_head, whole, logs


def attend(place, queries, kv_window):
    tok_rows, features = queries.shape
    window_rows = kv_window.shape[0]
    pairs = features // HD // PAIR
    place_spec, by_head, whole, logs = attention_specs(tok_rows, features // HD, window_rows)
    work = tok_rows * features * window_rows
    return pl.pallas_call(
        attend_kernel,
        grid=(pairs,),
        out_shape=(
            jax.ShapeDtypeStruct((tok_rows, features), BF16),
            jax.ShapeDtypeStruct((pairs, PAIR * tok_rows, LANES), F32),
        ),
        in_specs=[place_spec, by_head, whole],
        out_specs=(by_head, logs),
        compiler_params=pltpu.CompilerParams(vmem_limit_bytes=VMEM_BYTES),
        cost_estimate=pl.CostEstimate(
            flops=4 * work, bytes_accessed=8 * kv_window.size, transcendentals=work // HD
        ),
        name="attend",
    )(place, queries, kv_window)


def attend_back(place, queries, kv_window, logs_in, grad):
    tok_rows, features = queries.shape
    window_rows = kv_window.shape[0]
    pairs = features // HD // PAIR
    place_spec, by_head, whole, logs = attention_specs(tok_rows, features // HD, window_rows)
    work = tok_rows * features * window_rows
    return pl.pallas_call(
        attend_back_kernel,
        grid=(pairs,),
        out_shape=(
            jax.ShapeDtypeStruct((tok_rows, features), F32),
            jax.ShapeDtypeStruct((window_rows, 2 * HD), F32),
        ),
        in_specs=[place_spec, by_head, whole, logs, by_head],
        out_specs=(by_head, whole),
        compiler_params=pltpu.CompilerParams(vmem_limit_bytes=VMEM_BYTES),
        cost_estimate=pl.CostEstimate(
            flops=10 * work, bytes_accessed=8 * kv_window.size, transcendentals=work // HD
        ),
        name="attend_back",
    )(place, queries, kv_window, logs_in, grad)


MESH=pl.DeviceIdType.MESH

class Place:
    def __init__(self):
        me = lax.axis_index(AXIS)
        self.core = me % 2
        self.x = (me // 2) % 2
        self.y = (me // 4) % 2
        self.z = me // 8
        self.sibling = self.index(self.z, self.y, self.x, 1 - self.core)
        self.next_x = self.index(self.z, self.y, 1 - self.x, self.core)
        self.next_y = self.index(self.z, 1 - self.y, self.x, self.core)
        self.plane = [self.z] + [(self.z + o) % 4 for o in (1, 2, 3)]
        self.line = [self.index(p, self.y, self.x, self.core) for p in self.plane]
    def index(self, z, y, x, core):
        return ((z * 2 + y) * 2 + x) * 2 + core
    def side(self, dy, dx):
        return (1 - self.y if dy else self.y), (1 - self.x if dx else self.x)
    def meet(self):
        barrier = pltpu.get_barrier_semaphore()
        partners = [self.sibling, self.next_x, self.next_y] + self.line[1:]
        for device in partners:
            pl.semaphore_signal(barrier, inc=1, device_id=(device,), device_id_type=MESH)
        pl.semaphore_wait(barrier, len(partners))

def send(src, dst, sems, device):
    copy = pltpu.make_async_remote_copy(src_ref=src, dst_ref=dst, send_sem=sems[0], recv_sem=sems[1], device_id=(device,), device_id_type=MESH)
    copy.start()
    return copy

TILE=16

CORNERS = ((1, 1), (0, 1), (1, 0), (0, 0))

def add_tiles(count, rows, target, parts):
    steps = rows // TILE
    @pl.loop(0, count * steps)
    def _(i):
        index, here = i // steps, pl.ds(pl.multiple_of((i % steps) * TILE, TILE), TILE)
        total = None
        for ref, first in parts:
            at = here if first == 0 else pl.ds(pl.multiple_of((i % steps) * TILE + first, TILE), TILE)
            part = ref[index, at].astype(F32)
            total = part if total is None else total + part
        ref, first = target
        at = here if first == 0 else pl.ds(pl.multiple_of((i % steps) * TILE + first, TILE), TILE)
        ref[index, at] = total.astype(BF16)

class SumBuffers:
    def __init__(self, refs):
        self.acc, self.core, self.diag_x, self.diag_y, self.x, self.y, self.z, self.sems = refs
    @staticmethod
    def shapes(rows, columns, units):
        upper = (rows // 2 + TILE - 1) // TILE * TILE
        buf = lambda *shape: pltpu.VMEM(shape + (columns,), BF16)
        return [buf(4, 4, rows), buf(4, 4, rows), buf(4, upper), buf(4, rows - upper), buf(4, rows), buf(4, rows), buf(3, rows),
                pltpu.SemaphoreType.DMA((units, 2, Sum.COPIES))]
    COUNT = 8

class Sum:
    COPIES = 14
    def __init__(self, place, bufs, unit, cols, own, other, out):
        self.p, self.b, self.unit, self.own, self.other, self.out = place, bufs, unit, own, other, out
        self.rows = bufs.acc.shape[2]
        self.upper = bufs.diag_x.shape[1]
        self.lower = self.rows - self.upper
        self.acc = bufs.acc.at[:, :, :, cols]
        self.core = bufs.core.at[:, :, :, cols]
        self.diag_x, self.diag_y = bufs.diag_x.at[:, :, cols], bufs.diag_y.at[:, :, cols]
        self.x, self.y, self.z = bufs.x.at[:, :, cols], bufs.y.at[:, :, cols], bufs.z.at[:, :, cols]
        self.copies = {}
    def push(self, slot, src, dst, device):
        sems = self.b.sems
        self.copies[slot] = send(src, dst, (sems.at[self.unit, 0, slot], sems.at[self.unit, 1, slot]), device)
    def begin(self):
        for i in range(4):
            self.push(i, self.other(i), self.core.at[i], self.p.sibling)
    def stage0(self):
        top, bottom = pl.ds(0, self.upper), pl.ds(self.upper, self.lower)
        for i in range(4):
            self.copies[i].wait_recv()
            add_tiles(4, self.rows, (self.acc.at[i], 0), [(self.own(i), 0), (self.core.at[i], 0)])
            if i == 0:
                self.push(4, self.acc.at[0, :, top], self.diag_x, self.p.next_x)
                self.push(5, self.acc.at[0, :, bottom], self.diag_y, self.p.next_y)
            if i == 1:
                self.push(6, self.acc.at[1, :, top], self.x.at[:, top], self.p.next_x)
            if i == 2:
                self.push(7, self.acc.at[2, :, bottom], self.y.at[:, bottom], self.p.next_y)
    def stage1(self):
        top, bottom = pl.ds(0, self.upper), pl.ds(self.upper, self.lower)
        self.copies[4].wait_recv()
        add_tiles(4, self.upper, (self.acc.at[2], 0), [(self.acc.at[2], 0), (self.diag_x, 0)])
        self.push(8, self.acc.at[2, :, top], self.y.at[:, top], self.p.next_y)
        self.copies[5].wait_recv()
        add_tiles(4, self.lower, (self.acc.at[1], self.upper), [(self.acc.at[1], self.upper), (self.diag_y, 0)])
        self.push(9, self.acc.at[1, :, bottom], self.x.at[:, bottom], self.p.next_x)
    def stage2(self):
        for slot in (6, 7, 8, 9):
            self.copies[slot].wait_recv()
        add_tiles(4, self.rows, (self.acc.at[3], 0), [(self.acc.at[3], 0), (self.x, 0), (self.y, 0)])
        for o in (1, 2, 3):
            self.push(9 + o, self.acc.at[3, self.p.plane[o]], self.z.at[o - 1], self.p.line[o])
    def stage3(self):
        for o in (1, 2, 3):
            self.copies[9 + o].wait_recv()
        @pl.loop(0, self.rows // TILE)
        def _(i):
            here = pl.ds(pl.multiple_of(i * TILE, TILE), TILE)
            total = self.acc[3, self.p.z, here].astype(F32)
            for o in range(3):
                total += self.z[o, here].astype(F32)
            self.out[here] = total
    def core_sent(self):
        for i in range(4): self.copies[i].wait_send()
    def finish(self):
        for slot in range(4, 13): self.copies[slot].wait_send()

def product_units(place, bufs, part, chunk, left, right, out, extra):
    rows = out.shape[0]
    wide = 8 * rows
    units = []

    def add_unit(k, first):
        slot = k % 2
        span = min(chunk, right.shape[1] - first)

        def half(i, core):
            y, x = place.side(*CORNERS[i])
            return part.at[slot, :, y, x, core]

        unit = Sum(
            place, bufs, k, pl.ds(k * chunk, chunk),
            lambda i: half(i, place.core), lambda i: half(i, 1 - place.core),
            out.at[:, pl.ds(first, chunk)],
        )

        def make():
            if k >= 2:
                units[k - 2][0].core_sent()

            @pl.loop(0, 4)
            def _(z):
                here = pl.ds(pl.multiple_of(z * wide, wide), wide)
                product = dot(left[:, here], right[:, pl.ds(first, span)], ((0,), (0,)))
                block = (2, 2, 2, rows)
                part[slot, z, :, :, :, :, pl.ds(0, span)] = product.astype(BF16).reshape(block + (span,))
                if span < chunk:
                    part[slot, z, :, :, :, :, pl.ds(span, chunk - span)] = extra[here].reshape(
                        block + (chunk - span,)
                    )

            unit.begin()

        units.append((unit, make))

    for k, first in enumerate(range(0, out.shape[1], chunk)):
        add_unit(k, first)
    return units


def product_sum_kernel(chunk, left, right, extra, out, part, *scratch):
    place = Place()
    units = product_units(place, SumBuffers(scratch), part, chunk, left, right, out, extra)
    place.meet()
    count = len(units)
    stages = [lambda k: units[k][1]()] + [
        lambda k, name=name: getattr(units[k][0], name)()
        for name in ("stage0", "stage1", "stage2", "stage3")
    ]
    for step in range(count + 4):
        for s in (1, 2, 3, 4, 0):
            if 0 <= step - s < count:
                stages[s](step - s)
    for unit, _ in units[-2:]:
        unit.core_sent()
    for unit, _ in units:
        unit.finish()


def product_sum(left, right, extra, chunk, collective_id, name):
    rows = left.shape[1] // 32
    columns = right.shape[1] + extra.shape[1]
    vmem = pl.BlockSpec(memory_space=pltpu.VMEM)
    return pl.pallas_call(
        functools.partial(product_sum_kernel, chunk),
        out_shape=jax.ShapeDtypeStruct((rows, columns), F32),
        in_specs=[vmem] * 3,
        out_specs=vmem,
        scratch_shapes=[pltpu.VMEM((2, 4, 2, 2, 2, rows, chunk), BF16)]
        + SumBuffers.shapes(rows, columns, columns // chunk),
        compiler_params=pltpu.CompilerParams(
            collective_id=collective_id, has_side_effects=True, vmem_limit_bytes=62 * 1024 * 1024
        ),
        name=name,
    )(left, right, extra)


def back_sums_kernel(
    chunk, left, right, query_ref, window, log_ref, grad_ref,
    out, query_grad_ref, kv_grad_ref, part, kv_total, kv_part, *scratch,
):
    place = Place()
    me = lax.axis_index(AXIS)
    tok_rows, features = query_ref.shape
    blocks = window.shape[0] // tok_rows
    start = jnp.maximum(me - (blocks - 1), 0)
    ahead = (me - start) * tok_rows
    units = product_units(
        place, SumBuffers(scratch[: SumBuffers.COUNT]), part, chunk, left, right, out, None
    )
    sums = [unit for unit, _ in units]

    def half(i, core):
        y, x = place.side(*CORNERS[i])
        return kv_part.at[:, y, x, core]

    kv = Sum(
        place, SumBuffers(scratch[SumBuffers.COUNT :]), 0, pl.ds(0, 2 * HD),
        lambda i: half(i, place.core), lambda i: half(i, 1 - place.core), kv_grad_ref,
    )
    place.meet()
    units[0][1]()
    units[1][1]()
    sums[0].stage0()
    sums[1].stage0()
    kv_total[...] = jnp.zeros_like(kv_total)
    kv_part[...] = jnp.zeros_like(kv_part)

    @pl.loop(0, features // (PAIR * HD))
    def _(i):
        here = pl.ds(pl.multiple_of(i * PAIR * HD, PAIR * HD), PAIR * HD)
        query_grad, key_part, value_part = attend_back_pair(
            ahead, query_ref[:, here], grad_ref[:, here], window[:, :HD], window[:, HD:],
            log_ref[i][:, :1],
        )
        query_grad_ref[:, here] = query_grad
        kv_total[:, :HD] += key_part
        kv_total[:, HD:] += value_part

    for j in range(blocks):
        block = start + j
        kv_part[block // 8, (block // 4) % 2, (block // 2) % 2, block % 2] = kv_total[
            j * tok_rows : (j + 1) * tok_rows
        ].astype(BF16)
    kv.begin()
    sums[0].stage1()
    kv.stage0()
    sums[1].stage1()
    units[2][1]()
    kv.stage1()
    sums[0].stage2()
    sums[2].stage0()
    kv.stage2()
    sums[1].stage2()
    units[3][1]()
    sums[2].stage1()
    sums[3].stage0()
    kv.stage3()
    sums[0].stage3()
    sums[2].stage2()
    sums[3].stage1()
    sums[1].stage3()
    sums[3].stage2()
    sums[2].stage3()
    sums[3].stage3()
    for unit in sums[2:] + [kv]:
        unit.core_sent()
    for unit in sums + [kv]:
        unit.finish()


def back_sums(left, right, queries, kv_window, logs, grad, collective_id):
    rows, columns = left.shape[1] // 32, right.shape[1]
    tok_rows, features = queries.shape
    chunk = columns // 4
    vmem = pl.BlockSpec(memory_space=pltpu.VMEM)
    return pl.pallas_call(
        functools.partial(back_sums_kernel, chunk),
        out_shape=(
            jax.ShapeDtypeStruct((rows, columns), F32),
            jax.ShapeDtypeStruct((tok_rows, features), F32),
            jax.ShapeDtypeStruct((tok_rows, 2 * HD), F32),
        ),
        in_specs=[vmem] * 6,
        out_specs=(vmem,) * 3,
        scratch_shapes=[
            pltpu.VMEM((2, 4, 2, 2, 2, rows, chunk), BF16),
            pltpu.VMEM(kv_window.shape, F32),
            pltpu.VMEM((4, 2, 2, 2, tok_rows, 2 * HD), BF16),
        ]
        + SumBuffers.shapes(rows, columns, 4)
        + SumBuffers.shapes(tok_rows, 2 * HD, 1),
        compiler_params=pltpu.CompilerParams(
            collective_id=collective_id, has_side_effects=True, vmem_limit_bytes=62 * 1024 * 1024
        ),
        name="back_sums",
    )(left, right, queries, kv_window, logs, grad)


PLANES=4
def plane_order(z):
    near = jnp.minimum(z, 3 - z)
    flip = z // 2
    order = []
    for k in range(4):
        swapped = 1 - k if k < 2 else k
        plane = near * swapped + (1 - near) * k
        order.append(flip * (3 - plane) + (1 - flip) * plane)
    return order

class Gather:
    COPIES = 11
    def __init__(self, place, own, held, cols, sems):
        self.place, self.held, self.cols, self.sems = place, held, cols, sems
        self.own = own.at[:, cols]
        rows = held.shape[4]
        upper = (rows // 2 + TILE - 1) // TILE * TILE
        self.halves = pl.ds(0, upper), pl.ds(upper, rows - upper)
        self.order = plane_order(place.z)
        self.sent = []
        self.kept = []
    def at(self, plane, y, x, core, part=slice(None)):
        return self.held.at[plane, y, x, core, part, self.cols]
    def pair(self, slot, k):
        return self.sems.at[0, slot, k], self.sems.at[1, slot, k]
    def push(self, src, dst, slot, k, device):
        copy = send(src, dst, self.pair(slot, k), device)
        self.sent.append(copy)
    def arrived(self, ref, slot, k):
        pltpu.make_async_remote_copy(src_ref=ref, dst_ref=ref, send_sem=self.sems.at[0, slot, k], recv_sem=self.sems.at[1, slot, k], device_id=(self.place.sibling,), device_id_type=MESH).wait_recv()
    def start(self):
        p = self.place
        mine = self.at(p.z, p.y, p.x, p.core)
        keep = pltpu.make_async_copy(self.own, mine, self.sems.at[0, 10, 0])
        keep.start()
        self.kept.append(keep)
        for k in (1, 2, 3):
            plane = self.order[k]
            copy = pltpu.make_async_remote_copy(src_ref=self.own, dst_ref=mine, send_sem=self.sems.at[0, 0, k], recv_sem=self.sems.at[1, 0, p.z], device_id=(p.index(plane, p.y, p.x, p.core),), device_id_type=MESH)
            copy.start(); self.sent.append(copy)
    def line(self, k):
        p = self.place
        plane = self.order[k]
        block = self.at(plane, p.y, p.x, p.core)
        source = self.own if k == 0 else block
        if k > 0:
            pltpu.make_async_remote_copy(src_ref=block, dst_ref=block, send_sem=self.sems.at[0, 0, k], recv_sem=self.sems.at[1, 0, plane], device_id=(p.sibling,), device_id_type=MESH).wait_recv()
        self.push(source, block, 1, k, p.next_x)
        self.push(source, block, 2, k, p.next_y)
        self.push(source, block, 5, k, p.sibling)
    def side(self, k):
        p, plane = self.place, self.order[k]
        top, bottom = self.halves
        self.arrived(self.at(plane, p.y, 1 - p.x, p.core), 1, k)
        block = self.at(plane, p.y, 1 - p.x, p.core, top)
        self.push(block, block, 4, k, p.next_y)
        block = self.at(plane, p.y, 1 - p.x, p.core)
        self.push(block, block, 6, k, p.sibling)
        self.arrived(self.at(plane, 1 - p.y, p.x, p.core), 2, k)
        block = self.at(plane, 1 - p.y, p.x, p.core, bottom)
        self.push(block, block, 3, k, p.next_x)
        block = self.at(plane, 1 - p.y, p.x, p.core)
        self.push(block, block, 7, k, p.sibling)
    def diag(self, k):
        p, plane = self.place, self.order[k]
        for slot, part in ((4, self.halves[0]), (3, self.halves[1])):
            block = self.at(plane, 1 - p.y, 1 - p.x, p.core, part)
            self.arrived(block, slot, k)
            self.push(block, block, slot + 5, k, p.sibling)
    def ready(self, k):
        p, plane = self.place, self.order[k]
        top, bottom = self.halves
        if k == 0:
            for keep in self.kept: keep.wait()
        other = 1 - p.core
        self.arrived(self.at(plane, p.y, p.x, other), 5, k)
        self.arrived(self.at(plane, p.y, 1 - p.x, other), 6, k)
        self.arrived(self.at(plane, 1 - p.y, p.x, other), 7, k)
        self.arrived(self.at(plane, 1 - p.y, 1 - p.x, other, top), 9, k)
        self.arrived(self.at(plane, 1 - p.y, 1 - p.x, other, bottom), 8, k)
    def finish(self):
        for copy in self.sent: copy.wait_send()

def pipeline(stages, count):
    for step in range(count + len(stages) - 1):
        for s in range(len(stages) - 1, -1, -1):
            if 0 <= step - s < count:
                stages[s](step - s)

def gather_kernel(chunks, *refs):
    n = len(chunks)
    ins, outs, sems = refs[:n], refs[n:2*n], refs[2*n:]
    place = Place()
    place.meet()
    items = []
    for a in range(n):
        width = ins[a].shape[1] // chunks[a]
        for j in range(chunks[a]):
            items.append(Gather(place, ins[a], outs[a], pl.ds(j * width, width), sems[a].at[j]))
    def line(s):
        if s % PLANES == 0:
            items[s // PLANES].start()
        items[s // PLANES].line(s % PLANES)
    def side(s): items[s // PLANES].side(s % PLANES)
    def diag(s): items[s // PLANES].diag(s % PLANES)
    pipeline([line, side, diag], len(items) * PLANES)
    for item in items:
        for k in range(PLANES): item.ready(k)
    for item in items: item.finish()

def gather_all(arrays, chunks, collective_id, name):
    outs = pl.pallas_call(
        functools.partial(gather_kernel, chunks),
        out_shape=tuple(jax.ShapeDtypeStruct((4,2,2,2)+a.shape, BF16) for a in arrays),
        in_specs=[pl.BlockSpec(memory_space=pl.ANY)]*len(arrays),
        out_specs=tuple(pl.BlockSpec(memory_space=pl.ANY) for _ in arrays),
        scratch_shapes=[pltpu.SemaphoreType.DMA((c, 2, Gather.COPIES, PLANES)) for c in chunks],
        compiler_params=pltpu.CompilerParams(collective_id=collective_id, has_side_effects=True),
        name=name,
    )(*arrays)
    return [o.reshape(32 * a.shape[0], a.shape[1]) for o, a in zip(outs, arrays)]


GELU_SCALE = math.sqrt(2.0 / math.pi)
GELU_CUBE = 0.044715

def gelu_and_slope(v):
    square = v * v
    t = jnp.tanh(GELU_SCALE * v * (1.0 + GELU_CUBE * square))
    half = 0.5 * (1.0 + t)
    slope = half + 0.5 * v * (1.0 - t * t) * (GELU_SCALE * (1.0 + 3.0 * GELU_CUBE * square))
    return v * half, slope

def gather_attend_kernel(
    kv_ref, weight_ref, cotangent_ref, query_ref,
    kv_held, weight_held, cotangent_held, window, out_ref, log_ref,
    kv_sems, weight_sems, cotangent_sems, load_sems,
):
    place = Place()
    me = lax.axis_index(AXIS)
    tok_rows, features = query_ref.shape
    blocks = window.shape[0] // tok_rows
    start = jnp.maximum(me - (blocks - 1), 0)
    place.meet()

    def item(own, held, sems):
        return Gather(place, own, held, pl.ds(0, own.shape[1]), sems)

    kv = item(kv_ref, kv_held, kv_sems)
    weight = item(weight_ref, weight_held, weight_sems)
    cotangent = item(cotangent_ref, cotangent_held, cotangent_sems)
    for one in (kv, weight, cotangent):
        one.start()

    def run(*steps):
        for one, name, k in steps:
            getattr(one, name)(k)

    run(
        (kv, "line", 0), (weight, "line", 0), (kv, "line", 1), (kv, "side", 0),
        (kv, "line", 2), (kv, "side", 1), (kv, "diag", 0), (kv, "line", 3),
        (kv, "side", 2), (kv, "diag", 1), (kv, "side", 3), (kv, "diag", 2), (kv, "diag", 3),
        (weight, "line", 1), (cotangent, "line", 0), (weight, "side", 0), (weight, "line", 2),
        (weight, "side", 1), (weight, "diag", 0), (weight, "line", 3), (cotangent, "line", 1),
        (kv, "ready", 0), (kv, "ready", 1), (kv, "ready", 2), (kv, "ready", 3),
    )
    loads = []
    for j in range(blocks):
        block = start + j
        load = pltpu.make_async_copy(
            kv_held.at[block // 8, (block // 4) % 2, (block // 2) % 2, block % 2],
            window.at[pl.ds(j * tok_rows, tok_rows)],
            load_sems.at[j],
        )
        load.start()
        loads.append(load)
    for load in loads:
        load.wait()
    run((weight, "side", 2), (weight, "diag", 1))
    ahead = (me - start) * tok_rows

    @pl.loop(0, features // (PAIR * HD))
    def _(i):
        here = pl.ds(pl.multiple_of(i * PAIR * HD, PAIR * HD), PAIR * HD)
        attended, logs = attend_pair(ahead, query_ref[:, here], window[:, :HD], window[:, HD:])
        out_ref[:, here] = attended
        log_ref[i] = jnp.broadcast_to(logs, log_ref.shape[1:])

    run(
        (cotangent, "side", 0), (weight, "side", 3), (weight, "diag", 2), (cotangent, "line", 2),
        (weight, "diag", 3), (cotangent, "side", 1), (cotangent, "diag", 0),
        (cotangent, "line", 3), (cotangent, "side", 2), (cotangent, "diag", 1),
        (cotangent, "side", 3), (cotangent, "diag", 2), (cotangent, "diag", 3),
    )
    for one in (weight, cotangent):
        for k in range(PLANES):
            one.ready(k)
    for one in (kv, weight, cotangent):
        one.finish()


def gather_attend(own_kv, out_weight, out_cotangent, queries, collective_id):
    tok_rows, features = queries.shape
    blocks = (WINDOW + tok_rows - 2) // tok_rows + 1
    pairs = features // HD // PAIR
    arrays = (own_kv, out_weight, out_cotangent)
    hbm = pl.BlockSpec(memory_space=pl.ANY)
    vmem = pl.BlockSpec(memory_space=pltpu.VMEM)
    outs = pl.pallas_call(
        gather_attend_kernel,
        out_shape=tuple(jax.ShapeDtypeStruct((4, 2, 2, 2) + a.shape, BF16) for a in arrays)
        + (
            jax.ShapeDtypeStruct((blocks * tok_rows, own_kv.shape[1]), BF16),
            jax.ShapeDtypeStruct((tok_rows, features), BF16),
            jax.ShapeDtypeStruct((pairs, PAIR * tok_rows, LANES), F32),
        ),
        in_specs=[hbm] * 3 + [vmem],
        out_specs=(hbm,) * 3 + (vmem,) * 3,
        scratch_shapes=[pltpu.SemaphoreType.DMA((2, Gather.COPIES, PLANES)) for _ in arrays]
        + [pltpu.SemaphoreType.DMA((blocks,))],
        compiler_params=pltpu.CompilerParams(
            collective_id=collective_id, has_side_effects=True, vmem_limit_bytes=VMEM_BYTES
        ),
        name="gather_attend",
    )(*arrays, queries)
    full = [o.reshape(32 * a.shape[0], a.shape[1]) for o, a in zip(outs[1:3], arrays[1:])]
    return full[0], full[1], outs[3], outs[4], outs[5]


class PlaneSum:
    SLOTS = 10
    def __init__(self, place, order, kind, k, acc, outgoing, out, land, load, sems, line_sems, load_sems):
        self.p, self.k, self.order = place, k, order
        self.acc, self.outgoing = acc.at[kind, k], outgoing.at[kind]
        self.out = out
        core, diag_x, diag_y, side_x, side_y, line = land
        self.core, self.side_x, self.side_y = core.at[kind, k], side_x.at[kind, k], side_y.at[kind, k]
        self.diag_x, self.diag_y, self.land = diag_x.at[kind, k], diag_y.at[kind, k], line.at[kind]
        self.load, self.load_sems = load, load_sems
        self.sems, self.line_sems = sems.at[kind, k], line_sems.at[kind]
        self.rows = self.acc.shape[1]
        self.upper = self.diag_x.shape[0]
        self.top, self.bottom = pl.ds(0, self.upper), pl.ds(self.upper, self.rows - self.upper)
    def mine(self, i): return self.acc.at[i]
    def copy(self, src, dst, slot, device):
        return pltpu.make_async_remote_copy(src_ref=src, dst_ref=dst, send_sem=self.sems.at[0, slot], recv_sem=self.sems.at[1, slot], device_id=(device,), device_id_type=MESH)
    def across(self, i):
        return self.copy(self.outgoing.at[i % 2], self.core.at[i], i, self.p.sibling)
    def make(self, slot):
        p, mine = self.p, self.mine
        src, dst, device = {
            4: (mine(0).at[self.top], self.diag_x, p.next_x),
            5: (mine(0).at[self.bottom], self.diag_y, p.next_y),
            6: (mine(1).at[self.top], self.side_x.at[self.top], p.next_x),
            7: (mine(2).at[self.bottom], self.side_y.at[self.bottom], p.next_y),
            8: (mine(2).at[self.top], self.side_y.at[self.top], p.next_y),
            9: (mine(1).at[self.bottom], self.side_x.at[self.bottom], p.next_x),
        }[slot]
        return self.copy(src, dst, slot, device)
    def line_copy(self):
        p, plane = self.p, self.order[self.k]
        return pltpu.make_async_remote_copy(src_ref=self.mine(3), dst_ref=self.land.at[p.z], send_sem=self.line_sems.at[0, self.k], recv_sem=self.line_sems.at[1, p.z], device_id=(p.index(plane, p.y, p.x, p.core),), device_id_type=MESH)
    def fetch(self, src, slot):
        rows = src.shape[0]
        copy = pltpu.make_async_copy(src, self.load.at[slot, pl.ds(0, rows)], self.load_sems.at[slot])
        copy.start()
        return copy
    def add(self, target, slots, rows):
        @pl.loop(0, rows // TILE)
        def _(i):
            here = pl.ds(pl.multiple_of(i * TILE, TILE), TILE)
            total = target[here].astype(F32)
            for slot in slots: total += self.load[slot, here].astype(F32)
            target[here] = total.astype(target.dtype)
    def stage0(self):
        self.across(0).wait_recv()
        fetched = self.fetch(self.core.at[0], 0)
        for i in range(4):
            current = fetched
            if i < 3:
                self.across(i + 1).wait_recv()
                fetched = self.fetch(self.core.at[i + 1], (i + 1) % 2)
            current.wait()
            self.add(self.mine(i), [i % 2], self.rows)
            for slot in ((4, 5), (6,), (7,), ())[i]:
                self.make(slot).start()
    def stage1(self):
        self.make(4).wait_recv()
        self.fetch(self.diag_x, 0).wait()
        self.add(self.mine(2).at[self.top], [0], self.upper)
        self.make(8).start()
        self.make(5).wait_recv()
        self.fetch(self.diag_y, 1).wait()
        self.add(self.mine(1).at[self.bottom], [1], self.rows - self.upper)
        self.make(9).start()
    def stage2(self):
        for slot in (6, 9): self.make(slot).wait_recv()
        first = self.fetch(self.side_x, 0)
        for slot in (7, 8): self.make(slot).wait_recv()
        second = self.fetch(self.side_y, 1)
        first.wait(); second.wait()
        if self.k > 0:
            self.add(self.mine(3), [0, 1], self.rows)
            self.line_copy().start()
        else:
            mine, out = self.mine(3), self.out
            @pl.loop(0, self.rows // TILE)
            def _(i):
                here = pl.ds(pl.multiple_of(i * TILE, TILE), TILE)
                out[here] = mine[here].astype(F32) + self.load[0, here].astype(F32) + self.load[1, here].astype(F32)
    def sent(self):
        for slot in range(4, 10): self.make(slot).wait_send()
        if self.k > 0: self.line_copy().wait_send()
    def last(self):
        p, plane = self.p, self.order[self.k]
        land = self.land.at[plane]
        pltpu.make_async_remote_copy(src_ref=land, dst_ref=land, send_sem=self.line_sems.at[0, self.k], recv_sem=self.line_sems.at[1, plane], device_id=(p.sibling,), device_id_type=MESH).wait_recv()
        self.fetch(land, self.k % 2).wait()
        self.add(self.out, [self.k % 2], self.rows)

def ffn_kernel(hidden_ref, cotangent_ref, both_ref, down_ref, bias_ref,
               hidden_sum, ffn_sum, grad_both_ref, grad_down_ref, bias_grad_ref,
               held, land_core, land_dx, land_dy, land_x, land_y, land_z,
               tokens, cot, both_keep, ffn_keep, acc, outgoing, load, gather_sems, cot_sems, sum_sems, line_sems, load_sems):
    place = Place()
    width = hidden_ref.shape[1]
    pad = down_ref.shape[0]
    rows = 2 * hidden_ref.shape[0]
    order = plane_order(place.z)
    def fetch_cot(k): return pltpu.make_async_copy(cotangent_ref.at[order[k]], cot, cot_sems.at[0, k])
    def fetch_tokens(k): return pltpu.make_async_copy(held.at[order[k]], tokens, cot_sems.at[1, k])
    fetch_cot(0).start()
    place.meet()
    gather = Gather(place, hidden_ref, held, pl.ds(0, width), gather_sems)
    gather.start()
    grad_both_ref[...] = jnp.zeros_like(grad_both_ref)
    grad_down_ref[...] = jnp.zeros_like(grad_down_ref)
    bias_grad_ref[...] = jnp.zeros_like(bias_grad_ref)
    land = (land_core, land_dx, land_dy, land_x, land_y, land_z)
    sums = [[PlaneSum(place, order, kind, k, acc, outgoing, (hidden_sum, ffn_sum)[kind], land, load, sum_sems, line_sems, load_sems) for k in range(PLANES)] for kind in range(2)]

    def compute(k):
        gather.ready(k)
        fetch_tokens(k).start()
        fetch_tokens(k).wait()
        fetch_cot(k).wait()
        half = rows // 2
        @pl.loop(0, 4)
        def _(i):
            dy, dx = 1 - i % 2, 1 - i // 2
            y, x = place.y + dy * (1 - 2 * place.y), place.x + dx * (1 - 2 * place.x)
            hidden = tokens[y, x].reshape(rows, width)
            cotangent = cot[y, x].reshape(rows, width)
            both_pre = dot(hidden, both_ref[...], ((1,), (0,))) + bias_ref[0:1]
            hidden_grad = dot(cotangent, down_ref[...], ((1,), (1,)))
            activated, slope = gelu_and_slope(both_pre[:, :pad])
            up_pre = both_pre[:, pad:]
            hidden_ffn = (activated * up_pre).astype(BF16)
            both_grad = jnp.concatenate([(hidden_grad * up_pre * slope).astype(BF16), (hidden_grad * activated).astype(BF16)], axis=1)
            here = pl.ds(pl.multiple_of((y * 2 + x) * rows, rows), rows)
            both_keep[here] = both_grad
            ffn_keep[here] = hidden_ffn
            bias_grad_ref[...] += jnp.sum(both_grad.astype(F32), axis=0, keepdims=True)
            def drain():
                for kind in range(2): sums[kind][k].across(i - 2).wait_send()
            def drain_before():
                for kind in range(2): sums[kind][k - 1].across(i + 2).wait_send()
            pl.when(i >= 2)(drain)
            if k > 0: pl.when(i < 2)(drain_before)
            for kind, part in ((0, lambda: dot(both_grad, both_ref[...], ((1,), (1,)))), (1, lambda: dot(hidden_ffn, down_ref[...], ((1,), (0,))))):
                result = part().astype(BF16)
                low, high = result[:half], result[half:]
                acc[kind, k, i] = jnp.where(place.core == 0, low, high)
                outgoing[kind, i % 2] = jnp.where(place.core == 0, high, low)
                sums[kind][k].across(i).start()

    def weight_grads(k):
        step = 512
        @pl.loop(0, width // step)
        def _(j):
            cols = pl.ds(pl.multiple_of(j * step, step), step)
            hidden = tokens[:, :, :, :, cols].reshape(4 * rows, step)
            grad_both_ref[:, cols] += dot(both_keep[...], hidden, ((0,), (0,)))
            cotangent = cot[:, :, :, :, cols].reshape(4 * rows, step)
            grad_down_ref[:, cols] += dot(ffn_keep[...], cotangent, ((0,), (0,)))
        if k + 1 < PLANES: fetch_cot(k + 1).start()

    def both(name, k):
        for kind in range(2): getattr(sums[kind][k], name)()

    gather.line(0)
    gather.line(1)
    gather.side(0)
    gather.line(2)
    gather.side(1)
    gather.diag(0)
    compute(0)
    gather.line(3)
    gather.side(2)
    weight_grads(0)
    gather.diag(1)
    compute(1)
    gather.side(3)
    both("stage0", 1)
    gather.diag(2)
    weight_grads(1)
    gather.diag(3)
    both("stage1", 1)
    compute(2)
    both("stage0", 2)
    both("stage2", 1)
    weight_grads(2)
    compute(3)
    both("stage1", 2)
    both("stage0", 3)
    both("stage2", 2)
    both("stage1", 3)
    both("stage0", 0)
    weight_grads(3)
    both("stage2", 3)
    both("stage1", 0)
    both("stage2", 0)
    for kind in range(2):
        for i in (2, 3): sums[kind][3].across(i).wait_send()
    for kind in range(2):
        for k in (1, 2, 3): sums[kind][k].last()
    for k in range(PLANES): both("sent", k)
    gather.finish()

def ffn(hidden_two, cotangent_full, both_own, both_bias, down_own, collective_id):
    tok_rows, width = hidden_two.shape
    pad = down_own.shape[0]
    full = (4, 2, 2, 2, tok_rows, width)
    upper = (tok_rows // 2 + TILE - 1) // TILE * TILE
    hbm = pl.BlockSpec(memory_space=pl.ANY)
    vmem = pl.BlockSpec(memory_space=pltpu.VMEM)
    dma = pltpu.SemaphoreType.DMA
    low = lambda *shape: jax.ShapeDtypeStruct(shape + (width,), BF16)
    outs = pl.pallas_call(
        ffn_kernel,
        out_shape=(
            jax.ShapeDtypeStruct((tok_rows, width), F32),
            jax.ShapeDtypeStruct((tok_rows, width), F32),
            jax.ShapeDtypeStruct((2 * pad, width), F32),
            jax.ShapeDtypeStruct((pad, width), F32),
            jax.ShapeDtypeStruct((8, 2 * pad), F32),
            low(4, 2, 2, 2, tok_rows),
            low(2, 4, 4, tok_rows), low(2, 4, upper), low(2, 4, tok_rows - upper),
            low(2, 4, tok_rows), low(2, 4, tok_rows), low(2, 4, tok_rows),
        ),
        in_specs=[hbm, hbm, vmem, vmem, vmem],
        out_specs=(vmem,) * 5 + (hbm,) * 7,
        scratch_shapes=[
            pltpu.VMEM(full[1:], BF16),
            pltpu.VMEM(full[1:], BF16),
            pltpu.VMEM((8 * tok_rows, 2 * pad), BF16),
            pltpu.VMEM((8 * tok_rows, pad), BF16),
            pltpu.VMEM((2, 4, 4, tok_rows, width), BF16),
            pltpu.VMEM((2, 2, tok_rows, width), BF16),
            pltpu.VMEM((2, tok_rows, width), BF16),
            dma((2, Gather.COPIES, PLANES)), dma((2, PLANES)), dma((2, PLANES, 2, PlaneSum.SLOTS)), dma((2, 2, PLANES)), dma((2,)),
        ],
        compiler_params=pltpu.CompilerParams(collective_id=collective_id, has_side_effects=True, vmem_limit_bytes=63*1024*1024),
        name="feed_forward",
    )(hidden_two, cotangent_full.reshape(full), both_own, down_own, jnp.broadcast_to(both_bias, (8, 2 * pad)))
    return outs[0], outs[1], outs[2], outs[3], outs[4][0]


def gather_rows(arrays, collective_id, name):
    if lax.axis_size(AXIS) == DEVICES:
        return gather_all(arrays, [1] * len(arrays), collective_id, name)
    return [lax.all_gather(values, AXIS, axis=0, tiled=True) for values in arrays]


def sum_rows(partial):
    return lax.psum_scatter(
        partial.astype(BF16), AXIS, scatter_dimension=0, tiled=True
    ).astype(F32)


def swap(pieces):
    return lax.all_to_all(pieces, AXIS, 0, 0, tiled=False)


def feed_forward(hidden_two, cotangent_full, both_own, both_bias, down_own, rows):
    peers = lax.axis_size(AXIS)
    device = lax.axis_index(AXIS)
    tok_rows, width = hidden_two.shape
    ffn_pad = down_own.shape[0]
    own_cotangent = lax.dynamic_slice_in_dim(cotangent_full, device * rows, rows, 1)
    down_bias_share = jnp.sum(own_cotangent.astype(F32), axis=0)
    if peers == DEVICES:
        normed_grad, ffn_out, grad_both, grad_down, bias_share = ffn(
            hidden_two, cotangent_full, both_own, both_bias, down_own, 7
        )
        return normed_grad, ffn_out, grad_both.T, grad_down, bias_share, down_bias_share

    def piece(sums, here):
        hidden_own, cotangent_piece = here
        hidden_full = gather_rows([hidden_own], None, None)[0]
        both_pre = jnp.dot(hidden_full, both_own, preferred_element_type=F32) + both_bias
        activated, slope = gelu_and_slope(both_pre[:, :ffn_pad])
        up_pre = both_pre[:, ffn_pad:]
        hidden_ffn = (activated * up_pre).astype(BF16)
        hidden_grad = dot(cotangent_piece, down_own, ((1,), (1,)))
        gate_grad = (hidden_grad * up_pre * slope).astype(BF16)
        up_grad = (hidden_grad * activated).astype(BF16)
        both_grad = jnp.concatenate([gate_grad, up_grad], axis=1)
        normed_grad = sum_rows(dot(both_grad, both_own, ((1,), (1,))))
        ffn_out = sum_rows(jnp.dot(hidden_ffn, down_own, preferred_element_type=F32))
        shares = (
            dot(hidden_full, both_grad, ((0,), (0,))),
            dot(hidden_ffn, cotangent_piece, ((0,), (0,))),
            jnp.sum(both_grad.astype(F32), axis=0),
        )
        return jax.tree.map(jnp.add, sums, shares), (normed_grad, ffn_out)

    pieces = max(1, peers // DEVICES)
    cut = tok_rows // pieces
    zeros = (
        jnp.zeros((width, 2 * ffn_pad), F32),
        jnp.zeros((ffn_pad, width), F32),
        jnp.zeros((2 * ffn_pad,), F32),
    )
    cotangent_pieces = cotangent_full.reshape(peers, pieces, cut, width).transpose(1, 0, 2, 3)
    shares, outs = lax.scan(
        piece,
        zeros,
        (hidden_two.reshape(pieces, cut, width), cotangent_pieces.reshape(pieces, -1, width)),
    )
    normed_grad, ffn_out = (part.reshape(tok_rows, width) for part in outs)
    return (normed_grad, ffn_out) + shares + (down_bias_share,)


def body(
    layer_input,
    norm1_scale,
    query_weight,
    keyvalue_weight,
    out_weight,
    norm2_scale,
    gate_weight,
    gate_bias,
    up_weight,
    up_bias,
    down_weight,
    down_bias,
    out_cotangent,
):
    peers = lax.axis_size(AXIS)
    device = lax.axis_index(AXIS)
    tok_rows, width = layer_input.shape
    rows = query_weight.shape[0]
    query_cols = query_weight.shape[1]
    kv_cols = keyvalue_weight.shape[1]
    heads = query_cols // HD
    quarter = HD // 4
    query_scale = 1.0 / math.sqrt(HD)
    ffn_own = down_weight.shape[0]
    ffn_pad = round_up(ffn_own, LANES)

    vectors = jnp.stack([norm1_scale, norm2_scale, down_bias], axis=1)
    packed = jnp.concatenate(
        [query_weight, keyvalue_weight, pad_columns(vectors, LANES)], axis=1
    )
    first = gather_rows([packed], 5, "gather_weights")[0]
    proj_cols = query_cols + kv_cols
    proj_full = first[:, :proj_cols]
    gains = first[:, proj_cols:].astype(F32).T
    gain_one, gain_two, bias_down = gains[0], gains[1], gains[2]

    resid_in = layer_input.astype(F32)
    square_one = jnp.mean(resid_in * resid_in, axis=1, keepdims=True)
    scale_one = lax.rsqrt(square_one + EPSILON)
    normed_one = resid_in * scale_one
    hidden_one = (normed_one * gain_one).astype(BF16)
    projected = jnp.dot(hidden_one, proj_full, preferred_element_type=F32)
    position = device * tok_rows + jnp.arange(tok_rows, dtype=jnp.int32)
    cosine, sine_table = rotary_tables(position.astype(F32), quarter)
    queries = (
        rotate(
            projected[:, :query_cols].reshape(tok_rows, heads, HD),
            cosine[:, None, :],
            sine_table[:, None, :],
            quarter,
        )
        * query_scale
    ).astype(BF16)
    queries = queries.reshape(tok_rows, query_cols)
    keys_rot = rotate(projected[:, query_cols : query_cols + HD], cosine, sine_table, quarter)
    own_kv = jnp.concatenate([keys_rot, projected[:, query_cols + HD :]], axis=1).astype(BF16)

    reach = min((WINDOW + tok_rows - 2) // tok_rows, peers - 1)
    window_rows = (reach + 1) * tok_rows
    window_start = jnp.maximum(device - reach, 0) * tok_rows
    place = (device * tok_rows - window_start).astype(jnp.int32).reshape(1)
    if peers == DEVICES:
        out_full, cotangent_full, kv_window, attention, logs = gather_attend(
            own_kv, out_weight, out_cotangent, queries, 6
        )
    else:
        kv_full, out_full, cotangent_full = gather_rows(
            [own_kv, out_weight, out_cotangent], None, None
        )
        kv_window = lax.dynamic_slice_in_dim(kv_full, window_start, window_rows, 0)
        attention, logs = attend(place, queries, kv_window)

    residual_mid = resid_in + jnp.dot(attention, out_full, preferred_element_type=F32)
    square_two = jnp.mean(residual_mid * residual_mid, axis=1, keepdims=True)
    scale_two = lax.rsqrt(square_two + EPSILON)
    normed_two = residual_mid * scale_two
    hidden_two = (normed_two * gain_two).astype(BF16)

    gate_pieces = pad_columns(gate_weight.reshape(rows, peers, ffn_own), ffn_pad)
    up_pieces = pad_columns(up_weight.reshape(rows, peers, ffn_own), ffn_pad)
    both_own = swap(
        jnp.concatenate([gate_pieces, up_pieces], axis=2).transpose(1, 0, 2)
    ).reshape(peers * rows, 2 * ffn_pad)
    both_bias = jnp.concatenate(
        [pad_columns(gate_bias, ffn_pad), pad_columns(up_bias, ffn_pad)]
    ).astype(F32)
    down_own = jnp.pad(down_weight, ((0, ffn_pad - ffn_own), (0, 0)))

    normed_grad_two, ffn_out, grad_both, grad_down, bias_share, down_bias_share = feed_forward(
        hidden_two, cotangent_full, both_own, both_bias, down_own, rows
    )
    layer_output = (residual_mid + (ffn_out + bias_down)).astype(BF16)
    rms_values = jnp.stack(
        [jnp.sqrt(square_one[:, 0] + EPSILON), jnp.sqrt(square_two[:, 0] + EPSILON)], axis=0
    )
    grad_down = grad_down[:ffn_own]
    grad_both = swap(grad_both.astype(BF16).reshape(peers, rows, 2 * ffn_pad)).transpose(1, 0, 2)
    grad_both = grad_both.astype(F32)
    grad_gate = grad_both[:, :, :ffn_own].reshape(rows, peers * ffn_own)
    grad_up = grad_both[:, :, ffn_pad : ffn_pad + ffn_own].reshape(rows, peers * ffn_own)

    norm2_part = jnp.sum(normed_grad_two * normed_two, axis=0)
    weighted_two = normed_grad_two * gain_two
    mid_grad = out_cotangent.astype(F32) + scale_two * (
        weighted_two - normed_two * jnp.mean(weighted_two * normed_two, axis=1, keepdims=True)
    )
    mid_grad_low = mid_grad.astype(BF16)
    attention_grad = dot(mid_grad_low, out_full, ((1,), (1,))).astype(BF16)

    if peers == DEVICES:
        grad_out, query_grad, kv_grad = back_sums(
            attention, mid_grad_low, queries, kv_window, logs, attention_grad, 3
        )
    else:
        grad_out = sum_rows(dot(attention, mid_grad_low, ((0,), (0,))))
        query_grad, kv_part = attend_back(place, queries, kv_window, logs, attention_grad)
        kv_grad = sum_rows(
            lax.dynamic_update_slice_in_dim(
                jnp.zeros((peers * tok_rows, 2 * HD), BF16), kv_part.astype(BF16), window_start, 0
            )
        )
    query_raw_grad = (
        rotate(
            query_grad.reshape(tok_rows, heads, HD) * query_scale,
            cosine[:, None, :],
            -sine_table[:, None, :],
            quarter,
        )
        .reshape(tok_rows, query_cols)
        .astype(BF16)
    )
    key_raw_grad = rotate(kv_grad[:, :HD], cosine, -sine_table, quarter)
    kv_raw_grad = jnp.concatenate([key_raw_grad, kv_grad[:, HD:]], axis=1).astype(BF16)
    proj_grad = jnp.concatenate([query_raw_grad, kv_raw_grad], axis=1)
    normed_grad_one = dot(proj_grad, proj_full, ((1,), (1,)))
    norm1_part = jnp.sum(normed_grad_one * normed_one, axis=0)
    weighted_one = normed_grad_one * gain_one
    input_grad = (
        mid_grad
        + scale_one
        * (weighted_one - normed_one * jnp.mean(weighted_one * normed_one, axis=1, keepdims=True))
    ).astype(BF16)

    parts = pad_columns(jnp.stack([norm1_part, norm2_part], axis=1), LANES)
    if peers == DEVICES:
        tail = product_sum(hidden_one, proj_grad, parts.astype(BF16), 640, 2, "sum_projections")
    else:
        tail = sum_rows(
            jnp.concatenate(
                [dot(hidden_one, proj_grad, ((0,), (0,))).astype(BF16), parts.astype(BF16)], axis=1
            )
        )
    grad_proj = tail[:, :proj_cols]
    norm1_share = tail[:, proj_cols]
    norm2_share = tail[:, proj_cols + 1]
    return (
        layer_output,
        residual_mid,
        rms_values,
        input_grad,
        norm1_share,
        grad_proj[:, :query_cols],
        grad_proj[:, query_cols:],
        grad_out,
        norm2_share,
        grad_gate,
        bias_share[:ffn_own],
        grad_up,
        bias_share[ffn_pad : ffn_pad + ffn_own],
        grad_down,
        down_bias_share,
    )


def solution(mesh):
    by_rows, by_entry = P(AXIS, None), P(AXIS)
    in_specs = (
        by_rows,
        by_entry,
        by_rows,
        by_rows,
        by_rows,
        by_entry,
        by_rows,
        by_entry,
        by_rows,
        by_entry,
        by_rows,
        by_entry,
        by_rows,
    )
    out_specs = (
        by_rows,
        by_rows,
        P(None, AXIS),
        by_rows,
        by_entry,
        by_rows,
        by_rows,
        by_rows,
        by_entry,
        by_rows,
        by_entry,
        by_rows,
        by_entry,
        by_rows,
        by_entry,
    )
    return jax.shard_map(body, mesh=mesh, in_specs=in_specs, out_specs=out_specs, check_vma=False)
```

```python
import functools
import math

import jax
import jax.numpy as jnp
from jax import lax
from jax.experimental import pallas as pl
from jax.experimental.pallas import tpu as pltpu
from jax.sharding import PartitionSpec as P

HD = 256
WINDOW = 2048
EPSILON = 1e-06
NEGATIVE = -1e30
ROTARY_BASE = 10000.0
AXIS = "blk"
LANES = 128
DEVICES = 32
PAIR = 2
VMEM_BYTES = 48 * 1024 * 1024
F32 = jnp.float32
BF16 = jnp.bfloat16


def rotary_tables(positions, quarter):
    frequency = ROTARY_BASE ** (-(jnp.arange(quarter, dtype=F32) / quarter))
    angles = positions[:, None] * frequency[None, :]
    return (jnp.cos(angles), jnp.sin(angles))


def rotate(vector, cosine, sine_table, quarter):
    leading = vector[..., :quarter]
    trailing = vector[..., quarter : 2 * quarter]
    return jnp.concatenate(
        [
            leading * cosine - trailing * sine_table,
            trailing * cosine + leading * sine_table,
            vector[..., 2 * quarter :],
        ],
        axis=-1,
    )


def dot(left, right, contract):
    return lax.dot_general(left, right, (contract, ((), ())), preferred_element_type=F32)


def round_up(count, step):
    return (count + step - 1) // step * step


def pad_columns(values, columns):
    pad = [(0, 0)] * (values.ndim - 1) + [(0, columns - values.shape[-1])]
    return jnp.pad(values, pad)


def masked_scores(ahead, query_rows, keys, tok_rows):
    scores = dot(query_rows, keys, ((1,), (1,)))
    rows = lax.broadcasted_iota(jnp.int32, scores.shape, 0) % tok_rows
    columns = lax.broadcasted_iota(jnp.int32, scores.shape, 1)
    distance = rows - columns + ahead
    return jnp.where((distance >= 0) & (distance < WINDOW), scores, NEGATIVE)


def stack_heads(block):
    return jnp.concatenate([block[:, i * HD : (i + 1) * HD] for i in range(PAIR)], axis=0)


def unstack_heads(rows):
    tok_rows = rows.shape[0] // PAIR
    return jnp.concatenate([rows[i * tok_rows : (i + 1) * tok_rows] for i in range(PAIR)], axis=1)


def attend_pair(ahead, query, keys, values):
    tok_rows = query.shape[0]
    scores = masked_scores(ahead, stack_heads(query), keys, tok_rows)
    row_max = jnp.max(scores, axis=1, keepdims=True)
    probs = jnp.exp(scores - row_max)
    row_sum = jnp.sum(probs, axis=1, keepdims=True)
    probs_low = (probs * (1.0 / row_sum)).astype(BF16)
    attended = dot(probs_low, values, ((1,), (0,)))
    return unstack_heads(attended).astype(BF16), row_max + jnp.log(row_sum)


def attend_kernel(place_ref, query_ref, kv_ref, out_ref, log_ref):
    attended, logs = attend_pair(place_ref[0], query_ref[...], kv_ref[:, :HD], kv_ref[:, HD:])
    out_ref[...] = attended
    log_ref[0] = jnp.broadcast_to(logs, log_ref.shape[1:])


def attend_back_pair(ahead, query, grad, keys, values, logs):
    tok_rows = query.shape[0]
    query_rows, grad_rows = stack_heads(query), stack_heads(grad)
    scores = masked_scores(ahead, query_rows, keys, tok_rows)
    probs = jnp.exp(scores - logs)
    prob_grad = dot(grad_rows, values, ((1,), (1,)))
    delta = jnp.sum(probs * prob_grad, axis=1, keepdims=True)
    score_grad = (probs * (prob_grad - delta)).astype(BF16)
    query_grad = unstack_heads(dot(score_grad, keys, ((1,), (0,))))
    key_part = dot(score_grad, query_rows, ((0,), (0,)))
    value_part = dot(probs.astype(BF16), grad_rows, ((0,), (0,)))
    return query_grad, key_part, value_part


def attend_back_kernel(place_ref, query_ref, kv_ref, log_ref, grad_ref, query_grad_ref, kv_grad_ref):
    query_grad_ref[...], key_part, value_part = attend_back_pair(
        place_ref[0], query_ref[...], grad_ref[...], kv_ref[:, :HD], kv_ref[:, HD:], log_ref[0][:, :1]
    )

    @pl.when(pl.program_id(0) == 0)
    def _():
        kv_grad_ref[:, :HD] = key_part
        kv_grad_ref[:, HD:] = value_part

    @pl.when(pl.program_id(0) > 0)
    def _():
        kv_grad_ref[:, :HD] += key_part
        kv_grad_ref[:, HD:] += value_part


def attention_specs(tok_rows, heads, window_rows):
    place = pl.BlockSpec(memory_space=pltpu.SMEM)
    by_head = pl.BlockSpec((tok_rows, PAIR * HD), lambda i: (0, i))
    whole = pl.BlockSpec((window_rows, 2 * HD), lambda i: (0, 0))
    logs = pl.BlockSpec((1, PAIR * tok_rows, LANES), lambda i: (i, 0, 0))
    return place, by_head, whole, logs


def attend(place, queries, kv_window):
    tok_rows, features = queries.shape
    window_rows = kv_window.shape[0]
    pairs = features // HD // PAIR
    place_spec, by_head, whole, logs = attention_specs(tok_rows, features // HD, window_rows)
    work = tok_rows * features * window_rows
    return pl.pallas_call(
        attend_kernel,
        grid=(pairs,),
        out_shape=(
            jax.ShapeDtypeStruct((tok_rows, features), BF16),
            jax.ShapeDtypeStruct((pairs, PAIR * tok_rows, LANES), F32),
        ),
        in_specs=[place_spec, by_head, whole],
        out_specs=(by_head, logs),
        compiler_params=pltpu.CompilerParams(vmem_limit_bytes=VMEM_BYTES),
        cost_estimate=pl.CostEstimate(
            flops=4 * work, bytes_accessed=8 * kv_window.size, transcendentals=work // HD
        ),
        name="attend",
    )(place, queries, kv_window)


def attend_back(place, queries, kv_window, logs_in, grad):
    tok_rows, features = queries.shape
    window_rows = kv_window.shape[0]
    pairs = features // HD // PAIR
    place_spec, by_head, whole, logs = attention_specs(tok_rows, features // HD, window_rows)
    work = tok_rows * features * window_rows
    return pl.pallas_call(
        attend_back_kernel,
        grid=(pairs,),
        out_shape=(
            jax.ShapeDtypeStruct((tok_rows, features), F32),
            jax.ShapeDtypeStruct((window_rows, 2 * HD), F32),
        ),
        in_specs=[place_spec, by_head, whole, logs, by_head],
        out_specs=(by_head, whole),
        compiler_params=pltpu.CompilerParams(vmem_limit_bytes=VMEM_BYTES),
        cost_estimate=pl.CostEstimate(
            flops=10 * work, bytes_accessed=8 * kv_window.size, transcendentals=work // HD
        ),
        name="attend_back",
    )(place, queries, kv_window, logs_in, grad)


MESH=pl.DeviceIdType.MESH

class Place:
    def __init__(self):
        me = lax.axis_index(AXIS)
        self.core = me % 2
        self.x = (me // 2) % 2
        self.y = (me // 4) % 2
        self.z = me // 8
        self.sibling = self.index(self.z, self.y, self.x, 1 - self.core)
        self.next_x = self.index(self.z, self.y, 1 - self.x, self.core)
        self.next_y = self.index(self.z, 1 - self.y, self.x, self.core)
        self.plane = [self.z] + [(self.z + o) % 4 for o in (1, 2, 3)]
        self.line = [self.index(p, self.y, self.x, self.core) for p in self.plane]
    def index(self, z, y, x, core):
        return ((z * 2 + y) * 2 + x) * 2 + core
    def side(self, dy, dx):
        return (1 - self.y if dy else self.y), (1 - self.x if dx else self.x)
    def meet(self):
        barrier = pltpu.get_barrier_semaphore()
        partners = [self.sibling, self.next_x, self.next_y] + self.line[1:]
        for device in partners:
            pl.semaphore_signal(barrier, inc=1, device_id=(device,), device_id_type=MESH)
        pl.semaphore_wait(barrier, len(partners))

def send(src, dst, sems, device):
    copy = pltpu.make_async_remote_copy(src_ref=src, dst_ref=dst, send_sem=sems[0], recv_sem=sems[1], device_id=(device,), device_id_type=MESH)
    copy.start()
    return copy

TILE=16

CORNERS = ((1, 1), (0, 1), (1, 0), (0, 0))

def add_tiles(count, rows, target, parts):
    steps = rows // TILE
    @pl.loop(0, count * steps, unroll=2)
    def _(i):
        index, here = i // steps, pl.ds(pl.multiple_of((i % steps) * TILE, TILE), TILE)
        total = None
        for ref, first in parts:
            at = here if first == 0 else pl.ds(pl.multiple_of((i % steps) * TILE + first, TILE), TILE)
            part = ref[index, at].astype(F32)
            total = part if total is None else total + part
        ref, first = target
        at = here if first == 0 else pl.ds(pl.multiple_of((i % steps) * TILE + first, TILE), TILE)
        ref[index, at] = total.astype(BF16)

class SumBuffers:
    def __init__(self, refs):
        self.acc, self.core, self.diag_x, self.diag_y, self.x, self.y, self.z, self.sems = refs
    @staticmethod
    def shapes(rows, columns, units):
        upper = (rows // 2 + TILE - 1) // TILE * TILE
        buf = lambda *shape: pltpu.VMEM(shape + (columns,), BF16)
        return [buf(4, 4, rows), buf(4, 4, rows), buf(4, upper), buf(4, rows - upper), buf(4, rows), buf(4, rows), buf(3, rows),
                pltpu.SemaphoreType.DMA((units, 2, Sum.COPIES))]
    COUNT = 8

class Sum:
    COPIES = 14
    def __init__(self, place, bufs, unit, cols, own, other, out):
        self.p, self.b, self.unit, self.own, self.other, self.out = place, bufs, unit, own, other, out
        self.rows = bufs.acc.shape[2]
        self.upper = bufs.diag_x.shape[1]
        self.lower = self.rows - self.upper
        self.acc = bufs.acc.at[:, :, :, cols]
        self.core = bufs.core.at[:, :, :, cols]
        self.diag_x, self.diag_y = bufs.diag_x.at[:, :, cols], bufs.diag_y.at[:, :, cols]
        self.x, self.y, self.z = bufs.x.at[:, :, cols], bufs.y.at[:, :, cols], bufs.z.at[:, :, cols]
        self.copies = {}
    def push(self, slot, src, dst, device):
        sems = self.b.sems
        self.copies[slot] = send(src, dst, (sems.at[self.unit, 0, slot], sems.at[self.unit, 1, slot]), device)
    def begin(self):
        for i in range(4):
            self.push(i, self.other(i), self.core.at[i], self.p.sibling)
    def stage0(self):
        top, bottom = pl.ds(0, self.upper), pl.ds(self.upper, self.lower)
        for i in range(4):
            self.copies[i].wait_recv()
            add_tiles(4, self.rows, (self.acc.at[i], 0), [(self.own(i), 0), (self.core.at[i], 0)])
            if i == 0:
                self.push(4, self.acc.at[0, :, top], self.diag_x, self.p.next_x)
                self.push(5, self.acc.at[0, :, bottom], self.diag_y, self.p.next_y)
            if i == 1:
                self.push(6, self.acc.at[1, :, top], self.x.at[:, top], self.p.next_x)
            if i == 2:
                self.push(7, self.acc.at[2, :, bottom], self.y.at[:, bottom], self.p.next_y)
    def stage1(self):
        top, bottom = pl.ds(0, self.upper), pl.ds(self.upper, self.lower)
        self.copies[4].wait_recv()
        add_tiles(4, self.upper, (self.acc.at[2], 0), [(self.acc.at[2], 0), (self.diag_x, 0)])
        self.push(8, self.acc.at[2, :, top], self.y.at[:, top], self.p.next_y)
        self.copies[5].wait_recv()
        add_tiles(4, self.lower, (self.acc.at[1], self.upper), [(self.acc.at[1], self.upper), (self.diag_y, 0)])
        self.push(9, self.acc.at[1, :, bottom], self.x.at[:, bottom], self.p.next_x)
    def stage2(self):
        for slot in (6, 7, 8, 9):
            self.copies[slot].wait_recv()
        add_tiles(4, self.rows, (self.acc.at[3], 0), [(self.acc.at[3], 0), (self.x, 0), (self.y, 0)])
        for o in (1, 2, 3):
            self.push(9 + o, self.acc.at[3, self.p.plane[o]], self.z.at[o - 1], self.p.line[o])
    def stage3(self):
        for o in (1, 2, 3):
            self.copies[9 + o].wait_recv()
        @pl.loop(0, self.rows // TILE)
        def _(i):
            here = pl.ds(pl.multiple_of(i * TILE, TILE), TILE)
            total = self.acc[3, self.p.z, here].astype(F32)
            for o in range(3):
                total += self.z[o, here].astype(F32)
            self.out[here] = total
    def core_sent(self):
        for i in range(4): self.copies[i].wait_send()
    def finish(self):
        for slot in range(4, 13): self.copies[slot].wait_send()

def product_units(place, bufs, part, chunk, left, right, out, extra):
    rows = out.shape[0]
    wide = 8 * rows
    units = []

    def add_unit(k, first):
        slot = k % 2
        span = min(chunk, right.shape[1] - first)

        def half(i, core):
            y, x = place.side(*CORNERS[i])
            return part.at[slot, :, y, x, core]

        unit = Sum(
            place, bufs, k, pl.ds(k * chunk, chunk),
            lambda i: half(i, place.core), lambda i: half(i, 1 - place.core),
            out.at[:, pl.ds(first, chunk)],
        )

        def make():
            if k >= 2:
                units[k - 2][0].core_sent()

            @pl.loop(0, 4)
            def _(z):
                here = pl.ds(pl.multiple_of(z * wide, wide), wide)
                product = dot(left[:, here], right[:, pl.ds(first, span)], ((0,), (0,)))
                block = (2, 2, 2, rows)
                part[slot, z, :, :, :, :, pl.ds(0, span)] = product.astype(BF16).reshape(block + (span,))
                if span < chunk:
                    part[slot, z, :, :, :, :, pl.ds(span, chunk - span)] = extra[here].reshape(
                        block + (chunk - span,)
                    )

            unit.begin()

        units.append((unit, make))

    for k, first in enumerate(range(0, out.shape[1], chunk)):
        add_unit(k, first)
    return units


def product_sum_kernel(chunk, left, right, extra, out, part, *scratch):
    place = Place()
    units = product_units(place, SumBuffers(scratch), part, chunk, left, right, out, extra)
    place.meet()
    count = len(units)
    stages = [lambda k: units[k][1]()] + [
        lambda k, name=name: getattr(units[k][0], name)()
        for name in ("stage0", "stage1", "stage2", "stage3")
    ]
    for step in range(count + 4):
        for s in (1, 2, 3, 4, 0):
            if 0 <= step - s < count:
                stages[s](step - s)
    for unit, _ in units[-2:]:
        unit.core_sent()
    for unit, _ in units:
        unit.finish()


def product_sum(left, right, extra, chunk, collective_id, name):
    rows = left.shape[1] // 32
    columns = right.shape[1] + extra.shape[1]
    vmem = pl.BlockSpec(memory_space=pltpu.VMEM)
    return pl.pallas_call(
        functools.partial(product_sum_kernel, chunk),
        out_shape=jax.ShapeDtypeStruct((rows, columns), F32),
        in_specs=[vmem] * 3,
        out_specs=vmem,
        scratch_shapes=[pltpu.VMEM((2, 4, 2, 2, 2, rows, chunk), BF16)]
        + SumBuffers.shapes(rows, columns, columns // chunk),
        compiler_params=pltpu.CompilerParams(
            collective_id=collective_id, has_side_effects=True, vmem_limit_bytes=62 * 1024 * 1024
        ),
        name=name,
    )(left, right, extra)


def back_sums_kernel(
    chunk, left, right, query_ref, window, log_ref, grad_ref,
    out, query_grad_ref, kv_grad_ref, part, kv_total, kv_part, *scratch,
):
    place = Place()
    me = lax.axis_index(AXIS)
    tok_rows, features = query_ref.shape
    blocks = window.shape[0] // tok_rows
    start = jnp.maximum(me - (blocks - 1), 0)
    ahead = (me - start) * tok_rows
    units = product_units(
        place, SumBuffers(scratch[: SumBuffers.COUNT]), part, chunk, left, right, out, None
    )
    sums = [unit for unit, _ in units]

    def half(i, core):
        y, x = place.side(*CORNERS[i])
        return kv_part.at[:, y, x, core]

    kv = Sum(
        place, SumBuffers(scratch[SumBuffers.COUNT :]), 0, pl.ds(0, 2 * HD),
        lambda i: half(i, place.core), lambda i: half(i, 1 - place.core), kv_grad_ref,
    )
    place.meet()
    units[0][1]()
    units[1][1]()
    sums[0].stage0()
    sums[1].stage0()
    kv_total[...] = jnp.zeros_like(kv_total)
    kv_part[...] = jnp.zeros_like(kv_part)

    @pl.loop(0, features // (PAIR * HD))
    def _(i):
        here = pl.ds(pl.multiple_of(i * PAIR * HD, PAIR * HD), PAIR * HD)
        query_grad, key_part, value_part = attend_back_pair(
            ahead, query_ref[:, here], grad_ref[:, here], window[:, :HD], window[:, HD:],
            log_ref[i][:, :1],
        )
        query_grad_ref[:, here] = query_grad
        kv_total[:, :HD] += key_part
        kv_total[:, HD:] += value_part

    for j in range(blocks):
        block = start + j
        kv_part[block // 8, (block // 4) % 2, (block // 2) % 2, block % 2] = kv_total[
            j * tok_rows : (j + 1) * tok_rows
        ].astype(BF16)
    kv.begin()
    sums[0].stage1()
    kv.stage0()
    sums[1].stage1()
    units[2][1]()
    kv.stage1()
    sums[0].stage2()
    sums[2].stage0()
    kv.stage2()
    sums[1].stage2()
    units[3][1]()
    sums[2].stage1()
    sums[3].stage0()
    kv.stage3()
    sums[0].stage3()
    sums[2].stage2()
    sums[3].stage1()
    sums[1].stage3()
    sums[3].stage2()
    sums[2].stage3()
    sums[3].stage3()
    for unit in sums[2:] + [kv]:
        unit.core_sent()
    for unit in sums + [kv]:
        unit.finish()


def back_sums(left, right, queries, kv_window, logs, grad, collective_id):
    rows, columns = left.shape[1] // 32, right.shape[1]
    tok_rows, features = queries.shape
    chunk = columns // 4
    vmem = pl.BlockSpec(memory_space=pltpu.VMEM)
    return pl.pallas_call(
        functools.partial(back_sums_kernel, chunk),
        out_shape=(
            jax.ShapeDtypeStruct((rows, columns), F32),
            jax.ShapeDtypeStruct((tok_rows, features), F32),
            jax.ShapeDtypeStruct((tok_rows, 2 * HD), F32),
        ),
        in_specs=[vmem] * 6,
        out_specs=(vmem,) * 3,
        scratch_shapes=[
            pltpu.VMEM((2, 4, 2, 2, 2, rows, chunk), BF16),
            pltpu.VMEM(kv_window.shape, F32),
            pltpu.VMEM((4, 2, 2, 2, tok_rows, 2 * HD), BF16),
        ]
        + SumBuffers.shapes(rows, columns, 4)
        + SumBuffers.shapes(tok_rows, 2 * HD, 1),
        compiler_params=pltpu.CompilerParams(
            collective_id=collective_id, has_side_effects=True, vmem_limit_bytes=62 * 1024 * 1024
        ),
        name="back_sums",
    )(left, right, queries, kv_window, logs, grad)


PLANES=4
def plane_order(z):
    near = jnp.minimum(z, 3 - z)
    flip = z // 2
    order = []
    for k in range(4):
        swapped = 1 - k if k < 2 else k
        plane = near * swapped + (1 - near) * k
        order.append(flip * (3 - plane) + (1 - flip) * plane)
    return order

class Gather:
    COPIES = 11
    def __init__(self, place, own, held, cols, sems):
        self.place, self.held, self.cols, self.sems = place, held, cols, sems
        self.own = own.at[:, cols]
        rows = held.shape[4]
        upper = (rows // 2 + TILE - 1) // TILE * TILE
        self.halves = pl.ds(0, upper), pl.ds(upper, rows - upper)
        self.order = plane_order(place.z)
        self.sent = []
        self.kept = []
    def at(self, plane, y, x, core, part=slice(None)):
        return self.held.at[plane, y, x, core, part, self.cols]
    def pair(self, slot, k):
        return self.sems.at[0, slot, k], self.sems.at[1, slot, k]
    def push(self, src, dst, slot, k, device):
        copy = send(src, dst, self.pair(slot, k), device)
        self.sent.append(copy)
    def arrived(self, ref, slot, k):
        pltpu.make_async_remote_copy(src_ref=ref, dst_ref=ref, send_sem=self.sems.at[0, slot, k], recv_sem=self.sems.at[1, slot, k], device_id=(self.place.sibling,), device_id_type=MESH).wait_recv()
    def start(self):
        p = self.place
        mine = self.at(p.z, p.y, p.x, p.core)
        keep = pltpu.make_async_copy(self.own, mine, self.sems.at[0, 10, 0])
        keep.start()
        self.kept.append(keep)
        for k in (1, 2, 3):
            plane = self.order[k]
            copy = pltpu.make_async_remote_copy(src_ref=self.own, dst_ref=mine, send_sem=self.sems.at[0, 0, k], recv_sem=self.sems.at[1, 0, p.z], device_id=(p.index(plane, p.y, p.x, p.core),), device_id_type=MESH)
            copy.start(); self.sent.append(copy)
    def line(self, k):
        p = self.place
        plane = self.order[k]
        block = self.at(plane, p.y, p.x, p.core)
        source = self.own if k == 0 else block
        if k > 0:
            pltpu.make_async_remote_copy(src_ref=block, dst_ref=block, send_sem=self.sems.at[0, 0, k], recv_sem=self.sems.at[1, 0, plane], device_id=(p.sibling,), device_id_type=MESH).wait_recv()
        self.push(source, block, 1, k, p.next_x)
        self.push(source, block, 2, k, p.next_y)
        self.push(source, block, 5, k, p.sibling)
    def side(self, k):
        p, plane = self.place, self.order[k]
        top, bottom = self.halves
        self.arrived(self.at(plane, p.y, 1 - p.x, p.core), 1, k)
        block = self.at(plane, p.y, 1 - p.x, p.core, top)
        self.push(block, block, 4, k, p.next_y)
        block = self.at(plane, p.y, 1 - p.x, p.core)
        self.push(block, block, 6, k, p.sibling)
        self.arrived(self.at(plane, 1 - p.y, p.x, p.core), 2, k)
        block = self.at(plane, 1 - p.y, p.x, p.core, bottom)
        self.push(block, block, 3, k, p.next_x)
        block = self.at(plane, 1 - p.y, p.x, p.core)
        self.push(block, block, 7, k, p.sibling)
    def diag(self, k):
        p, plane = self.place, self.order[k]
        for slot, part in ((4, self.halves[0]), (3, self.halves[1])):
            block = self.at(plane, 1 - p.y, 1 - p.x, p.core, part)
            self.arrived(block, slot, k)
            self.push(block, block, slot + 5, k, p.sibling)
    def ready(self, k):
        p, plane = self.place, self.order[k]
        top, bottom = self.halves
        if k == 0:
            for keep in self.kept: keep.wait()
        other = 1 - p.core
        self.arrived(self.at(plane, p.y, p.x, other), 5, k)
        self.arrived(self.at(plane, p.y, 1 - p.x, other), 6, k)
        self.arrived(self.at(plane, 1 - p.y, p.x, other), 7, k)
        self.arrived(self.at(plane, 1 - p.y, 1 - p.x, other, top), 9, k)
        self.arrived(self.at(plane, 1 - p.y, 1 - p.x, other, bottom), 8, k)
    def finish(self):
        for copy in self.sent: copy.wait_send()

def pipeline(stages, count):
    for step in range(count + len(stages) - 1):
        for s in range(len(stages) - 1, -1, -1):
            if 0 <= step - s < count:
                stages[s](step - s)

def gather_kernel(chunks, *refs):
    n = len(chunks)
    ins, outs, sems = refs[:n], refs[n:2*n], refs[2*n:]
    place = Place()
    place.meet()
    items = []
    for a in range(n):
        width = ins[a].shape[1] // chunks[a]
        for j in range(chunks[a]):
            items.append(Gather(place, ins[a], outs[a], pl.ds(j * width, width), sems[a].at[j]))
    def line(s):
        if s % PLANES == 0:
            items[s // PLANES].start()
        items[s // PLANES].line(s % PLANES)
    def side(s): items[s // PLANES].side(s % PLANES)
    def diag(s): items[s // PLANES].diag(s % PLANES)
    pipeline([line, side, diag], len(items) * PLANES)
    for item in items:
        for k in range(PLANES): item.ready(k)
    for item in items: item.finish()

def gather_all(arrays, chunks, collective_id, name):
    outs = pl.pallas_call(
        functools.partial(gather_kernel, chunks),
        out_shape=tuple(jax.ShapeDtypeStruct((4,2,2,2)+a.shape, BF16) for a in arrays),
        in_specs=[pl.BlockSpec(memory_space=pl.ANY)]*len(arrays),
        out_specs=tuple(pl.BlockSpec(memory_space=pl.ANY) for _ in arrays),
        scratch_shapes=[pltpu.SemaphoreType.DMA((c, 2, Gather.COPIES, PLANES)) for c in chunks],
        compiler_params=pltpu.CompilerParams(collective_id=collective_id, has_side_effects=True),
        name=name,
    )(*arrays)
    return [o.reshape(32 * a.shape[0], a.shape[1]) for o, a in zip(outs, arrays)]


GELU_SCALE = math.sqrt(2.0 / math.pi)
GELU_CUBE = 0.044715

def gelu_and_slope(v):
    square = v * v
    t = jnp.tanh(GELU_SCALE * v * (1.0 + GELU_CUBE * square))
    half = 0.5 * (1.0 + t)
    slope = half + 0.5 * v * (1.0 - t * t) * (GELU_SCALE * (1.0 + 3.0 * GELU_CUBE * square))
    return v * half, slope

def gather_attend_kernel(
    kv_ref, weight_ref, cotangent_ref, query_ref,
    kv_held, weight_held, cotangent_held, window, out_ref, log_ref,
    kv_sems, weight_sems, cotangent_sems, load_sems,
):
    place = Place()
    me = lax.axis_index(AXIS)
    tok_rows, features = query_ref.shape
    blocks = window.shape[0] // tok_rows
    start = jnp.maximum(me - (blocks - 1), 0)
    place.meet()

    def item(own, held, sems):
        return Gather(place, own, held, pl.ds(0, own.shape[1]), sems)

    kv = item(kv_ref, kv_held, kv_sems)
    weight = item(weight_ref, weight_held, weight_sems)
    cotangent = item(cotangent_ref, cotangent_held, cotangent_sems)
    for one in (kv, weight, cotangent):
        one.start()

    def run(*steps):
        for one, name, k in steps:
            getattr(one, name)(k)

    run(
        (kv, "line", 0), (weight, "line", 0), (kv, "line", 1), (kv, "side", 0),
        (kv, "line", 2), (kv, "side", 1), (kv, "diag", 0), (kv, "line", 3),
        (kv, "side", 2), (kv, "diag", 1), (kv, "side", 3), (kv, "diag", 2), (kv, "diag", 3),
        (weight, "line", 1), (cotangent, "line", 0), (weight, "side", 0), (weight, "line", 2),
        (weight, "side", 1), (weight, "diag", 0), (weight, "line", 3), (cotangent, "line", 1),
        (kv, "ready", 0), (kv, "ready", 1), (kv, "ready", 2), (kv, "ready", 3),
    )
    loads = []
    for j in range(blocks):
        block = start + j
        load = pltpu.make_async_copy(
            kv_held.at[block // 8, (block // 4) % 2, (block // 2) % 2, block % 2],
            window.at[pl.ds(j * tok_rows, tok_rows)],
            load_sems.at[j],
        )
        load.start()
        loads.append(load)
    for load in loads:
        load.wait()
    run((weight, "side", 2), (weight, "diag", 1))
    ahead = (me - start) * tok_rows

    @pl.loop(0, features // (PAIR * HD))
    def _(i):
        here = pl.ds(pl.multiple_of(i * PAIR * HD, PAIR * HD), PAIR * HD)
        attended, logs = attend_pair(ahead, query_ref[:, here], window[:, :HD], window[:, HD:])
        out_ref[:, here] = attended
        log_ref[i] = jnp.broadcast_to(logs, log_ref.shape[1:])

    run(
        (cotangent, "side", 0), (weight, "side", 3), (weight, "diag", 2), (cotangent, "line", 2),
        (weight, "diag", 3), (cotangent, "side", 1), (cotangent, "diag", 0),
        (cotangent, "line", 3), (cotangent, "side", 2), (cotangent, "diag", 1),
        (cotangent, "side", 3), (cotangent, "diag", 2), (cotangent, "diag", 3),
    )
    for one in (weight, cotangent):
        for k in range(PLANES):
            one.ready(k)
    for one in (kv, weight, cotangent):
        one.finish()


def gather_attend(own_kv, out_weight, out_cotangent, queries, collective_id):
    tok_rows, features = queries.shape
    blocks = (WINDOW + tok_rows - 2) // tok_rows + 1
    pairs = features // HD // PAIR
    arrays = (own_kv, out_weight, out_cotangent)
    hbm = pl.BlockSpec(memory_space=pl.ANY)
    vmem = pl.BlockSpec(memory_space=pltpu.VMEM)
    outs = pl.pallas_call(
        gather_attend_kernel,
        out_shape=tuple(jax.ShapeDtypeStruct((4, 2, 2, 2) + a.shape, BF16) for a in arrays)
        + (
            jax.ShapeDtypeStruct((blocks * tok_rows, own_kv.shape[1]), BF16),
            jax.ShapeDtypeStruct((tok_rows, features), BF16),
            jax.ShapeDtypeStruct((pairs, PAIR * tok_rows, LANES), F32),
        ),
        in_specs=[hbm] * 3 + [vmem],
        out_specs=(hbm,) * 3 + (vmem,) * 3,
        scratch_shapes=[pltpu.SemaphoreType.DMA((2, Gather.COPIES, PLANES)) for _ in arrays]
        + [pltpu.SemaphoreType.DMA((blocks,))],
        compiler_params=pltpu.CompilerParams(
            collective_id=collective_id, has_side_effects=True, vmem_limit_bytes=VMEM_BYTES
        ),
        name="gather_attend",
    )(*arrays, queries)
    full = [o.reshape(32 * a.shape[0], a.shape[1]) for o, a in zip(outs[1:3], arrays[1:])]
    return full[0], full[1], outs[3], outs[4], outs[5]


class PlaneSum:
    SLOTS = 10
    def __init__(self, place, order, kind, k, acc, outgoing, out, land, load, sems, line_sems, load_sems):
        self.p, self.k, self.order = place, k, order
        self.acc, self.outgoing = acc.at[kind, k], outgoing.at[kind]
        self.out = out
        core, diag_x, diag_y, side_x, side_y, line = land
        self.core, self.side_x, self.side_y = core.at[kind, k], side_x.at[kind, k], side_y.at[kind, k]
        self.diag_x, self.diag_y, self.land = diag_x.at[kind, k], diag_y.at[kind, k], line.at[kind]
        self.load, self.load_sems = load, load_sems
        self.sems, self.line_sems = sems.at[kind, k], line_sems.at[kind]
        self.rows = self.acc.shape[1]
        self.upper = self.diag_x.shape[0]
        self.top, self.bottom = pl.ds(0, self.upper), pl.ds(self.upper, self.rows - self.upper)
    def mine(self, i): return self.acc.at[i]
    def copy(self, src, dst, slot, device):
        return pltpu.make_async_remote_copy(src_ref=src, dst_ref=dst, send_sem=self.sems.at[0, slot], recv_sem=self.sems.at[1, slot], device_id=(device,), device_id_type=MESH)
    def across(self, i):
        return self.copy(self.outgoing.at[i % 2], self.core.at[i], i, self.p.sibling)
    def make(self, slot):
        p, mine = self.p, self.mine
        src, dst, device = {
            4: (mine(0).at[self.top], self.diag_x, p.next_x),
            5: (mine(0).at[self.bottom], self.diag_y, p.next_y),
            6: (mine(1).at[self.top], self.side_x.at[self.top], p.next_x),
            7: (mine(2).at[self.bottom], self.side_y.at[self.bottom], p.next_y),
            8: (mine(2).at[self.top], self.side_y.at[self.top], p.next_y),
            9: (mine(1).at[self.bottom], self.side_x.at[self.bottom], p.next_x),
        }[slot]
        return self.copy(src, dst, slot, device)
    def line_copy(self):
        p, plane = self.p, self.order[self.k]
        return pltpu.make_async_remote_copy(src_ref=self.mine(3), dst_ref=self.land.at[p.z], send_sem=self.line_sems.at[0, self.k], recv_sem=self.line_sems.at[1, p.z], device_id=(p.index(plane, p.y, p.x, p.core),), device_id_type=MESH)
    def fetch(self, src, slot):
        rows = src.shape[0]
        copy = pltpu.make_async_copy(src, self.load.at[slot, pl.ds(0, rows)], self.load_sems.at[slot])
        copy.start()
        return copy
    def add(self, target, slots, rows):
        @pl.loop(0, rows // TILE, unroll=2)
        def _(i):
            here = pl.ds(pl.multiple_of(i * TILE, TILE), TILE)
            total = target[here].astype(F32)
            for slot in slots: total += self.load[slot, here].astype(F32)
            target[here] = total.astype(target.dtype)
    def stage0(self):
        self.across(0).wait_recv()
        fetched = self.fetch(self.core.at[0], 0)
        for i in range(4):
            current = fetched
            if i < 3:
                self.across(i + 1).wait_recv()
                fetched = self.fetch(self.core.at[i + 1], (i + 1) % 2)
            current.wait()
            self.add(self.mine(i), [i % 2], self.rows)
            for slot in ((4, 5), (6,), (7,), ())[i]:
                self.make(slot).start()
    def stage1(self):
        self.make(4).wait_recv()
        self.fetch(self.diag_x, 0).wait()
        self.add(self.mine(2).at[self.top], [0], self.upper)
        self.make(8).start()
        self.make(5).wait_recv()
        self.fetch(self.diag_y, 1).wait()
        self.add(self.mine(1).at[self.bottom], [1], self.rows - self.upper)
        self.make(9).start()
    def stage2(self):
        for slot in (6, 9): self.make(slot).wait_recv()
        first = self.fetch(self.side_x, 0)
        for slot in (7, 8): self.make(slot).wait_recv()
        second = self.fetch(self.side_y, 1)
        first.wait(); second.wait()
        if self.k > 0:
            self.add(self.mine(3), [0, 1], self.rows)
            self.line_copy().start()
        else:
            mine, out = self.mine(3), self.out
            @pl.loop(0, self.rows // TILE)
            def _(i):
                here = pl.ds(pl.multiple_of(i * TILE, TILE), TILE)
                out[here] = mine[here].astype(F32) + self.load[0, here].astype(F32) + self.load[1, here].astype(F32)
    def sent(self):
        for slot in range(4, 10): self.make(slot).wait_send()
        if self.k > 0: self.line_copy().wait_send()
    def last(self):
        p, plane = self.p, self.order[self.k]
        land = self.land.at[plane]
        pltpu.make_async_remote_copy(src_ref=land, dst_ref=land, send_sem=self.line_sems.at[0, self.k], recv_sem=self.line_sems.at[1, plane], device_id=(p.sibling,), device_id_type=MESH).wait_recv()
        self.fetch(land, self.k % 2).wait()
        self.add(self.out, [self.k % 2], self.rows)

def ffn_kernel(hidden_ref, cotangent_ref, both_ref, down_ref, bias_ref,
               hidden_sum, ffn_sum, grad_both_ref, grad_down_ref, bias_grad_ref,
               held, land_core, land_dx, land_dy, land_x, land_y, land_z,
               tokens, cot, both_keep, ffn_keep, acc, outgoing, load, gather_sems, cot_sems, sum_sems, line_sems, load_sems):
    place = Place()
    width = hidden_ref.shape[1]
    pad = down_ref.shape[0]
    rows = 2 * hidden_ref.shape[0]
    order = plane_order(place.z)
    def fetch_cot(k): return pltpu.make_async_copy(cotangent_ref.at[order[k]], cot, cot_sems.at[0, k])
    def fetch_tokens(k): return pltpu.make_async_copy(held.at[order[k]], tokens, cot_sems.at[1, k])
    fetch_cot(0).start()
    place.meet()
    gather = Gather(place, hidden_ref, held, pl.ds(0, width), gather_sems)
    gather.start()
    grad_both_ref[...] = jnp.zeros_like(grad_both_ref)
    grad_down_ref[...] = jnp.zeros_like(grad_down_ref)
    bias_grad_ref[...] = jnp.zeros_like(bias_grad_ref)
    land = (land_core, land_dx, land_dy, land_x, land_y, land_z)
    sums = [[PlaneSum(place, order, kind, k, acc, outgoing, (hidden_sum, ffn_sum)[kind], land, load, sum_sems, line_sems, load_sems) for k in range(PLANES)] for kind in range(2)]

    def compute(k):
        gather.ready(k)
        fetch_tokens(k).start()
        fetch_tokens(k).wait()
        fetch_cot(k).wait()
        half = rows // 2
        @pl.loop(0, 4)
        def _(i):
            dy, dx = 1 - i % 2, 1 - i // 2
            y, x = place.y + dy * (1 - 2 * place.y), place.x + dx * (1 - 2 * place.x)
            hidden = tokens[y, x].reshape(rows, width)
            cotangent = cot[y, x].reshape(rows, width)
            both_pre = dot(hidden, both_ref[...], ((1,), (0,))) + bias_ref[0:1]
            hidden_grad = dot(cotangent, down_ref[...], ((1,), (1,)))
            activated, slope = gelu_and_slope(both_pre[:, :pad])
            up_pre = both_pre[:, pad:]
            hidden_ffn = (activated * up_pre).astype(BF16)
            both_grad = jnp.concatenate([(hidden_grad * up_pre * slope).astype(BF16), (hidden_grad * activated).astype(BF16)], axis=1)
            here = pl.ds(pl.multiple_of((y * 2 + x) * rows, rows), rows)
            both_keep[here] = both_grad
            ffn_keep[here] = hidden_ffn
            bias_grad_ref[...] += jnp.sum(both_grad.astype(F32), axis=0, keepdims=True)
            def drain():
                for kind in range(2): sums[kind][k].across(i - 2).wait_send()
            def drain_before():
                for kind in range(2): sums[kind][k - 1].across(i + 2).wait_send()
            pl.when(i >= 2)(drain)
            if k > 0: pl.when(i < 2)(drain_before)
            for kind, part in ((0, lambda: dot(both_grad, both_ref[...], ((1,), (1,)))), (1, lambda: dot(hidden_ffn, down_ref[...], ((1,), (0,))))):
                result = part().astype(BF16)
                low, high = result[:half], result[half:]
                acc[kind, k, i] = jnp.where(place.core == 0, low, high)
                outgoing[kind, i % 2] = jnp.where(place.core == 0, high, low)
                sums[kind][k].across(i).start()

    def weight_grads(k):
        step = 512
        @pl.loop(0, width // step)
        def _(j):
            cols = pl.ds(pl.multiple_of(j * step, step), step)
            hidden = tokens[:, :, :, :, cols].reshape(4 * rows, step)
            grad_both_ref[:, cols] += dot(both_keep[...], hidden, ((0,), (0,)))
            cotangent = cot[:, :, :, :, cols].reshape(4 * rows, step)
            grad_down_ref[:, cols] += dot(ffn_keep[...], cotangent, ((0,), (0,)))
        if k + 1 < PLANES: fetch_cot(k + 1).start()

    def both(name, k):
        for kind in range(2): getattr(sums[kind][k], name)()

    gather.line(0)
    gather.line(1)
    gather.side(0)
    gather.line(2)
    gather.side(1)
    gather.diag(0)
    compute(0)
    gather.line(3)
    gather.side(2)
    weight_grads(0)
    gather.diag(1)
    compute(1)
    gather.side(3)
    both("stage0", 1)
    gather.diag(2)
    weight_grads(1)
    gather.diag(3)
    both("stage1", 1)
    compute(2)
    both("stage0", 2)
    both("stage2", 1)
    weight_grads(2)
    compute(3)
    both("stage1", 2)
    both("stage0", 3)
    both("stage2", 2)
    both("stage1", 3)
    both("stage0", 0)
    weight_grads(3)
    both("stage2", 3)
    both("stage1", 0)
    both("stage2", 0)
    for kind in range(2):
        for i in (2, 3): sums[kind][3].across(i).wait_send()
    for kind in range(2):
        for k in (1, 2, 3): sums[kind][k].last()
    for k in range(PLANES): both("sent", k)
    gather.finish()

def ffn(hidden_two, cotangent_full, both_own, both_bias, down_own, collective_id):
    tok_rows, width = hidden_two.shape
    pad = down_own.shape[0]
    full = (4, 2, 2, 2, tok_rows, width)
    upper = (tok_rows // 2 + TILE - 1) // TILE * TILE
    hbm = pl.BlockSpec(memory_space=pl.ANY)
    vmem = pl.BlockSpec(memory_space=pltpu.VMEM)
    dma = pltpu.SemaphoreType.DMA
    low = lambda *shape: jax.ShapeDtypeStruct(shape + (width,), BF16)
    outs = pl.pallas_call(
        ffn_kernel,
        out_shape=(
            jax.ShapeDtypeStruct((tok_rows, width), F32),
            jax.ShapeDtypeStruct((tok_rows, width), F32),
            jax.ShapeDtypeStruct((2 * pad, width), F32),
            jax.ShapeDtypeStruct((pad, width), F32),
            jax.ShapeDtypeStruct((8, 2 * pad), F32),
            low(4, 2, 2, 2, tok_rows),
            low(2, 4, 4, tok_rows), low(2, 4, upper), low(2, 4, tok_rows - upper),
            low(2, 4, tok_rows), low(2, 4, tok_rows), low(2, 4, tok_rows),
        ),
        in_specs=[hbm, hbm, vmem, vmem, vmem],
        out_specs=(vmem,) * 5 + (hbm,) * 7,
        scratch_shapes=[
            pltpu.VMEM(full[1:], BF16),
            pltpu.VMEM(full[1:], BF16),
            pltpu.VMEM((8 * tok_rows, 2 * pad), BF16),
            pltpu.VMEM((8 * tok_rows, pad), BF16),
            pltpu.VMEM((2, 4, 4, tok_rows, width), BF16),
            pltpu.VMEM((2, 2, tok_rows, width), BF16),
            pltpu.VMEM((2, tok_rows, width), BF16),
            dma((2, Gather.COPIES, PLANES)), dma((2, PLANES)), dma((2, PLANES, 2, PlaneSum.SLOTS)), dma((2, 2, PLANES)), dma((2,)),
        ],
        compiler_params=pltpu.CompilerParams(collective_id=collective_id, has_side_effects=True, vmem_limit_bytes=63*1024*1024),
        name="feed_forward",
    )(hidden_two, cotangent_full.reshape(full), both_own, down_own, jnp.broadcast_to(both_bias, (8, 2 * pad)))
    return outs[0], outs[1], outs[2], outs[3], outs[4][0]


def gather_rows(arrays, collective_id, name):
    if lax.axis_size(AXIS) == DEVICES:
        return gather_all(arrays, [1] * len(arrays), collective_id, name)
    return [lax.all_gather(values, AXIS, axis=0, tiled=True) for values in arrays]


def sum_rows(partial):
    return lax.psum_scatter(
        partial.astype(BF16), AXIS, scatter_dimension=0, tiled=True
    ).astype(F32)


def swap(pieces):
    return lax.all_to_all(pieces, AXIS, 0, 0, tiled=False)


def feed_forward(hidden_two, cotangent_full, both_own, both_bias, down_own, rows):
    peers = lax.axis_size(AXIS)
    device = lax.axis_index(AXIS)
    tok_rows, width = hidden_two.shape
    ffn_pad = down_own.shape[0]
    own_cotangent = lax.dynamic_slice_in_dim(cotangent_full, device * rows, rows, 1)
    down_bias_share = jnp.sum(own_cotangent.astype(F32), axis=0)
    if peers == DEVICES:
        normed_grad, ffn_out, grad_both, grad_down, bias_share = ffn(
            hidden_two, cotangent_full, both_own, both_bias, down_own, 7
        )
        return normed_grad, ffn_out, grad_both.T, grad_down, bias_share, down_bias_share

    def piece(sums, here):
        hidden_own, cotangent_piece = here
        hidden_full = gather_rows([hidden_own], None, None)[0]
        both_pre = jnp.dot(hidden_full, both_own, preferred_element_type=F32) + both_bias
        activated, slope = gelu_and_slope(both_pre[:, :ffn_pad])
        up_pre = both_pre[:, ffn_pad:]
        hidden_ffn = (activated * up_pre).astype(BF16)
        hidden_grad = dot(cotangent_piece, down_own, ((1,), (1,)))
        gate_grad = (hidden_grad * up_pre * slope).astype(BF16)
        up_grad = (hidden_grad * activated).astype(BF16)
        both_grad = jnp.concatenate([gate_grad, up_grad], axis=1)
        normed_grad = sum_rows(dot(both_grad, both_own, ((1,), (1,))))
        ffn_out = sum_rows(jnp.dot(hidden_ffn, down_own, preferred_element_type=F32))
        shares = (
            dot(hidden_full, both_grad, ((0,), (0,))),
            dot(hidden_ffn, cotangent_piece, ((0,), (0,))),
            jnp.sum(both_grad.astype(F32), axis=0),
        )
        return jax.tree.map(jnp.add, sums, shares), (normed_grad, ffn_out)

    pieces = max(1, peers // DEVICES)
    cut = tok_rows // pieces
    zeros = (
        jnp.zeros((width, 2 * ffn_pad), F32),
        jnp.zeros((ffn_pad, width), F32),
        jnp.zeros((2 * ffn_pad,), F32),
    )
    cotangent_pieces = cotangent_full.reshape(peers, pieces, cut, width).transpose(1, 0, 2, 3)
    shares, outs = lax.scan(
        piece,
        zeros,
        (hidden_two.reshape(pieces, cut, width), cotangent_pieces.reshape(pieces, -1, width)),
    )
    normed_grad, ffn_out = (part.reshape(tok_rows, width) for part in outs)
    return (normed_grad, ffn_out) + shares + (down_bias_share,)


def body(
    layer_input,
    norm1_scale,
    query_weight,
    keyvalue_weight,
    out_weight,
    norm2_scale,
    gate_weight,
    gate_bias,
    up_weight,
    up_bias,
    down_weight,
    down_bias,
    out_cotangent,
):
    peers = lax.axis_size(AXIS)
    device = lax.axis_index(AXIS)
    tok_rows, width = layer_input.shape
    rows = query_weight.shape[0]
    query_cols = query_weight.shape[1]
    kv_cols = keyvalue_weight.shape[1]
    heads = query_cols // HD
    quarter = HD // 4
    query_scale = 1.0 / math.sqrt(HD)
    ffn_own = down_weight.shape[0]
    ffn_pad = round_up(ffn_own, LANES)

    vectors = jnp.stack([norm1_scale, norm2_scale, down_bias], axis=1)
    packed = jnp.concatenate(
        [query_weight, keyvalue_weight, pad_columns(vectors, LANES)], axis=1
    )
    first = gather_rows([packed], 5, "gather_weights")[0]
    proj_cols = query_cols + kv_cols
    proj_full = first[:, :proj_cols]
    gains = first[:, proj_cols:].astype(F32).T
    gain_one, gain_two, bias_down = gains[0], gains[1], gains[2]

    resid_in = layer_input.astype(F32)
    square_one = jnp.mean(resid_in * resid_in, axis=1, keepdims=True)
    scale_one = lax.rsqrt(square_one + EPSILON)
    normed_one = resid_in * scale_one
    hidden_one = (normed_one * gain_one).astype(BF16)
    projected = jnp.dot(hidden_one, proj_full, preferred_element_type=F32)
    position = device * tok_rows + jnp.arange(tok_rows, dtype=jnp.int32)
    cosine, sine_table = rotary_tables(position.astype(F32), quarter)
    queries = (
        rotate(
            projected[:, :query_cols].reshape(tok_rows, heads, HD),
            cosine[:, None, :],
            sine_table[:, None, :],
            quarter,
        )
        * query_scale
    ).astype(BF16)
    queries = queries.reshape(tok_rows, query_cols)
    keys_rot = rotate(projected[:, query_cols : query_cols + HD], cosine, sine_table, quarter)
    own_kv = jnp.concatenate([keys_rot, projected[:, query_cols + HD :]], axis=1).astype(BF16)

    reach = min((WINDOW + tok_rows - 2) // tok_rows, peers - 1)
    window_rows = (reach + 1) * tok_rows
    window_start = jnp.maximum(device - reach, 0) * tok_rows
    place = (device * tok_rows - window_start).astype(jnp.int32).reshape(1)
    if peers == DEVICES:
        out_full, cotangent_full, kv_window, attention, logs = gather_attend(
            own_kv, out_weight, out_cotangent, queries, 6
        )
    else:
        kv_full, out_full, cotangent_full = gather_rows(
            [own_kv, out_weight, out_cotangent], None, None
        )
        kv_window = lax.dynamic_slice_in_dim(kv_full, window_start, window_rows, 0)
        attention, logs = attend(place, queries, kv_window)

    residual_mid = resid_in + jnp.dot(attention, out_full, preferred_element_type=F32)
    square_two = jnp.mean(residual_mid * residual_mid, axis=1, keepdims=True)
    scale_two = lax.rsqrt(square_two + EPSILON)
    normed_two = residual_mid * scale_two
    hidden_two = (normed_two * gain_two).astype(BF16)

    gate_pieces = pad_columns(gate_weight.reshape(rows, peers, ffn_own), ffn_pad)
    up_pieces = pad_columns(up_weight.reshape(rows, peers, ffn_own), ffn_pad)
    both_own = swap(
        jnp.concatenate([gate_pieces, up_pieces], axis=2).transpose(1, 0, 2)
    ).reshape(peers * rows, 2 * ffn_pad)
    both_bias = jnp.concatenate(
        [pad_columns(gate_bias, ffn_pad), pad_columns(up_bias, ffn_pad)]
    ).astype(F32)
    down_own = jnp.pad(down_weight, ((0, ffn_pad - ffn_own), (0, 0)))

    normed_grad_two, ffn_out, grad_both, grad_down, bias_share, down_bias_share = feed_forward(
        hidden_two, cotangent_full, both_own, both_bias, down_own, rows
    )
    layer_output = (residual_mid + (ffn_out + bias_down)).astype(BF16)
    rms_values = jnp.stack(
        [jnp.sqrt(square_one[:, 0] + EPSILON), jnp.sqrt(square_two[:, 0] + EPSILON)], axis=0
    )
    grad_down = grad_down[:ffn_own]
    grad_both = swap(grad_both.astype(BF16).reshape(peers, rows, 2 * ffn_pad)).transpose(1, 0, 2)
    grad_both = grad_both.astype(F32)
    grad_gate = grad_both[:, :, :ffn_own].reshape(rows, peers * ffn_own)
    grad_up = grad_both[:, :, ffn_pad : ffn_pad + ffn_own].reshape(rows, peers * ffn_own)

    norm2_part = jnp.sum(normed_grad_two * normed_two, axis=0)
    weighted_two = normed_grad_two * gain_two
    mid_grad = out_cotangent.astype(F32) + scale_two * (
        weighted_two - normed_two * jnp.mean(weighted_two * normed_two, axis=1, keepdims=True)
    )
    mid_grad_low = mid_grad.astype(BF16)
    attention_grad = dot(mid_grad_low, out_full, ((1,), (1,))).astype(BF16)

    if peers == DEVICES:
        grad_out, query_grad, kv_grad = back_sums(
            attention, mid_grad_low, queries, kv_window, logs, attention_grad, 3
        )
    else:
        grad_out = sum_rows(dot(attention, mid_grad_low, ((0,), (0,))))
        query_grad, kv_part = attend_back(place, queries, kv_window, logs, attention_grad)
        kv_grad = sum_rows(
            lax.dynamic_update_slice_in_dim(
                jnp.zeros((peers * tok_rows, 2 * HD), BF16), kv_part.astype(BF16), window_start, 0
            )
        )
    query_raw_grad = (
        rotate(
            query_grad.reshape(tok_rows, heads, HD) * query_scale,
            cosine[:, None, :],
            -sine_table[:, None, :],
            quarter,
        )
        .reshape(tok_rows, query_cols)
        .astype(BF16)
    )
    key_raw_grad = rotate(kv_grad[:, :HD], cosine, -sine_table, quarter)
    kv_raw_grad = jnp.concatenate([key_raw_grad, kv_grad[:, HD:]], axis=1).astype(BF16)
    proj_grad = jnp.concatenate([query_raw_grad, kv_raw_grad], axis=1)
    normed_grad_one = dot(proj_grad, proj_full, ((1,), (1,)))
    norm1_part = jnp.sum(normed_grad_one * normed_one, axis=0)
    weighted_one = normed_grad_one * gain_one
    input_grad = (
        mid_grad
        + scale_one
        * (weighted_one - normed_one * jnp.mean(weighted_one * normed_one, axis=1, keepdims=True))
    ).astype(BF16)

    parts = pad_columns(jnp.stack([norm1_part, norm2_part], axis=1), LANES)
    if peers == DEVICES:
        tail = product_sum(hidden_one, proj_grad, parts.astype(BF16), 640, 2, "sum_projections")
    else:
        tail = sum_rows(
            jnp.concatenate(
                [dot(hidden_one, proj_grad, ((0,), (0,))).astype(BF16), parts.astype(BF16)], axis=1
            )
        )
    grad_proj = tail[:, :proj_cols]
    norm1_share = tail[:, proj_cols]
    norm2_share = tail[:, proj_cols + 1]
    return (
        layer_output,
        residual_mid,
        rms_values,
        input_grad,
        norm1_share,
        grad_proj[:, :query_cols],
        grad_proj[:, query_cols:],
        grad_out,
        norm2_share,
        grad_gate,
        bias_share[:ffn_own],
        grad_up,
        bias_share[ffn_pad : ffn_pad + ffn_own],
        grad_down,
        down_bias_share,
    )


def solution(mesh):
    by_rows, by_entry = P(AXIS, None), P(AXIS)
    in_specs = (
        by_rows,
        by_entry,
        by_rows,
        by_rows,
        by_rows,
        by_entry,
        by_rows,
        by_entry,
        by_rows,
        by_entry,
        by_rows,
        by_entry,
        by_rows,
    )
    out_specs = (
        by_rows,
        by_rows,
        P(None, AXIS),
        by_rows,
        by_entry,
        by_rows,
        by_rows,
        by_rows,
        by_entry,
        by_rows,
        by_entry,
        by_rows,
        by_entry,
        by_rows,
        by_entry,
    )
    return jax.shard_map(body, mesh=mesh, in_specs=in_specs, out_specs=out_specs, check_vma=False)
```
